32 devices in a mesh: fsdp: 2 (over x), ctx: 4 (over z), tensor: 4 (over y, core).
Axes of the slice: x: 2, y: 2, z: 4, core: 2. Of those that a mesh axis runs over, the one named last changes fastest.
Arguments:
- tokens: bfloat16 [2, 2, 1536, 2560], P(None, 'fsdp', 'ctx'), may hold values from -6 to 6
- segments: int32 [2, 2, 1536], P(None, 'fsdp'), may hold values from 0 to 2, as said below
- attn_gain: bfloat16 [2560], P(('fsdp', 'ctx')), may hold values from 0.099609375 to 1.8984375
- query_down: bfloat16 [2560, 768], P(('fsdp', 'ctx')), may hold values from -0.125 to 0.125
- query_gain: bfloat16 [768], P(('fsdp', 'ctx')), may hold values from 0.099609375 to 1.8984375
- query_up: bfloat16 [768, 3840], P(('fsdp', 'ctx'), 'tensor'), may hold values from -0.21875 to 0.21875
- latent_down: bfloat16 [2560, 288], P(('fsdp', 'ctx')), may hold values from -0.125 to 0.125
- latent_gain: bfloat16 [256], P(('fsdp', 'ctx')), may hold values from 0.099609375 to 1.8984375
- latent_up: bfloat16 [256, 5120], P(('fsdp', 'ctx'), 'tensor'), may hold values from -0.375 to 0.375
- out_weight: bfloat16 [2560, 2560], P(('fsdp', 'ctx'), 'tensor'), may hold values from -2.5 to 2.5
- ffn_gain: bfloat16 [2560], P(('fsdp', 'ctx')), may hold values from 0.099609375 to 1.8984375
- gate_weight: bfloat16 [2560, 6400], P(('fsdp', 'ctx'), 'tensor'), may hold values from -0.125 to 0.125
- up_weight: bfloat16 [2560, 6400], P(('fsdp', 'ctx'), 'tensor'), may hold values from -0.125 to 0.125
- down_weight: bfloat16 [2560, 6400], P(('fsdp', 'ctx'), 'tensor'), may hold values from -0.625 to 0.625
- cotangent: bfloat16 [2, 2, 1536, 2560], P(None, 'fsdp', 'ctx'), may hold values from -6 to 6
Outputs:
- mixed: bfloat16 [2, 2, 1536, 2560], P(None, 'fsdp', 'ctx')
- grad_tokens: float32 [2, 2, 1536, 2560], P(None, 'fsdp', 'ctx')
- grad_attn_gain: float32 [2560], P(('fsdp', 'ctx'))
- grad_query_down: float32 [2560, 768], P(('fsdp', 'ctx'))
- grad_query_gain: float32 [768], P(('fsdp', 'ctx'))
- grad_query_up: float32 [768, 3840], P(('fsdp', 'ctx'), 'tensor')
- grad_latent_down: float32 [2560, 288], P(('fsdp', 'ctx'))
- grad_latent_gain: float32 [256], P(('fsdp', 'ctx'))
- grad_latent_up: float32 [256, 5120], P(('fsdp', 'ctx'), 'tensor')
- grad_out_weight: float32 [2560, 2560], P(('fsdp', 'ctx'), 'tensor')
- grad_ffn_gain: float32 [2560], P(('fsdp', 'ctx'))
- grad_gate_weight: float32 [2560, 6400], P(('fsdp', 'ctx'), 'tensor')
- grad_up_weight: float32 [2560, 6400], P(('fsdp', 'ctx'), 'tensor')
- grad_down_weight: float32 [2560, 6400], P(('fsdp', 'ctx'), 'tensor')
The draws below stay inside these ranges and needn't reach their ends.
Inputs may be any that keep to these rules, and one draw needn't show every extreme that they name: `segments`: each row holds exactly three documents, numbered 0, 1, 2 in order: document 0 starts the row and ends before position 384, document 1 covers the positions from below 384 to 1152 or later, and document 2 ends the row.
All inputs are finite; a program needn't handle non-finite values.
Results may differ from the reference program's by a relative error of at most 0.025.
Values may be sent and summed in bfloat16 or wider, within the bound.
A program may use at most 256 MiB of HBM per device.

```python
import math
import jax
import jax.numpy as jnp
from jax import lax

D = 2560
QR = 768
KVR = 256
ROPE = 32
HD = 64
VD = 64
H = 40
FF = 6400
SEQ_DEV = 384
MICRO = 2
BATCH = 2
SEQ = 1536


def draw_segments(key, part):
    key = jax.random.fold_in(key, 11)
    first_key, second_key = jax.random.split(key, 2)
    shape = (MICRO, BATCH)
    long_start = jax.random.randint(first_key, shape + (1,), 1, SEQ_DEV)
    long_finish = jax.random.randint(second_key, shape + (1,), SEQ - SEQ_DEV + 1, SEQ)
    places = jnp.arange(SEQ, dtype=jnp.int32)
    flags = (places >= long_start).astype(jnp.int32) + (places >= long_finish).astype(jnp.int32)
    return flags.astype(jnp.int32)


def steps_of(own_key, dims, cuts, smallest, largest):
    loudness = 1.0
    for position, blocks in cuts:
        draws = jax.random.uniform(jax.random.fold_in(jax.random.fold_in(own_key, 6), position), (blocks,), jnp.float32, smallest / len(cuts), largest / len(cuts))
        loudness = loudness * jnp.repeat(jnp.exp(draws), dims[position] // blocks).reshape((-1,) + (1,) * (len(dims) - 1 - position))
    return loudness


def normal_values(rng, dims, width, bound, cuts=(), held_as=jnp.bfloat16):
    values = jax.random.normal(rng, dims, jnp.float32) * width
    if len(cuts) > 0:
        values = steps_of(rng, dims, cuts, -0.22, 0.18) * values
    return jnp.clip(values, min=-bound, max=bound).astype(held_as)


def setup_inputs(seed: int = 0) -> dict:
    seeds = jax.random.split(jax.random.key(seed), 16)
    tokens = normal_values(seeds[0], (MICRO, BATCH, SEQ, D), 1.0, 6.0, ((1, 2), (2, 4)))
    segments = draw_segments(jax.random.fold_in(seeds[15], 71), 0)
    attn_gain = jnp.clip(1.0 + 0.18 * jax.random.normal(seeds[2], (D,), jnp.float32), 0.099609375, 1.8984375).astype(jnp.bfloat16)
    query_down = normal_values(seeds[3], (D, QR), D ** -0.5, 0.125, ((0, 8),))
    query_gain = jnp.clip(1.0 + 0.18 * jax.random.normal(seeds[4], (QR,), jnp.float32), 0.099609375, 1.8984375).astype(jnp.bfloat16)
    query_up = normal_values(seeds[5], (QR, H * (HD + ROPE)), QR ** -0.5, 0.21875, ((0, 8), (1, 4)))
    latent_down = normal_values(seeds[6], (D, KVR + ROPE), D ** -0.5, 0.125, ((0, 8),))
    latent_gain = jnp.clip(1.0 + 0.18 * jax.random.normal(seeds[7], (KVR,), jnp.float32), 0.099609375, 1.8984375).astype(jnp.bfloat16)
    latent_up = normal_values(seeds[8], (KVR, H * (HD + VD)), KVR ** -0.5, 0.375, ((0, 8), (1, 4)))
    out_weight = normal_values(seeds[9], (D, H * VD), (max(H * VD // 512, 2)) ** -0.5, 2.5, ((0, 8), (1, 4)))
    ffn_gain = jnp.clip(1.0 + 0.18 * jax.random.normal(seeds[10], (D,), jnp.float32), 0.099609375, 1.8984375).astype(jnp.bfloat16)
    gate_weight = normal_values(seeds[11], (D, FF), D ** -0.5, 0.125, ((0, 8), (1, 4)))
    up_weight = normal_values(seeds[12], (D, FF), D ** -0.5, 0.125, ((0, 8), (1, 4)))
    down_weight = normal_values(seeds[13], (D, FF), (max(FF // 64, 2)) ** -0.5, 0.625, ((0, 8), (1, 4)))
    cotangent = normal_values(seeds[14], (MICRO, BATCH, SEQ, D), 1.0, 6.0, ((1, 2), (2, 4)))
    return {"tokens": tokens, "segments": segments, "attn_gain": attn_gain, "query_down": query_down, "query_gain": query_gain, "query_up": query_up, "latent_down": latent_down, "latent_gain": latent_gain, "latent_up": latent_up, "out_weight": out_weight, "ffn_gain": ffn_gain, "gate_weight": gate_weight, "up_weight": up_weight, "down_weight": down_weight, "cotangent": cotangent}


@jax.custom_vjp
def low(v):
    return lax.optimization_barrier(v.astype(jnp.bfloat16)).astype(jnp.float32)

@jax.custom_vjp
def low_back(v):
    return v

def low_keep(v):
    return (low(v), None)

def low_pass(kept, grad):
    return (grad,)

def back_keep(v):
    return (v, None)

def back_low(kept, grad):
    return (low(grad),)
low.defvjp(low_keep, low_pass)
low_back.defvjp(back_keep, back_low)
norm_eps = 1e-05
branch_scale = 1.4 / math.sqrt(62.0)
rope_base = 10000.0
masked_fill = -1e+30

def exact_product(left_side, right_side):
    return jnp.dot(left_side, right_side, precision=lax.Precision.HIGHEST, preferred_element_type=jnp.float32)

def rms_scale(values, gain_vec):
    return values * lax.rsqrt(lax.optimization_barrier(jnp.mean(values * values, axis=-1, keepdims=True)) + norm_eps) * gain_vec

def rotate(values, cosine, sine):
    half_width = values.shape[-1] // 2
    first_half = values[..., :half_width]
    second = values[..., half_width:]
    return jnp.concatenate([first_half * cosine - second * sine, first_half * sine + second * cosine], axis=-1)

def segment_positions(segment_ids):
    length = segment_ids.shape[0]
    places = jnp.arange(length, dtype=jnp.int32)
    starts_new = jnp.concatenate([jnp.ones((1,), jnp.int32), (segment_ids[1:] != segment_ids[:-1]).astype(jnp.int32)])
    return places - lax.cummax(places * starts_new, axis=0)

def rope_tables(places):
    half_width = ROPE // 2
    frequency = rope_base ** (-jnp.arange(half_width, dtype=jnp.float32) * (2.0 / ROPE))
    angles = places.astype(jnp.float32)[:, None] * frequency[None, :]
    return (jnp.cos(angles), jnp.sin(angles))

def row_forward(inputs, segment_ids, weights):
    gain_attn, down_query, gain_query, up_query, down_latent, gain_latent, up_latent, weight_out, gain_ffn, weight_gate, weight_up, weight_down = weights
    length = inputs.shape[0]
    att_scale = (HD + ROPE) ** (-0.5)
    cosine, sine = rope_tables(segment_positions(segment_ids))
    index_all = jnp.arange(length, dtype=jnp.int32)
    allowed = (index_all[None, :] <= index_all[:, None]) & (segment_ids[None, :] == segment_ids[:, None])
    normed = low(rms_scale(inputs, gain_attn))
    query_latent = low_back(exact_product(normed, down_query))
    query_normed = low(rms_scale(query_latent, gain_query))
    query_raw = low_back(exact_product(query_normed, up_query)).reshape(length, H, HD + ROPE)
    queries = low(jnp.concatenate([query_raw[..., :HD], rotate(query_raw[..., HD:], cosine[:, None, :], sine[:, None, :])], axis=-1))
    latent_raw = low_back(exact_product(normed, down_latent))
    latent = low(rms_scale(latent_raw[:, :KVR], gain_latent))
    key_rope = low(rotate(latent_raw[:, KVR:], cosine, sine))
    key_value = low(low_back(exact_product(latent, up_latent))).reshape(length, H, HD + VD)
    keys = jnp.concatenate([key_value[..., :HD], jnp.broadcast_to(key_rope[:, None, :], (length, H, ROPE))], axis=-1)
    values = key_value[..., HD:]

    def attend_head(parts):
        query_head, key_head, value_head = parts
        scores = low_back(exact_product(query_head, key_head.T)) * att_scale
        scores = jnp.where(allowed, scores, masked_fill)
        scores = scores - lax.optimization_barrier(jnp.max(scores, axis=-1, keepdims=True))
        exps = jnp.exp(scores)
        probs = exps / lax.optimization_barrier(jnp.sum(exps, axis=-1, keepdims=True))
        return low(low_back(exact_product(low(probs), value_head)))
    attended_heads = lax.map(jax.checkpoint(attend_head), (queries.transpose(1, 0, 2), keys.transpose(1, 0, 2), values.transpose(1, 0, 2)))
    attended = attended_heads.transpose(1, 0, 2).reshape(length, H * VD)
    attn_branch = low_back(exact_product(attended, weight_out.T))
    middle = inputs + branch_scale * attn_branch
    ffn_in = low(rms_scale(middle, gain_ffn))
    gate_val = low_back(exact_product(ffn_in, weight_gate))
    up_val = low_back(exact_product(ffn_in, weight_up))
    hidden = low(jax.nn.silu(gate_val) * up_val)
    ffn_branch = low_back(exact_product(hidden, weight_down.T))
    return middle + branch_scale * ffn_branch

def reference(tokens, segments, attn_gain, query_down, query_gain, query_up, latent_down, latent_gain, latent_up, out_weight, ffn_gain, gate_weight, up_weight, down_weight, cotangent):
    weights = tuple((item.astype(jnp.float32) for item in (attn_gain, query_down, query_gain, query_up, latent_down, latent_gain, latent_up, out_weight, ffn_gain, gate_weight, up_weight, down_weight)))
    row_count = MICRO * BATCH
    inputs = tokens.astype(jnp.float32).reshape(row_count, SEQ, D)
    segment_rows = segments.reshape(row_count, SEQ)
    upstream = cotangent.astype(jnp.float32).reshape(row_count, SEQ, D)

    def forward(inputs, weights):
        return lax.map(lambda paired: row_forward(paired[0], paired[1], weights), (inputs, segment_rows))
    outputs, pullback = jax.vjp(forward, inputs, weights)
    grad_inputs, grad_weights = pullback(upstream)
    return (outputs.astype(jnp.bfloat16).reshape(tokens.shape), grad_inputs.reshape(tokens.shape), grad_weights[0], grad_weights[1], grad_weights[2], grad_weights[3], grad_weights[4], grad_weights[5], grad_weights[6], grad_weights[7], grad_weights[8], grad_weights[9], grad_weights[10], grad_weights[11])
```

```python
import functools
import math

import jax
import jax.numpy as jnp
from jax import lax
from jax.experimental import pallas as pl
from jax.experimental.pallas import tpu as pltpu
from jax.sharding import PartitionSpec as P

KVR = 256
ROPE = 32
HD = 64
VD = 64
LANES = 128
GAIN_ROWS = 16
TENSOR = 4

norm_eps = 1e-05
branch_scale = 1.4 / math.sqrt(62.0)
rope_base = 10000.0
masked_fill = -1e30
att_scale = (HD + ROPE) ** (-0.5)
att_scale_log2 = att_scale / math.log(2.0)

bf16 = jnp.bfloat16
f32 = jnp.float32


def product(left_side, right_side):
    return jnp.dot(left_side, right_side, preferred_element_type=f32)


def contract_rows(left_side, right_side):
    return lax.dot_general(
        left_side, right_side, (((0,), (0,)), ((), ())), preferred_element_type=f32
    )


def contract_cols(left_side, right_side):
    return lax.dot_general(
        left_side, right_side, (((1,), (1,)), ((), ())), preferred_element_type=f32
    )


def rms_scale(values, gain_vec):
    return (
        values * lax.rsqrt(jnp.mean(values * values, axis=-1, keepdims=True) + norm_eps) * gain_vec
    )


def norm_back(values, gain_vec, gradient):
    return jax.vjp(rms_scale, values, gain_vec)[1](gradient)


def add_low(left_side, right_side):
    return (left_side.astype(f32) + right_side.astype(f32)).astype(bf16)


def turn(values, axis):
    size = lax.axis_size(axis)
    return lax.ppermute(values, axis, [(i, (i + 1) % size) for i in range(size)])


def gather_blocks(shard):
    nx, nz = lax.axis_size("fsdp"), lax.axis_size("ctx")
    x, z = lax.axis_index("fsdp"), lax.axis_index("ctx")
    whole = jnp.zeros((nx * nz,) + shard.shape, shard.dtype)
    piece = shard
    for d in range(nz):
        if d:
            piece = turn(piece, "ctx")
        far = piece
        for e in range(nx):
            if e:
                far = turn(far, "fsdp")
            owner = ((x - e) % nx) * nz + (z - d) % nz
            whole = lax.dynamic_update_slice_in_dim(whole, far[None], owner, 0)
    return whole


def scatter_blocks(blocks):
    nx, nz = lax.axis_size("fsdp"), lax.axis_size("ctx")
    x, z = lax.axis_index("fsdp"), lax.axis_index("ctx")

    def block(xx, zz):
        return lax.dynamic_index_in_dim(blocks, (xx % nx) * nz + zz % nz, 0, keepdims=False)

    total = None
    for d in range(nz):
        part = None
        for e in range(nx):
            own = block(x - 1 - e, z - 1 - d)
            part = own if part is None else add_low(turn(part, "fsdp"), own)
        total = part if total is None else add_low(turn(total, "ctx"), part)
    return total


def gather_ctx(values):
    nz, z = lax.axis_size("ctx"), lax.axis_index("ctx")
    whole = jnp.zeros((nz,) + values.shape, values.dtype)
    piece = values
    for d in range(nz):
        if d:
            piece = turn(piece, "ctx")
        whole = lax.dynamic_update_slice_in_dim(whole, piece[None], (z - d) % nz, 0)
    return whole


def scatter_ctx(blocks):
    nz, z = lax.axis_size("ctx"), lax.axis_index("ctx")
    total = None
    for d in range(nz):
        own = lax.dynamic_index_in_dim(blocks, (z - 1 - d) % nz, 0, keepdims=False)
        total = own if total is None else add_low(turn(total, "ctx"), own)
    return total


def swap(values, bit):
    return lax.ppermute(values, "tensor", [(i, i ^ bit) for i in range(TENSOR)])


def tensor_gather(values):
    far = swap(values, 2)
    near = swap(jnp.stack([values, far]), 1)
    return [values, near[0], far, near[1]]


def tensor_scatter(slots):
    near = swap(jnp.stack([slots[1], slots[3]]), 1)
    kept = add_low(slots[0], near[0])
    far = swap(add_low(slots[2], near[1]), 2)
    return kept.astype(f32) + far.astype(f32)


def reorder(slots):
    t = lax.axis_index("tensor")
    low, high = (t & 1) == 1, (t & 2) == 2
    a = [
        jnp.where(low, slots[1], slots[0]),
        jnp.where(low, slots[0], slots[1]),
        jnp.where(low, slots[3], slots[2]),
        jnp.where(low, slots[2], slots[3]),
    ]
    return [
        jnp.where(high, a[2], a[0]),
        jnp.where(high, a[3], a[1]),
        jnp.where(high, a[0], a[2]),
        jnp.where(high, a[1], a[3]),
    ]


def quarters(values, axis=0):
    return jnp.split(values, TENSOR, axis=axis)


def rotate_lanes(values, cosine, sine):
    lane = lax.broadcasted_iota(jnp.int32, values.shape, 1)
    half = ROPE // 2
    other = jnp.where(
        lane < half, pltpu.roll(values, LANES - half, 1), pltpu.roll(values, half, 1)
    )
    return values * cosine + other * sine


def head_inputs(normed_ref, wq, latent_ref, rope_ref, lup, cos_ref, sin_ref):
    raw = product(normed_ref[0], wq)
    rotated = rotate_lanes(raw[:, LANES:], cos_ref[0], sin_ref[0])
    query = jnp.concatenate([raw[:, :LANES], rotated], axis=1).astype(bf16)
    pair = product(latent_ref[0], lup).astype(bf16)
    key = jnp.concatenate([pair, rope_ref[0]], axis=1)
    return query, pair, key


def allowed_mask(span_ref, shape):
    key_index = lax.broadcasted_iota(jnp.int32, shape, 0)
    return (key_index >= span_ref[0, 0:1, :]) & (key_index <= span_ref[0, 1:2, :])


def attend_kernel(
    normed_ref, wq_ref, latent_ref, rope_ref, lup_ref, cos_ref, sin_ref, span_ref, out_ref, log_ref
):
    found = []
    for j in range(2):
        query, pair, key = head_inputs(
            normed_ref,
            wq_ref[:, 2 * LANES * j : 2 * LANES * (j + 1)],
            latent_ref,
            rope_ref,
            lup_ref[:, LANES * j : LANES * (j + 1)],
            cos_ref,
            sin_ref,
        )
        scores = contract_cols(key, query)
        scores = jnp.where(allowed_mask(span_ref, scores.shape), scores, masked_fill)
        highest = jnp.max(scores, axis=0, keepdims=True)
        exps = jnp.exp2((scores - highest) * att_scale_log2)
        total = jnp.sum(exps, axis=0, keepdims=True)
        probs = (exps * (1.0 / total)).astype(bf16)
        found.append(contract_rows(pair, probs)[HD:, :])
        log_ref[0, 0, j : j + 1, :] = highest * att_scale_log2 + jnp.log2(total)
    out_ref[0] = jnp.concatenate(found, axis=0).T.astype(bf16)


def attend_back_kernel(
    normed_ref,
    wq_ref,
    latent_ref,
    rope_ref,
    lup_ref,
    cos_ref,
    sin_ref,
    span_ref,
    grad_ref,
    log_ref,
    g_normed_ref,
    g_latent_ref,
    g_rope_ref,
    g_wq_ref,
    g_lup_ref,
    sum_wq,
    sum_lup,
):
    step, micro = pl.program_id(0), pl.program_id(1)

    @pl.when(step == 0)
    def _():
        g_normed_ref[micro] = jnp.zeros(g_normed_ref.shape[1:], f32)
        g_latent_ref[micro] = jnp.zeros(g_latent_ref.shape[1:], f32)
        g_rope_ref[micro] = jnp.zeros(g_rope_ref.shape[1:], f32)

    @pl.when(micro == 0)
    def _():
        sum_wq[...] = jnp.zeros_like(sum_wq)
        sum_lup[...] = jnp.zeros_like(sum_lup)

    grad_pair = grad_ref[0].astype(f32)
    lane = lax.broadcasted_iota(jnp.int32, grad_pair.shape, 1)
    for j in range(2):
        wq = wq_ref[:, 2 * LANES * j : 2 * LANES * (j + 1)]
        lup = lup_ref[:, LANES * j : LANES * (j + 1)]
        query, pair, key = head_inputs(
            normed_ref, wq, latent_ref, rope_ref, lup, cos_ref, sin_ref
        )
        grad_head = pltpu.roll(grad_pair, HD, 1) if j == 0 else grad_pair
        grad_head = jnp.where(lane >= HD, grad_head, 0.0).astype(bf16)
        scores = contract_cols(key, query)
        probs = jnp.where(
            allowed_mask(span_ref, scores.shape),
            jnp.exp2(scores * att_scale_log2 - log_ref[0, 0, j : j + 1, :]),
            0.0,
        )
        grad_probs = contract_cols(pair, grad_head)
        delta = jnp.sum(probs * grad_probs, axis=0, keepdims=True)
        grad_scores = (probs * (grad_probs - delta) * att_scale).astype(bf16)
        grad_key = product(grad_scores, query)
        g_rope_ref[micro] += grad_key[:, LANES:]
        grad_key_value = (grad_key[:, :LANES] + product(probs.astype(bf16), grad_head)).astype(bf16)
        grad_query = contract_rows(grad_scores, key)
        rotated = rotate_lanes(grad_query[:, LANES:], cos_ref[0], -sin_ref[0])
        plain = jnp.where(lane < HD, grad_query[:, :LANES], 0.0)
        grad_raw = jnp.concatenate([plain, rotated], axis=1).astype(bf16)
        sum_lup[:, LANES * j : LANES * (j + 1)] += contract_rows(latent_ref[0], grad_key_value)
        g_latent_ref[micro] += contract_cols(grad_key_value, lup)
        sum_wq[:, 2 * LANES * j : 2 * LANES * (j + 1)] += contract_rows(normed_ref[0], grad_raw)
        g_normed_ref[micro] += contract_cols(grad_raw, wq)

    @pl.when(micro == pl.num_programs(1) - 1)
    def _():
        g_wq_ref[...] = sum_wq[...].astype(bf16)
        g_lup_ref[...] = sum_lup[...].astype(bf16)


VMEM_ASKED = 56 * 1024 * 1024


def attend(query_normed, wq, latent_all, rope_all, lup, cosine, sine, spans):
    micros, rows, rank = query_normed.shape
    seq, kvr = latent_all.shape[1:]
    pairs = lup.shape[1] // (2 * LANES)
    flops = 2 * micros * 2 * pairs * (rows * rank * 256 + seq * kvr * 128 + seq * rows * 384)
    return pl.pallas_call(
        attend_kernel,
        grid=(micros, pairs),
        in_specs=[
            pl.BlockSpec((1, rows, rank), lambda m, h: (m, 0, 0)),
            pl.BlockSpec((rank, 4 * LANES), lambda m, h: (0, h)),
            pl.BlockSpec((1, seq, kvr), lambda m, h: (m, 0, 0)),
            pl.BlockSpec((1, seq, LANES), lambda m, h: (m, 0, 0)),
            pl.BlockSpec((kvr, 2 * LANES), lambda m, h: (0, h)),
            pl.BlockSpec((1, rows, LANES), lambda m, h: (m, 0, 0)),
            pl.BlockSpec((1, rows, LANES), lambda m, h: (m, 0, 0)),
            pl.BlockSpec((1, 8, rows), lambda m, h: (m, 0, 0)),
        ],
        out_specs=[
            pl.BlockSpec((1, rows, LANES), lambda m, h: (m, 0, h)),
            pl.BlockSpec((1, 1, 2, rows), lambda m, h: (m, h, 0, 0)),
        ],
        out_shape=[
            jax.ShapeDtypeStruct((micros, rows, pairs * LANES), bf16),
            jax.ShapeDtypeStruct((micros, pairs, 2, rows), f32),
        ],
        compiler_params=pltpu.CompilerParams(vmem_limit_bytes=VMEM_ASKED),
        cost_estimate=pl.CostEstimate(
            flops=flops, bytes_accessed=20_000_000, transcendentals=2 * micros * pairs * seq * rows
        ),
        name="attend",
    )(query_normed, wq, latent_all, rope_all, lup, cosine, sine, spans)


def attend_back(query_normed, wq, latent_all, rope_all, lup, cosine, sine, spans, grads, logs):
    micros, rows, rank = query_normed.shape
    seq, kvr = latent_all.shape[1:]
    pairs = lup.shape[1] // (2 * LANES)
    flops = 2 * micros * 2 * pairs * (rows * rank * 768 + seq * kvr * 384 + seq * rows * 1024)
    return pl.pallas_call(
        attend_back_kernel,
        grid=(pairs, micros),
        in_specs=[
            pl.BlockSpec((1, rows, rank), lambda h, m: (m, 0, 0)),
            pl.BlockSpec((rank, 4 * LANES), lambda h, m: (0, h)),
            pl.BlockSpec((1, seq, kvr), lambda h, m: (m, 0, 0)),
            pl.BlockSpec((1, seq, LANES), lambda h, m: (m, 0, 0)),
            pl.BlockSpec((kvr, 2 * LANES), lambda h, m: (0, h)),
            pl.BlockSpec((1, rows, LANES), lambda h, m: (m, 0, 0)),
            pl.BlockSpec((1, rows, LANES), lambda h, m: (m, 0, 0)),
            pl.BlockSpec((1, 8, rows), lambda h, m: (m, 0, 0)),
            pl.BlockSpec((1, rows, LANES), lambda h, m: (m, 0, h)),
            pl.BlockSpec((1, 1, 2, rows), lambda h, m: (m, h, 0, 0)),
        ],
        out_specs=[
            pl.BlockSpec((micros, rows, rank), lambda h, m: (0, 0, 0)),
            pl.BlockSpec((micros, seq, kvr), lambda h, m: (0, 0, 0)),
            pl.BlockSpec((micros, seq, LANES), lambda h, m: (0, 0, 0)),
            pl.BlockSpec((rank, 4 * LANES), lambda h, m: (0, h)),
            pl.BlockSpec((kvr, 2 * LANES), lambda h, m: (0, h)),
        ],
        out_shape=[
            jax.ShapeDtypeStruct((micros, rows, rank), f32),
            jax.ShapeDtypeStruct((micros, seq, kvr), f32),
            jax.ShapeDtypeStruct((micros, seq, LANES), f32),
            jax.ShapeDtypeStruct((rank, pairs * 4 * LANES), bf16),
            jax.ShapeDtypeStruct((kvr, pairs * 2 * LANES), bf16),
        ],
        scratch_shapes=[
            pltpu.VMEM((rank, 4 * LANES), f32),
            pltpu.VMEM((kvr, 2 * LANES), f32),
        ],
        compiler_params=pltpu.CompilerParams(vmem_limit_bytes=VMEM_ASKED),
        cost_estimate=pl.CostEstimate(
            flops=flops, bytes_accessed=30_000_000, transcendentals=2 * micros * pairs * seq * rows
        ),
        name="attend_back",
    )(query_normed, wq, latent_all, rope_all, lup, cosine, sine, spans, grads, logs)


def on_device(
    tokens,
    segments,
    attn_gain,
    query_down,
    query_gain,
    query_up,
    latent_down,
    latent_gain,
    latent_up,
    out_weight,
    ffn_gain,
    gate_weight,
    up_weight,
    down_weight,
    cotangent,
):
    nx, nz = lax.axis_size("fsdp"), lax.axis_size("ctx")
    owners = nx * nz
    z, t = lax.axis_index("ctx"), lax.axis_index("tensor")
    micros, _, rows, width = tokens.shape
    seq = segments.shape[2]
    count = micros * rows
    share = count // TENSOR
    heads = query_up.shape[1] // (HD + ROPE)
    q_cols, l_cols = query_down.shape[1] // TENSOR, latent_down.shape[1] // TENSOR
    part_cols = q_cols + l_cols
    own_rows = query_down.shape[0]
    gain_sizes = [v.shape[0] for v in (attn_gain, query_gain, latent_gain, ffn_gain)]
    gain_total = sum(gain_sizes)

    down_part = jnp.concatenate(
        [
            lax.dynamic_slice_in_dim(query_down, t * q_cols, q_cols, 1),
            lax.dynamic_slice_in_dim(latent_down, t * l_cols, l_cols, 1),
        ],
        axis=1,
    )
    gains = jnp.concatenate([attn_gain, query_gain, latent_gain, ffn_gain])
    gains = jnp.pad(gains, (0, GAIN_ROWS * part_cols - gain_total)).reshape(GAIN_ROWS, part_cols)
    bundle = gather_blocks(jnp.concatenate([down_part, gains], axis=0))
    down_cols = bundle[:, :own_rows].reshape(width, part_cols)
    gain_blocks = bundle[:, own_rows:].reshape(owners, -1).astype(f32)
    gain_list, start = [], 0
    for size in gain_sizes:
        gain_list.append(gain_blocks[:, start : start + size].reshape(-1))
        start += size
    gain_attn, gain_query, gain_latent, gain_ffn = gain_list

    def whole_weight(shard):
        return gather_blocks(shard).reshape((-1,) + shard.shape[1:])

    up_query = whole_weight(query_up)
    up_latent = whole_weight(latent_up)
    weight_out = whole_weight(out_weight)
    weight_gate = whole_weight(gate_weight)
    weight_up = whole_weight(up_weight)
    weight_down = whole_weight(down_weight)
    down_slots = tensor_gather(down_cols)

    seg = segments[:, 0]
    first_end = jnp.sum((seg < 1).astype(jnp.int32), axis=1, keepdims=True)
    second_end = jnp.sum((seg < 2).astype(jnp.int32), axis=1, keepdims=True)
    starts = jnp.where(seg < 1, 0, jnp.where(seg < 2, first_end, second_end))
    index = jnp.arange(seq, dtype=jnp.int32)
    places = (index[None, :] - starts).astype(f32)
    lane = jnp.arange(LANES, dtype=jnp.int32)
    half = ROPE // 2
    frequency = rope_base ** (-(lane % half).astype(f32) * (2.0 / ROPE))
    angles = places[:, :, None] * frequency
    cos_all = jnp.where(lane < ROPE, jnp.cos(angles), 0.0)
    sin_all = jnp.where(lane < ROPE, jnp.sin(angles), 0.0) * jnp.where(lane < half, -1.0, 1.0)
    cos_own = lax.dynamic_slice_in_dim(cos_all, z * rows, rows, 1)
    sin_own = lax.dynamic_slice_in_dim(sin_all, z * rows, rows, 1)
    own_starts = lax.dynamic_slice_in_dim(starts, z * rows, rows, 1)
    own_index = jnp.broadcast_to(z * rows + jnp.arange(rows, dtype=jnp.int32), own_starts.shape)
    spans = jnp.pad(jnp.stack([own_starts, own_index], axis=1), ((0, 0), (0, 6), (0, 0)))

    def rotated(values, cosine, sine):
        first, second = values[..., :half], values[..., half:]
        return jnp.concatenate(
            [first * cosine - second * sine, first * sine + second * cosine], axis=-1
        )

    inputs_low = tokens.reshape(count, width)
    normed = rms_scale(inputs_low.astype(f32), gain_attn).astype(bf16)
    raw = product(normed, down_cols).astype(bf16)
    query_latent = jnp.concatenate(reorder(tensor_gather(raw[:, :q_cols])), axis=1)
    latent_cols = gather_ctx(raw[:, q_cols:])
    latent_raw = jnp.concatenate(reorder(tensor_gather(latent_cols)), axis=2)
    query_normed = rms_scale(query_latent.astype(f32), gain_query).astype(bf16)
    latent_rows = (
        latent_raw.reshape(nz, micros, rows, KVR + ROPE)
        .transpose(1, 0, 2, 3)
        .reshape(micros, seq, KVR + ROPE)
        .astype(f32)
    )
    latent_all = rms_scale(latent_rows[..., :KVR], gain_latent).astype(bf16)
    rope_all = rotated(
        latent_rows[..., KVR:], cos_all[..., :half], sin_all[..., half:ROPE]
    ).astype(bf16)
    rope_all = jnp.pad(rope_all, ((0, 0), (0, 0), (0, LANES - ROPE)))

    column = jnp.arange(heads * (HD + ROPE), dtype=jnp.int32)
    feature = column % (HD + ROPE)
    target = (column // (HD + ROPE)) * (2 * LANES) + jnp.where(
        feature < HD, feature, feature - HD + LANES
    )
    spread = (target[:, None] == jnp.arange(heads * 2 * LANES)[None, :]).astype(bf16)
    wq = product(up_query, spread).astype(bf16)
    query_normed_rows = query_normed.reshape(micros, rows, -1)
    attended, logs = attend(
        query_normed_rows, wq, latent_all, rope_all, up_latent, cos_own, sin_own, spans
    )

    attended_slots = jnp.concatenate(reorder(quarters(attended.reshape(count, -1))), axis=0)
    attn_share = tensor_scatter(
        quarters(contract_cols(attended_slots, weight_out).astype(bf16))
    )
    tokens_share = lax.dynamic_slice_in_dim(inputs_low, t * share, share, 0).astype(f32)
    middle = tokens_share + branch_scale * attn_share
    ffn_in = jnp.concatenate(
        tensor_gather(rms_scale(middle, gain_ffn).astype(bf16)), axis=0
    )
    gate_val = product(ffn_in, weight_gate)
    up_val = product(ffn_in, weight_up)
    gate_sig = jax.nn.sigmoid(gate_val)
    hidden = (gate_val * gate_sig * up_val).astype(bf16)
    ffn_share = tensor_scatter(quarters(contract_cols(hidden, weight_down).astype(bf16)))
    mixed_share = (middle + branch_scale * ffn_share).astype(bf16)
    mixed = jnp.concatenate(reorder(tensor_gather(mixed_share)), axis=0)

    upstream_low = cotangent.reshape(count, width)
    upstream_slots = jnp.concatenate(reorder(quarters(upstream_low)), axis=0)
    upstream_share = upstream_slots[:share].astype(f32)
    grad_ffn = (branch_scale * upstream_slots.astype(f32)).astype(bf16)
    grad_hidden = product(grad_ffn, weight_down)
    grad_gate = (grad_hidden * up_val * gate_sig * (1.0 + gate_val * (1.0 - gate_sig))).astype(bf16)
    grad_up = (grad_hidden * gate_val * gate_sig).astype(bf16)
    grad_ffn_in = tensor_scatter(
        quarters(
            (contract_cols(grad_gate, weight_gate) + contract_cols(grad_up, weight_up)).astype(bf16)
        )
    )

    def blocks_of(gradient):
        return gradient.astype(bf16).reshape((owners, -1) + gradient.shape[1:])

    out_down = scatter_blocks(blocks_of(contract_rows(grad_ffn, hidden))).astype(f32)
    out_gate = scatter_blocks(blocks_of(contract_rows(ffn_in, grad_gate))).astype(f32)
    out_up = scatter_blocks(blocks_of(contract_rows(ffn_in, grad_up))).astype(f32)
    grad_middle, grad_gain_ffn = norm_back(middle, gain_ffn, grad_ffn_in)
    grad_middle = grad_middle + upstream_share

    grad_attn = jnp.concatenate(
        tensor_gather((branch_scale * grad_middle).astype(bf16)), axis=0
    )
    grad_attended = product(grad_attn, weight_out).astype(bf16)
    grad_attended = jnp.concatenate(reorder(quarters(grad_attended)), axis=0)
    out_out = scatter_blocks(blocks_of(contract_rows(grad_attn, attended_slots))).astype(f32)
    g_normed, g_latent, g_rope, g_wq, g_lup = attend_back(
        query_normed_rows,
        wq,
        latent_all,
        rope_all,
        up_latent,
        cos_own,
        sin_own,
        spans,
        grad_attended.reshape(micros, rows, -1),
        logs,
    )
    out_query_up = scatter_blocks(blocks_of(contract_cols(g_wq, spread))).astype(f32)
    out_latent_up = scatter_blocks(blocks_of(g_lup)).astype(f32)
    latent_part = (
        jnp.concatenate([g_latent, g_rope[..., :ROPE]], axis=2)
        .astype(bf16)
        .reshape(micros, nz, rows, KVR + ROPE)
        .transpose(1, 0, 2, 3)
        .reshape(nz, count, KVR + ROPE)
    )
    g_latent_share = scatter_ctx(
        tensor_scatter(reorder(quarters(latent_part, 1))).astype(bf16)
    ).astype(f32)
    g_query_share = tensor_scatter(
        reorder(quarters(g_normed.astype(bf16).reshape(count, -1)))
    )

    def own_share(values):
        return lax.dynamic_slice_in_dim(values, t * share, share, 0).astype(f32)

    grad_query_latent, grad_gain_query = norm_back(
        own_share(query_latent), gain_query, g_query_share
    )
    own_latent = own_share(lax.dynamic_index_in_dim(latent_raw, z, 0, keepdims=False))
    grad_latent_first, grad_gain_latent = norm_back(
        own_latent[:, :KVR], gain_latent, g_latent_share[:, :KVR]
    )
    cos_share = own_share(cos_own.reshape(count, LANES))[:, :half]
    sin_share = own_share(sin_own.reshape(count, LANES))[:, half:ROPE]
    grad_latent_raw = jnp.concatenate(
        [grad_latent_first, rotated(g_latent_share[:, KVR:], cos_share, -sin_share)], axis=1
    ).astype(bf16)
    grad_query_latent = grad_query_latent.astype(bf16)
    query_parts = quarters(grad_query_latent, 1)
    latent_parts = quarters(grad_latent_raw, 1)
    column_slots = reorder(
        [jnp.concatenate([a, b], axis=1) for a, b in zip(query_parts, latent_parts)]
    )
    grad_normed = contract_cols(
        jnp.concatenate(column_slots, axis=1), jnp.concatenate(down_slots, axis=1)
    )
    grad_inputs, grad_gain_attn = norm_back(tokens_share, gain_attn, grad_normed)
    grad_share = (grad_inputs + grad_middle).astype(bf16)
    grad_tokens = jnp.concatenate(reorder(tensor_gather(grad_share)), axis=0).astype(f32)

    near = swap(jnp.stack([column_slots[1], column_slots[3]]), 1)
    far = swap(jnp.stack([column_slots[2], near[1]]), 2)
    own_columns = jnp.concatenate(
        reorder([column_slots[0], near[0], far[0], far[1]]), axis=0
    )
    grad_down_cols = blocks_of(contract_rows(normed, own_columns))
    gain_grads = jnp.concatenate(
        [
            g.reshape(owners, -1)
            for g in (grad_gain_attn, grad_gain_query, grad_gain_latent, grad_gain_ffn)
        ],
        axis=1,
    ).astype(bf16)
    gain_grads = jnp.pad(
        gain_grads, ((0, 0), (0, GAIN_ROWS * part_cols - gain_total))
    ).reshape(owners, GAIN_ROWS, part_cols)
    bundle_share = scatter_blocks(jnp.concatenate([grad_down_cols, gain_grads], axis=1))
    bundle_slots = tensor_gather(bundle_share)
    bundle_list = reorder(bundle_slots)
    out_query_down = jnp.concatenate([b[:own_rows, :q_cols] for b in bundle_list], axis=1)
    out_latent_down = jnp.concatenate([b[:own_rows, q_cols:] for b in bundle_list], axis=1)
    gain_sum = sum(b[own_rows:].astype(f32) for b in bundle_list).reshape(-1)
    out_gains, start = [], 0
    for size in gain_sizes:
        out_gains.append(gain_sum[start : start + size])
        start += size

    return (
        mixed.reshape(tokens.shape),
        grad_tokens.reshape(tokens.shape),
        out_gains[0],
        out_query_down.astype(f32),
        out_gains[1],
        out_query_up,
        out_latent_down.astype(f32),
        out_gains[2],
        out_latent_up,
        out_out,
        out_gains[3],
        out_gate,
        out_up,
        out_down,
    )


def solution(mesh):
    return jax.shard_map(
        on_device,
        mesh=mesh,
        in_specs=(
            P(None, "fsdp", "ctx", None),
            P(None, "fsdp", None),
            P(("fsdp", "ctx")),
            P(("fsdp", "ctx"), None),
            P(("fsdp", "ctx")),
            P(("fsdp", "ctx"), "tensor"),
            P(("fsdp", "ctx"), None),
            P(("fsdp", "ctx")),
            P(("fsdp", "ctx"), "tensor"),
            P(("fsdp", "ctx"), "tensor"),
            P(("fsdp", "ctx")),
            P(("fsdp", "ctx"), "tensor"),
            P(("fsdp", "ctx"), "tensor"),
            P(("fsdp", "ctx"), "tensor"),
            P(None, "fsdp", "ctx", None),
        ),
        out_specs=(
            P(None, "fsdp", "ctx", None),
            P(None, "fsdp", "ctx", None),
            P(("fsdp", "ctx")),
            P(("fsdp", "ctx"), None),
            P(("fsdp", "ctx")),
            P(("fsdp", "ctx"), "tensor"),
            P(("fsdp", "ctx"), None),
            P(("fsdp", "ctx")),
            P(("fsdp", "ctx"), "tensor"),
            P(("fsdp", "ctx"), "tensor"),
            P(("fsdp", "ctx")),
            P(("fsdp", "ctx"), "tensor"),
            P(("fsdp", "ctx"), "tensor"),
            P(("fsdp", "ctx"), "tensor"),
        ),
        check_vma=False,
    )
```

```python
import functools
import math

import jax
import jax.numpy as jnp
from jax import lax
from jax.experimental import pallas as pl
from jax.experimental.pallas import tpu as pltpu
from jax.sharding import PartitionSpec as P

KVR = 256
ROPE = 32
HD = 64
VD = 64
LANES = 128
GAIN_ROWS = 16
TENSOR = 4

norm_eps = 1e-05
branch_scale = 1.4 / math.sqrt(62.0)
rope_base = 10000.0
masked_fill = -1e30
att_scale = (HD + ROPE) ** (-0.5)
att_scale_log2 = att_scale / math.log(2.0)

bf16 = jnp.bfloat16
f32 = jnp.float32


def product(left_side, right_side):
    return jnp.dot(left_side, right_side, preferred_element_type=f32)


def contract_rows(left_side, right_side):
    return lax.dot_general(
        left_side, right_side, (((0,), (0,)), ((), ())), preferred_element_type=f32
    )


def contract_cols(left_side, right_side):
    return lax.dot_general(
        left_side, right_side, (((1,), (1,)), ((), ())), preferred_element_type=f32
    )


def rms_scale(values, gain_vec):
    return (
        values * lax.rsqrt(jnp.mean(values * values, axis=-1, keepdims=True) + norm_eps) * gain_vec
    )


def norm_back(values, gain_vec, gradient):
    return jax.vjp(rms_scale, values, gain_vec)[1](gradient)


def add_low(left_side, right_side):
    return (left_side.astype(f32) + right_side.astype(f32)).astype(bf16)


def after(values, *others):
    return lax.optimization_barrier((values,) + others)[0]


def turn(values, axis):
    size = lax.axis_size(axis)
    return lax.ppermute(values, axis, [(i, (i + 1) % size) for i in range(size)])


class Order:
    def __init__(self):
        self.events = []

    def __call__(self, values):
        return after(values, *self.events[-6:]) if self.events else values

    def mark(self, event):
        self.events.append(event)


class Buffer:
    def __init__(self, shape, order):
        sizes = (lax.axis_size("fsdp"), lax.axis_size("ctx"))
        self.whole = jnp.broadcast_to(order(jnp.zeros((), bf16)), sizes + shape)

    def place(self, piece, x, z, row):
        self.whole = lax.dynamic_update_slice(self.whole, piece, (x, z, row, 0))

    def result(self):
        return self.whole.reshape((-1,) + self.whole.shape[2:])


class Gather:
    def __init__(self, shard):
        self.nx, self.nz = lax.axis_size("fsdp"), lax.axis_size("ctx")
        self.x, self.z = lax.axis_index("fsdp"), lax.axis_index("ctx")
        self.piece = shard
        self.step = 0
        self.waiting = []

    def start_x(self, order):
        far = order(self.piece)
        self.waiting.append((far, 0, self.step))
        self.sent = True
        for e in range(1, self.nx):
            far = turn(far, "fsdp")
            self.waiting.append((far, e, self.step))

    def start_z(self, order):
        if self.step + 1 < self.nz:
            self.piece = turn(order(self.piece), "ctx")
            self.step += 1

    def pass_on(self, order):
        held, step = self.piece, self.step
        self.start_z(order)
        piece, self.piece, self.step = self.piece, held, step
        self.start_x(order)
        if step + 1 < self.nz:
            self.piece, self.step = piece, step + 1

    def arrive(self, order):
        order.mark((self.piece, self.waiting[-1][0]) if self.waiting else self.piece)

    def place_old(self, buffer, order, row=0):
        last = self.waiting[-1][2]
        late = [w for w in self.waiting if w[2] == last]
        self.waiting = [w for w in self.waiting if w[2] != last]
        self.place(buffer, order, row)
        self.waiting = late

    def place(self, buffer, order, row=0):
        for far, e, step in self.waiting:
            buffer.place(
                order(far)[None, None], (self.x - e) % self.nx, (self.z - step) % self.nz, row
            )
        self.waiting = []


class PairGather:
    def __init__(self, shard, order):
        self.nx, self.nz = lax.axis_size("fsdp"), lax.axis_size("ctx")
        self.x, self.z = lax.axis_index("fsdp"), lax.axis_index("ctx")
        self.far = [order(shard)]
        for e in range(1, self.nx):
            self.far.append(turn(self.far[-1], "fsdp"))
        self.step = 0

    def line(self, order):
        piece = jnp.broadcast_to(order(jnp.zeros((), bf16)), (self.nx, 1) + self.far[0].shape)
        for e, far in enumerate(self.far):
            piece = lax.dynamic_update_slice(
                piece, order(far)[None, None], ((self.x - e) % self.nx, 0, 0, 0)
            )
        self.piece = piece

    def start_z(self, order):
        self.before = self.piece
        self.piece = turn(order(self.piece), "ctx")
        self.step += 1

    def arrive(self, order):
        order.mark(self.piece)

    def place_before(self, buffer, order, row):
        buffer.place(order(self.before), 0, (self.z - self.step + 1) % self.nz, row)

    def place(self, buffer, order, row):
        buffer.place(order(self.piece), 0, (self.z - self.step) % self.nz, row)


class Scatter:
    def __init__(self, blocks, groups):
        self.nx, self.nz = lax.axis_size("fsdp"), lax.axis_size("ctx")
        self.x, self.z = lax.axis_index("fsdp"), lax.axis_index("ctx")
        self.blocks = blocks
        self.size = self.nz // groups
        self.far = []
        self.total = None
        self.step = 0

    def own(self, e, d):
        owner = ((self.x - 1 - e) % self.nx) * self.nz + (self.z - 1 - d) % self.nz
        return lax.dynamic_index_in_dim(self.blocks, owner, 0, keepdims=False)

    def start_x(self, order):
        first = len(self.far) * self.size
        blocks, self.blocks = self.blocks, order(self.blocks)
        part = None
        for e in range(self.nx - 1):
            own = jnp.stack([self.own(e, first + k) for k in range(self.size)])
            part = turn(own if part is None else add_low(part, own), "fsdp")
        self.blocks = blocks
        self.far.append(part)

    def arrive(self, order):
        order.mark(self.far[-1])

    def forward(self, order):
        d = self.step
        total = self.own(self.nx - 1, d).astype(f32)
        if self.nx > 1:
            total = total + order(self.far[d // self.size])[d % self.size].astype(f32)
        if d:
            total = total + order(self.total).astype(f32)
        self.step += 1
        if self.step == self.nz:
            self.total = total
        else:
            total = total.astype(bf16)
            order.mark(total)
            self.total = turn(total, "ctx")


class PairScatter:
    def __init__(self, blocks, order):
        self.nx, self.nz = lax.axis_size("fsdp"), lax.axis_size("ctx")
        self.x, self.z = lax.axis_index("fsdp"), lax.axis_index("ctx")
        self.blocks = order(blocks).reshape((self.nx, self.nz) + blocks.shape[1:])
        self.step = 0
        self.total = turn(self.own(0), "ctx")

    def own(self, d):
        return lax.dynamic_index_in_dim(
            self.blocks, (self.z - 1 - d) % self.nz, 1, keepdims=False
        )

    def forward(self, order):
        self.step += 1
        total = add_low(order(self.total), self.own(self.step))
        order.mark(total)
        if self.step + 1 < self.nz:
            self.total = turn(total, "ctx")
            return
        part = None
        for e in range(self.nx):
            own = lax.dynamic_index_in_dim(total, (self.x - 1 - e) % self.nx, 0, keepdims=False)
            part = own if part is None else add_low(turn(part, "fsdp"), own)
        self.total = part

    def result(self):
        return self.total.astype(f32)


def shift(values, d):
    size = lax.axis_size("ctx")
    return lax.ppermute(values, "ctx", [(i, (i + d) % size) for i in range(size)])


def gather_ctx(values):
    nz, z = lax.axis_size("ctx"), lax.axis_index("ctx")
    pieces = [values] + [shift(values, d) for d in range(1, nz)]
    whole = jnp.zeros((nz,) + values.shape, values.dtype)
    for d, piece in enumerate(pieces):
        whole = lax.dynamic_update_slice_in_dim(whole, piece[None], (z - d) % nz, 0)
    return whole


def scatter_ctx(blocks):
    nz, z = lax.axis_size("ctx"), lax.axis_index("ctx")
    blocks = blocks.astype(bf16)
    total = None
    for d in range(nz):
        part = lax.dynamic_index_in_dim(blocks, (z + d) % nz, 0, keepdims=False)
        part = shift(part, d) if d else part
        total = part.astype(f32) if total is None else total + part.astype(f32)
    return total


SLOTS = (0, 2, 1, 3)


def swap(values, bit):
    return lax.ppermute(values, "tensor", [(i, i ^ bit) for i in range(TENSOR)])


def tensor_gather(values):
    near = swap(values, 1)
    far = swap(values, 2)
    return [values, far, near, swap(far, 1)]


def tensor_gather_now(values, order):
    order.mark(values)
    slots = tensor_gather(values)
    order.mark(tuple(slots[1:]))
    return slots


def tensor_scatter(kept, sent):
    near = swap(sent, 1)
    far = swap(add_low(kept[1], near[1]), 2)
    return kept[0].astype(f32) + near[0].astype(f32) + far.astype(f32)


def to_slots(blocks, axis=0):
    t = lax.axis_index("tensor")
    return [lax.dynamic_index_in_dim(blocks, t ^ j, axis, keepdims=False) for j in SLOTS]


def from_slots(slots):
    t = lax.axis_index("tensor")
    low, high = (t & 1) == 1, (t & 2) == 2
    own, far, near, both = slots
    a = [
        jnp.where(low, near, own),
        jnp.where(low, own, near),
        jnp.where(low, both, far),
        jnp.where(low, far, both),
    ]
    return [
        jnp.where(high, a[2], a[0]),
        jnp.where(high, a[3], a[1]),
        jnp.where(high, a[0], a[2]),
        jnp.where(high, a[1], a[3]),
    ]


MESH = pl.DeviceIdType.MESH
FRONT = 5


def front_kernel(nx, nz, *refs):
    shards, outs = refs[:FRONT], refs[FRONT : 2 * FRONT]
    own_sem, z_send, z_recv, x_send, x_recv, t_send, t_recv = refs[2 * FRONT :]
    x, z, t = lax.axis_index("fsdp"), lax.axis_index("ctx"), lax.axis_index("tensor")
    right_x, left_x = lax.rem(x + 1, nx), lax.rem(x + nx - 1, nx)
    right_z, left_z = lax.rem(z + 1, nz), lax.rem(z + nz - 1, nz)
    near_t = t + 1 - 2 * lax.rem(t, 2)
    far_t = lax.rem(t + 2, TENSOR)

    barrier = pltpu.get_barrier_semaphore()
    partners = (
        {"fsdp": right_x},
        {"fsdp": left_x},
        {"ctx": right_z},
        {"ctx": left_z},
        {"tensor": near_t},
        {"tensor": far_t},
    )
    for partner in partners:
        pl.semaphore_signal(barrier, 1, device_id=partner, device_id_type=MESH)
    pl.semaphore_wait(barrier, len(partners))

    def block(a, xx, zz):
        return outs[a].at[xx, zz, t] if a == 0 else outs[a].at[xx, zz]

    def own(a):
        return pltpu.make_async_copy(shards[a], block(a, x, z), own_sem.at[a])

    def along_z(a, d):
        zz = lax.rem(z + nz - d, nz)
        return pltpu.make_async_remote_copy(
            src_ref=shards[a] if d == 0 else block(a, x, zz),
            dst_ref=block(a, x, zz),
            send_sem=z_send.at[a, d],
            recv_sem=z_recv.at[a, d],
            device_id={"ctx": right_z},
            device_id_type=MESH,
        )

    def along_x(a, d, e):
        xx, zz = lax.rem(x + nx - e, nx), lax.rem(z + nz - d, nz)
        return pltpu.make_async_remote_copy(
            src_ref=shards[a] if d + e == 0 else block(a, xx, zz),
            dst_ref=block(a, xx, zz),
            send_sem=x_send.at[a, d, e],
            recv_sem=x_recv.at[a, d, e],
            device_id={"fsdp": right_x},
            device_id_type=MESH,
        )

    def along_t(k, owner, partner):
        part = outs[0].at[:, :, owner]
        return pltpu.make_async_remote_copy(
            src_ref=part,
            dst_ref=part,
            send_sem=t_send.at[k],
            recv_sem=t_recv.at[k],
            device_id={"tensor": partner},
            device_id_type=MESH,
        )

    early, late = (0, 1), (2, 3, 4)
    for a in range(FRONT):
        own(a).start()
    for a in early:
        along_z(a, 0).start()
        along_x(a, 0, 0).start()
    for d in range(1, nz):
        for a in early:
            along_z(a, d - 1).wait_recv()
            if d + 1 < nz:
                along_z(a, d).start()
            along_x(a, d, 0).start()
    for a in late:
        along_z(a, 0).start()
        along_x(a, 0, 0).start()
    for d in range(nz):
        for e in range(1, nx):
            for a in early:
                along_x(a, d, e - 1).wait_recv()
                if e + 1 < nx:
                    along_x(a, d, e).start()
    own(0).wait()
    along_t(0, t, near_t).start()
    along_t(1, t, far_t).start()
    for d in range(1, nz):
        for a in late:
            along_z(a, d - 1).wait_recv()
            if d + 1 < nz:
                along_z(a, d).start()
            along_x(a, d, 0).start()
    along_t(1, t, far_t).wait_recv()
    along_t(2, far_t, near_t).start()
    for d in range(nz):
        for e in range(1, nx):
            for a in late:
                along_x(a, d, e - 1).wait_recv()
                if e + 1 < nx:
                    along_x(a, d, e).start()
    along_t(0, t, near_t).wait_recv()
    along_t(2, far_t, near_t).wait_recv()
    for a in range(1, FRONT):
        own(a).wait()
    for a in range(FRONT):
        for d in range(nz):
            if d + 1 < nz:
                along_z(a, d).wait_send()
            for e in range(nx - 1):
                along_x(a, d, e).wait_send()
    along_t(0, t, near_t).wait_send()
    along_t(1, t, far_t).wait_send()
    along_t(2, far_t, near_t).wait_send()


def front_gather(down, gains, query_up, latent_up, out_weight):
    nx, nz = lax.axis_size("fsdp"), lax.axis_size("ctx")
    shards = (down, gains, query_up, latent_up, out_weight)
    shapes = [
        jax.ShapeDtypeStruct((nx, nz) + ((TENSOR,) if a == 0 else ()) + v.shape, v.dtype)
        for a, v in enumerate(shards)
    ]
    return pl.pallas_call(
        functools.partial(front_kernel, nx, nz),
        in_specs=[pl.BlockSpec(memory_space=pl.ANY)] * FRONT,
        out_specs=[pl.BlockSpec(memory_space=pl.ANY)] * FRONT,
        out_shape=shapes,
        scratch_shapes=[
            pltpu.SemaphoreType.DMA((FRONT,)),
            pltpu.SemaphoreType.DMA((FRONT, nz)),
            pltpu.SemaphoreType.DMA((FRONT, nz)),
            pltpu.SemaphoreType.DMA((FRONT, nz, nx)),
            pltpu.SemaphoreType.DMA((FRONT, nz, nx)),
            pltpu.SemaphoreType.DMA((3,)),
            pltpu.SemaphoreType.DMA((3,)),
        ],
        compiler_params=pltpu.CompilerParams(collective_id=0, has_side_effects=True),
        cost_estimate=cost(88),
        name="front_gather",
    )(*shards)


def rotate_lanes(values, cosine, sine):
    lane = lax.broadcasted_iota(jnp.int32, values.shape, 1)
    half = ROPE // 2
    other = jnp.where(
        lane < half, pltpu.roll(values, LANES - half, 1), pltpu.roll(values, half, 1)
    )
    return values * cosine + other * sine


def head_inputs(normed_ref, wq, latent, rope, lup, cos_ref, sin_ref):
    raw = product(normed_ref[0], wq)
    rotated = rotate_lanes(raw[:, LANES:], cos_ref[0], sin_ref[0])
    query = jnp.concatenate([raw[:, :LANES], rotated], axis=1).astype(bf16)
    pair = product(latent, lup).astype(bf16)
    key = jnp.concatenate([pair, rope], axis=1)
    return query, pair, key


def latent_rows(latent_ref):
    nz, _, rows, lanes = latent_ref.shape
    held = latent_ref[...].reshape(nz * rows, lanes)
    return held[:, :KVR], held[:, KVR:]


def allowed_mask(span_ref, shape):
    key_index = lax.broadcasted_iota(jnp.int32, shape, 0)
    return (key_index >= span_ref[0, 0:1, :]) & (key_index <= span_ref[0, 1:2, :])


def attend_kernel(
    normed_ref, wq_ref, latent_ref, lup_ref, cos_ref, sin_ref, span_ref, out_ref, log_ref
):
    latent, rope = latent_rows(latent_ref)
    found = []
    for j in range(2):
        query, pair, key = head_inputs(
            normed_ref,
            wq_ref[:, 2 * LANES * j : 2 * LANES * (j + 1)],
            latent,
            rope,
            lup_ref[:, LANES * j : LANES * (j + 1)],
            cos_ref,
            sin_ref,
        )
        scores = contract_cols(key, query)
        scores = jnp.where(allowed_mask(span_ref, scores.shape), scores, masked_fill)
        highest = jnp.max(scores, axis=0, keepdims=True)
        exps = jnp.exp2((scores - highest) * att_scale_log2)
        total = jnp.sum(exps, axis=0, keepdims=True)
        probs = (exps * (1.0 / total)).astype(bf16)
        found.append(contract_rows(pair, probs)[HD:, :])
        log_ref[0, 0, j : j + 1, :] = highest * att_scale_log2 + jnp.log2(total)
    out_ref[0] = jnp.concatenate(found, axis=0).T.astype(bf16)


def attend_back_kernel(
    normed_ref,
    wq_ref,
    latent_ref,
    lup_ref,
    cos_ref,
    sin_ref,
    span_ref,
    grad_ref,
    log_ref,
    g_normed_ref,
    g_latent_ref,
    g_wq_ref,
    g_lup_ref,
    sum_normed,
    sum_latent,
    sum_wq,
    sum_lup,
):
    step, micro = pl.program_id(0), pl.program_id(1)

    @pl.when(step == 0)
    def _():
        sum_normed[micro] = jnp.zeros(sum_normed.shape[1:], f32)
        sum_latent[micro] = jnp.zeros(sum_latent.shape[1:], f32)

    @pl.when(micro == 0)
    def _():
        sum_wq[...] = jnp.zeros_like(sum_wq)
        sum_lup[...] = jnp.zeros_like(sum_lup)

    latent, rope = latent_rows(latent_ref)
    grad_pair = grad_ref[0].astype(f32)
    lane = lax.broadcasted_iota(jnp.int32, grad_pair.shape, 1)
    for j in range(2):
        wq = wq_ref[:, 2 * LANES * j : 2 * LANES * (j + 1)]
        lup = lup_ref[:, LANES * j : LANES * (j + 1)]
        query, pair, key = head_inputs(normed_ref, wq, latent, rope, lup, cos_ref, sin_ref)
        grad_head = pltpu.roll(grad_pair, HD, 1) if j == 0 else grad_pair
        grad_head = jnp.where(lane >= HD, grad_head, 0.0).astype(bf16)
        scores = contract_cols(key, query)
        probs = jnp.where(
            allowed_mask(span_ref, scores.shape),
            jnp.exp2(scores * att_scale_log2 - log_ref[0, 0, j : j + 1, :]),
            0.0,
        )
        grad_probs = contract_cols(pair, grad_head)
        delta = jnp.sum(probs * grad_probs, axis=0, keepdims=True)
        grad_scores = (probs * (grad_probs - delta) * att_scale).astype(bf16)
        grad_key = product(grad_scores, query)
        sum_latent[micro, :, KVR:] += grad_key[:, LANES:]
        grad_key_value = (grad_key[:, :LANES] + product(probs.astype(bf16), grad_head)).astype(bf16)
        grad_query = contract_rows(grad_scores, key)
        rotated = rotate_lanes(grad_query[:, LANES:], cos_ref[0], -sin_ref[0])
        plain = jnp.where(lane < HD, grad_query[:, :LANES], 0.0)
        grad_raw = jnp.concatenate([plain, rotated], axis=1).astype(bf16)
        sum_lup[:, LANES * j : LANES * (j + 1)] += contract_rows(latent, grad_key_value)
        sum_latent[micro, :, :KVR] += contract_cols(grad_key_value, lup)
        sum_wq[:, 2 * LANES * j : 2 * LANES * (j + 1)] += contract_rows(normed_ref[0], grad_raw)
        sum_normed[micro] += contract_cols(grad_raw, wq)

    @pl.when(micro == pl.num_programs(1) - 1)
    def _():
        g_wq_ref[...] = sum_wq[...].astype(bf16)
        g_lup_ref[...] = sum_lup[...].astype(bf16)

    @pl.when(step == pl.num_programs(0) - 1)
    def _():
        g_normed_ref[micro] = sum_normed[micro].astype(bf16)
        nz, _, rows, lanes = g_latent_ref.shape
        g_latent_ref[:, micro] = sum_latent[micro].astype(bf16).reshape(nz, rows, lanes)


def cost(microseconds):
    return pl.CostEstimate(
        flops=int(microseconds * 1.15e9), bytes_accessed=1, transcendentals=0
    )


VMEM_ATTEND = 56 * 1024 * 1024
VMEM_FFN = 40 * 1024 * 1024


def attend(query_normed, wq, latent_all, lup, cosine, sine, spans):
    micros, rows, rank = query_normed.shape
    nz, _, _, lanes = latent_all.shape
    seq, kvr = nz * rows, KVR
    pairs = lup.shape[1] // (2 * LANES)
    return pl.pallas_call(
        attend_kernel,
        grid=(micros, pairs),
        in_specs=[
            pl.BlockSpec((1, rows, rank), lambda m, h: (m, 0, 0)),
            pl.BlockSpec((rank, 4 * LANES), lambda m, h: (0, h)),
            pl.BlockSpec((nz, 1, rows, lanes), lambda m, h: (0, m, 0, 0)),
            pl.BlockSpec((kvr, 2 * LANES), lambda m, h: (0, h)),
            pl.BlockSpec((1, rows, LANES), lambda m, h: (m, 0, 0)),
            pl.BlockSpec((1, rows, LANES), lambda m, h: (m, 0, 0)),
            pl.BlockSpec((1, 8, rows), lambda m, h: (m, 0, 0)),
        ],
        out_specs=[
            pl.BlockSpec((1, rows, LANES), lambda m, h: (m, 0, h)),
            pl.BlockSpec((1, 1, 2, rows), lambda m, h: (m, h, 0, 0)),
        ],
        out_shape=[
            jax.ShapeDtypeStruct((micros, rows, pairs * LANES), bf16),
            jax.ShapeDtypeStruct((micros, pairs, 2, rows), f32),
        ],
        compiler_params=pltpu.CompilerParams(vmem_limit_bytes=VMEM_ATTEND),
        cost_estimate=cost(42),
        name="attend",
    )(query_normed, wq, latent_all, lup, cosine, sine, spans)


def attend_back(first, pairs, query_normed, wq, latent_all, lup, cosine, sine, spans, grads, logs):
    micros, rows, rank = query_normed.shape
    nz, _, _, lanes = latent_all.shape
    seq, kvr = nz * rows, KVR
    return pl.pallas_call(
        attend_back_kernel,
        grid=(pairs, micros),
        in_specs=[
            pl.BlockSpec((1, rows, rank), lambda h, m: (m, 0, 0)),
            pl.BlockSpec((rank, 4 * LANES), lambda h, m: (0, h + first)),
            pl.BlockSpec((nz, 1, rows, lanes), lambda h, m: (0, m, 0, 0)),
            pl.BlockSpec((kvr, 2 * LANES), lambda h, m: (0, h + first)),
            pl.BlockSpec((1, rows, LANES), lambda h, m: (m, 0, 0)),
            pl.BlockSpec((1, rows, LANES), lambda h, m: (m, 0, 0)),
            pl.BlockSpec((1, 8, rows), lambda h, m: (m, 0, 0)),
            pl.BlockSpec((1, rows, LANES), lambda h, m: (m, 0, h + first)),
            pl.BlockSpec((1, 1, 2, rows), lambda h, m: (m, h + first, 0, 0)),
        ],
        out_specs=[
            pl.BlockSpec((micros, rows, rank), lambda h, m: (0, 0, 0)),
            pl.BlockSpec((nz, micros, rows, lanes), lambda h, m: (0, 0, 0, 0)),
            pl.BlockSpec((rank, 4 * LANES), lambda h, m: (0, h)),
            pl.BlockSpec((kvr, 2 * LANES), lambda h, m: (0, h)),
        ],
        out_shape=[
            jax.ShapeDtypeStruct((micros, rows, rank), bf16),
            jax.ShapeDtypeStruct((nz, micros, rows, lanes), bf16),
            jax.ShapeDtypeStruct((rank, pairs * 4 * LANES), bf16),
            jax.ShapeDtypeStruct((kvr, pairs * 2 * LANES), bf16),
        ],
        scratch_shapes=[
            pltpu.VMEM((micros, rows, rank), f32),
            pltpu.VMEM((micros, seq, lanes), f32),
            pltpu.VMEM((rank, 4 * LANES), f32),
            pltpu.VMEM((kvr, 2 * LANES), f32),
        ],
        compiler_params=pltpu.CompilerParams(vmem_limit_bytes=VMEM_ATTEND),
        cost_estimate=cost(18 * pairs),
        name="attend_back",
    )(query_normed, wq, latent_all, lup, cosine, sine, spans, grads, logs)


COLS = 256
WIDE = 512
WIDE_OUT = 640


def rows_of(ref):
    return ref[...].reshape(-1, ref.shape[2])


def column_block(weights, own_rows, kind):
    return pl.BlockSpec((weights.shape[0], own_rows, COLS), lambda i: (0, kind, i))


def ffn_up_kernel(x_ref, gate_ref, up_ref, gate_out, up_out, hidden_out):
    gate = product(x_ref[...], rows_of(gate_ref))
    up = product(x_ref[...], rows_of(up_ref))
    gate_out[...] = gate.astype(bf16)
    up_out[...] = up.astype(bf16)
    hidden_out[...] = (gate * jax.nn.sigmoid(gate) * up).astype(bf16)


def ffn_up(x, weights, own_rows):
    rows, width = x.shape
    units = weights.shape[2]
    tile = pl.BlockSpec((rows, COLS), lambda i: (0, i))
    return pl.pallas_call(
        ffn_up_kernel,
        grid=(pl.cdiv(units, COLS),),
        in_specs=[
            pl.BlockSpec((rows, width), lambda i: (0, 0)),
            column_block(weights, own_rows, 0),
            column_block(weights, own_rows, 1),
        ],
        out_specs=[tile] * 3,
        out_shape=[jax.ShapeDtypeStruct((rows, units), bf16)] * 3,
        compiler_params=pltpu.CompilerParams(vmem_limit_bytes=VMEM_FFN),
        cost_estimate=cost(18),
        name="ffn_up",
    )(x, weights, weights)


def ffn_back_kernel(x_ref, down_ref, gate_ref, up_ref, g_gate_out, g_up_out):
    grad = product(x_ref[...], rows_of(down_ref))
    gate = gate_ref[...].astype(f32)
    sig = jax.nn.sigmoid(gate)
    g_gate_out[...] = (
        grad * up_ref[...].astype(f32) * sig * (1.0 + gate * (1.0 - sig))
    ).astype(bf16)
    g_up_out[...] = (grad * gate * sig).astype(bf16)


def ffn_back(x, weights, gate, up, own_rows):
    rows, width = x.shape
    units = weights.shape[2]
    tile = pl.BlockSpec((rows, COLS), lambda i: (0, i))
    return pl.pallas_call(
        ffn_back_kernel,
        grid=(pl.cdiv(units, COLS),),
        in_specs=[
            pl.BlockSpec((rows, width), lambda i: (0, 0)),
            column_block(weights, own_rows, 2),
            tile,
            tile,
        ],
        out_specs=[tile] * 2,
        out_shape=[jax.ShapeDtypeStruct((rows, units), bf16)] * 2,
        compiler_params=pltpu.CompilerParams(vmem_limit_bytes=VMEM_FFN),
        cost_estimate=cost(12),
        name="ffn_back",
    )(x, weights, gate, up)


def to_width_kernel(count, *refs):
    total = None
    for a_ref, w_ref in zip(refs[:count], refs[count : 2 * count]):
        term = contract_cols(a_ref[...], rows_of(w_ref))
        total = term if total is None else total + term
    refs[-1][...] = total.astype(bf16)


def to_width(half, values, weights, kinds, own_rows):
    count = len(values)
    rows, units = values[0].shape[0] // 2, values[0].shape[1]
    width = weights.shape[0] * own_rows
    per = WIDE_OUT // own_rows

    def owner_block(kind):
        return pl.BlockSpec((per, own_rows, units), lambda i: (i, kind, 0))

    return pl.pallas_call(
        functools.partial(to_width_kernel, count),
        grid=(width // WIDE_OUT,),
        in_specs=[pl.BlockSpec((rows, units), lambda i: (half, 0))] * count
        + [owner_block(kind) for kind in kinds],
        out_specs=pl.BlockSpec((rows, WIDE_OUT), lambda i: (0, i)),
        out_shape=jax.ShapeDtypeStruct((rows, width), bf16),
        compiler_params=pltpu.CompilerParams(vmem_limit_bytes=VMEM_FFN),
        cost_estimate=cost(6 * count),
        name="to_width",
    )(*values, *([weights] * count))


def weight_grad_kernel(a_ref, b_ref, out_ref):
    out_ref[...] = contract_rows(a_ref[...], b_ref[...]).astype(bf16)


def weight_grad(a, b):
    rows, width = a.shape
    units = b.shape[1]
    return pl.pallas_call(
        weight_grad_kernel,
        grid=(width // WIDE,),
        in_specs=[
            pl.BlockSpec((rows, WIDE), lambda i: (0, i)),
            pl.BlockSpec((rows, units), lambda i: (0, 0)),
        ],
        out_specs=pl.BlockSpec((WIDE, units), lambda i: (i, 0)),
        out_shape=jax.ShapeDtypeStruct((width, units), bf16),
        compiler_params=pltpu.CompilerParams(vmem_limit_bytes=VMEM_FFN),
        cost_estimate=cost(units * 0.006),
        name="weight_grad",
    )(a, b)


def on_device(
    tokens,
    segments,
    attn_gain,
    query_down,
    query_gain,
    query_up,
    latent_down,
    latent_gain,
    latent_up,
    out_weight,
    ffn_gain,
    gate_weight,
    up_weight,
    down_weight,
    cotangent,
):
    nx, nz = lax.axis_size("fsdp"), lax.axis_size("ctx")
    owners = nx * nz
    z, t = lax.axis_index("ctx"), lax.axis_index("tensor")
    micros, _, rows, width = tokens.shape
    seq = segments.shape[2]
    count = micros * rows
    share = count // TENSOR
    heads = query_up.shape[1] // (HD + ROPE)
    rank = query_down.shape[1]
    down_cols = rank + KVR + ROPE
    own_rows = query_down.shape[0]
    part_rows = own_rows // TENSOR
    half = ROPE // 2
    gain_sizes = [v.shape[0] for v in (attn_gain, query_gain, latent_gain, ffn_gain)]
    gain_total = sum(gain_sizes)
    gain_pad = GAIN_ROWS * down_cols - gain_total

    def share_of(values):
        return lax.dynamic_slice_in_dim(values, t * share, share, 0)

    down_own = lax.dynamic_slice_in_dim(
        jnp.concatenate([query_down, latent_down], axis=1), t * part_rows, part_rows, 0
    )
    gains = jnp.concatenate([attn_gain, query_gain, latent_gain, ffn_gain])
    gains = jnp.pad(gains, (0, gain_pad)).reshape(GAIN_ROWS, down_cols)
    order = Order()
    down_all, gain_all, up_query, up_latent, weight_out = front_gather(
        down_own, gains, query_up, latent_up, out_weight
    )
    down_whole = down_all.reshape(width, down_cols)
    up_query = up_query.reshape(rank, -1)
    up_latent = up_latent.reshape(KVR, -1)
    weight_out = weight_out.reshape(width, -1)
    order.mark(gain_all)

    cut = own_rows // 2
    pack_cols = out_weight.shape[1]
    query_rows = query_up.size // pack_cols
    own_query_up, own_latent_up = query_up, latent_up
    units = gate_weight.shape[1]
    f_gather = Gather(jnp.concatenate([gate_weight, up_weight, down_weight[:cut]], axis=0))
    f_rows = 2 * own_rows + cut
    f_gather.start_x(order)
    h_gather = PairGather(down_weight[cut:], order)
    gain_blocks = gain_all.reshape(owners, -1).astype(f32)
    gain_list, start = [], 0
    for size in gain_sizes:
        gain_list.append(gain_blocks[:, start : start + size].reshape(-1))
        start += size
    gain_attn, gain_query, gain_latent, gain_ffn = gain_list

    seg = segments[:, 0]
    first_end = jnp.sum((seg < 1).astype(jnp.int32), axis=1, keepdims=True)
    second_end = jnp.sum((seg < 2).astype(jnp.int32), axis=1, keepdims=True)
    seg_own = lax.dynamic_slice_in_dim(seg, z * rows, rows, 1)
    own_starts = jnp.where(seg_own < 1, 0, jnp.where(seg_own < 2, first_end, second_end))
    own_index = jnp.broadcast_to(z * rows + jnp.arange(rows, dtype=jnp.int32), own_starts.shape)
    spans = jnp.pad(jnp.stack([own_starts, own_index], axis=1), ((0, 0), (0, 6), (0, 0)))
    lane = jnp.arange(LANES, dtype=jnp.int32)
    frequency = rope_base ** (-(lane % half).astype(f32) * (2.0 / ROPE))
    angles = (own_index - own_starts).astype(f32)[:, :, None] * frequency
    cos_own = jnp.where(lane < ROPE, jnp.cos(angles), 0.0)
    sin_own = jnp.where(lane < ROPE, jnp.sin(angles), 0.0) * jnp.where(lane < half, -1.0, 1.0)
    cos_share = share_of(cos_own.reshape(count, LANES))[:, :half]
    sin_share = share_of(sin_own.reshape(count, LANES))[:, half:ROPE]

    def rotated(values, cosine, sine):
        first, second = values[..., :half], values[..., half:]
        return jnp.concatenate(
            [first * cosine - second * sine, first * sine + second * cosine], axis=-1
        )

    inputs_low = tokens.reshape(count, width)
    tokens_share = share_of(inputs_low).astype(f32)
    normed_share = rms_scale(tokens_share, gain_attn).astype(bf16)
    raw = product(normed_share, down_whole)
    query_latent, latent_raw = raw[:, :rank], raw[:, rank:]
    query_normed = rms_scale(query_latent, gain_query).astype(bf16)
    latent = rms_scale(latent_raw[:, :KVR], gain_latent).astype(bf16)
    key_rope = rotated(latent_raw[:, KVR:], cos_share, sin_share).astype(bf16)
    latent = jnp.concatenate(
        [latent, jnp.pad(key_rope, ((0, 0), (0, LANES - ROPE)))], axis=1
    )
    order.mark(latent)
    lanes = KVR + LANES
    shared = gather_ctx(latent)

    column = jnp.arange(heads * (HD + ROPE), dtype=jnp.int32)
    feature = column % (HD + ROPE)
    target = (column // (HD + ROPE)) * (2 * LANES) + jnp.where(
        feature < HD, feature, feature - HD + LANES
    )
    spread = (target[:, None] == jnp.arange(heads * 2 * LANES)[None, :]).astype(bf16)
    wq = product(order(up_query), spread).astype(bf16)
    order.mark(wq)
    shared = jnp.concatenate([query_normed] + [shared[d] for d in range(nz)], axis=1)
    order.mark(shared)
    f_gather.start_z(order)
    shared_slots = tensor_gather(shared)
    order.mark((cos_own, spans))
    f_buffer = Buffer((3 * own_rows, units), order)
    order.mark(tuple(shared_slots[1:]))
    shared = jnp.stack(from_slots(order(tuple(shared_slots))))
    query_normed = shared[..., :rank].reshape(micros, rows, rank)
    latent_all = jnp.stack(
        [shared[..., rank + d * lanes : rank + (d + 1) * lanes] for d in range(nz)]
    ).reshape(nz, micros, rows, lanes)
    order.mark((query_normed, latent_all))
    attended, logs = attend(
        order(query_normed), wq, latent_all, up_latent, cos_own, sin_own, spans
    )
    order.mark(attended)
    f_gather.arrive(order)
    f_gather.pass_on(order)

    def slot_halves(values):
        slots = to_slots(values.reshape((TENSOR, share) + values.shape[1:]))
        return jnp.concatenate(slots[:2], axis=0), jnp.concatenate(slots[2:], axis=0)

    def halves(values):
        return values.reshape(2, share, width)

    attended_kept, attended_sent = slot_halves(attended.reshape(count, -1))
    sent = contract_cols(attended_sent, weight_out).astype(bf16)
    kept = contract_cols(attended_kept, weight_out).astype(bf16)
    order.mark((kept, sent))
    attn_share = tensor_scatter(halves(kept), halves(sent))
    f_gather.place_old(f_buffer, order)
    h_gather.line(order)
    h_gather.place(f_buffer, order, f_rows)
    order.mark(attn_share)
    middle = tokens_share + branch_scale * order(attn_share)
    ffn_share_in = rms_scale(middle, gain_ffn).astype(bf16)
    order.mark(ffn_share_in)
    ffn_slots = tensor_gather(ffn_share_in)
    f_gather.arrive(order)
    f_gather.pass_on(order)
    f_gather.place_old(f_buffer, order)
    upstream_slots = jnp.concatenate(slot_halves(order(cotangent).reshape(count, width)), axis=0)
    upstream_share = upstream_slots[:share].astype(f32)
    grad_ffn = (branch_scale * upstream_slots.astype(f32)).astype(bf16)
    ffn_in = jnp.concatenate(ffn_slots, axis=0)
    order.mark((grad_ffn, ffn_in))
    while f_gather.step + 1 < nz:
        f_gather.arrive(order)
        f_gather.pass_on(order)
        f_gather.place_old(f_buffer, order)
    f_gather.arrive(order)
    f_gather.start_x(order)
    f_gather.place_old(f_buffer, order)
    h_gather.start_z(order)
    while h_gather.step + 1 < nz:
        h_gather.arrive(order)
        h_gather.start_z(order)
        h_gather.place_before(f_buffer, order, f_rows)
    f_gather.place(f_buffer, order)
    gate_val, up_val, hidden = ffn_up(ffn_in, f_buffer.result(), own_rows)
    order.mark(hidden)

    def blocks_of(gradient):
        return gradient.reshape((owners, -1) + gradient.shape[1:])

    grad_down_weight = blocks_of(weight_grad(grad_ffn, hidden))
    order.mark(grad_down_weight)
    s_down = PairScatter(grad_down_weight, order)
    h_gather.arrive(order)
    h_gather.place(f_buffer, order, f_rows)
    weights = f_buffer.result()
    grad_gate, grad_up = ffn_back(order(grad_ffn), weights, gate_val, up_val, own_rows)
    s_gate = Scatter(blocks_of(weight_grad(ffn_in, grad_gate)), 2)
    order.mark(s_gate.blocks)
    s_gate.start_x(order)
    grad_gate, grad_up = order((grad_gate, grad_up))
    sent = to_width(1, (grad_gate, grad_up), weights, (0, 1), own_rows)
    order.mark(sent)
    kept = to_width(0, order((grad_gate, grad_up)), weights, (0, 1), own_rows)
    order.mark(kept)
    grad_ffn_in = tensor_scatter(halves(kept), halves(sent))
    s_up = Scatter(blocks_of(weight_grad(ffn_in, order(grad_up))), 2)
    order.mark(s_up.blocks)
    s_down.forward(order)
    s_gate.arrive(order)
    s_gate.start_x(order)
    grad_middle, grad_gain_ffn = norm_back(middle, gain_ffn, order(grad_ffn_in))
    grad_middle = grad_middle + upstream_share
    grad_attn_share = (branch_scale * grad_middle).astype(bf16)
    order.mark(grad_attn_share)
    grad_attn_slots = tensor_gather(grad_attn_share)

    hidden = order(hidden)
    mixed_sent = to_width(1, (hidden,), weights, (2,), own_rows)
    mixed_kept = to_width(0, (hidden,), weights, (2,), own_rows)
    order.mark((mixed_kept, mixed_sent))
    s_gate.forward(order)
    grad_attn = jnp.concatenate(order(tuple(grad_attn_slots)), axis=0)
    order.mark(grad_attn)
    ffn_share = tensor_scatter(halves(order(mixed_kept)), halves(order(mixed_sent)))

    grad_attended = product(grad_attn, weight_out).astype(bf16)
    grad_attended = jnp.concatenate(from_slots(jnp.split(grad_attended, TENSOR)), axis=0)
    attended_slots = jnp.concatenate([attended_kept, attended_sent], axis=0)
    s_out = Scatter(blocks_of(weight_grad(order(grad_attn), attended_slots)), 1)
    order.mark((s_out.blocks, grad_attended))
    s_down.forward(order)
    s_gate.arrive(order)
    s_up.start_x(order)
    operands = (
        query_normed,
        wq,
        latent_all,
        up_latent,
        cos_own,
        sin_own,
        spans,
        order(grad_attended).reshape(micros, rows, -1),
        logs,
    )
    pairs = heads // 2
    early = (pairs + 1) // 2
    one = attend_back(0, early, *operands)
    order.mark((one[0], ffn_share))
    s_gate.forward(order)
    s_down.forward(order)
    s_up.arrive(order)
    s_up.start_x(order)
    mixed_share = (middle + branch_scale * order(ffn_share)).astype(bf16)
    order.mark(mixed_share)
    mixed_slots = tensor_gather(mixed_share)
    two = attend_back(early, pairs - early, order(operands[0]), *operands[1:])
    order.mark((two[0], s_down.total) + tuple(mixed_slots))

    def slot_sums(values, axis):
        slots = [
            add_low(a, b)
            for a, b in zip(to_slots(values[0], axis), to_slots(values[1], axis))
        ]
        return jnp.stack(slots[:2]), jnp.stack(slots[2:])

    query_parts = [v[0].reshape(TENSOR, share, rank) for v in (one, two)]
    latent_parts = [v[1].reshape(nz, TENSOR, share, KVR + LANES) for v in (one, two)]
    latent_sums = slot_sums(latent_parts, 1)
    query_sums = slot_sums(query_parts, 0)
    order.mark((latent_sums[1], query_sums[1]))
    g_latent_slots = tensor_scatter(*latent_sums)
    s_gate.forward(order)
    s_up.arrive(order)
    s_out.start_x(order)
    mixed = jnp.concatenate(from_slots(order(tuple(mixed_slots))), axis=0)
    order.mark(g_latent_slots)
    g_latent_share = scatter_ctx(g_latent_slots)
    s_up.forward(order)
    g_query_share = tensor_scatter(*order(query_sums))
    g_wq = order(jnp.concatenate([one[2], two[2]], axis=1))
    grad_query_up = contract_cols(g_wq, spread).astype(bf16)
    order.mark(grad_query_up)
    s_gate.forward(order)
    s_up.forward(order)
    s_pack = Scatter(
        jnp.concatenate(
            [
                order(grad_query_up).reshape(owners, -1, pack_cols),
                jnp.concatenate([one[3], two[3]], axis=1).reshape(owners, -1, pack_cols),
            ],
            axis=1,
        ),
        1,
    )
    order.mark(s_pack.blocks)
    s_pack.start_x(order)
    s_out.forward(order)
    s_up.forward(order)
    order.mark(g_latent_share)
    grad_query_latent, grad_gain_query = norm_back(query_latent, gain_query, g_query_share)
    grad_latent_first, grad_gain_latent = norm_back(
        latent_raw[:, :KVR], gain_latent, g_latent_share[:, :KVR]
    )
    grad_rope = rotated(g_latent_share[:, KVR : KVR + ROPE], cos_share, -sin_share)
    grad_raw = jnp.concatenate(
        [grad_query_latent, grad_latent_first, grad_rope], axis=1
    ).astype(bf16)
    order.mark(grad_raw)
    grad_raw_slots = tensor_gather(grad_raw)
    s_out.forward(order)
    s_pack.forward(order)
    grad_normed = contract_cols(order(grad_raw), down_whole)
    grad_inputs, grad_gain_attn = norm_back(tokens_share, gain_attn, grad_normed)
    grad_share = (grad_inputs + grad_middle).astype(bf16)
    order.mark(grad_share)
    normed = rms_scale(order(inputs_low).astype(f32), gain_attn).astype(bf16)
    grad_raw_all = jnp.concatenate(from_slots(order(tuple(grad_raw_slots))), axis=0)
    grad_down = weight_grad(normed, grad_raw_all).reshape(owners, TENSOR, part_rows, down_cols)
    grad_down = lax.dynamic_index_in_dim(grad_down, t, 1, keepdims=False)
    gain_grads = jnp.concatenate(
        [
            g.reshape(owners, -1)
            for g in (grad_gain_attn, grad_gain_query, grad_gain_latent, grad_gain_ffn)
        ],
        axis=1,
    ).astype(bf16)
    gain_grads = jnp.pad(gain_grads, ((0, 0), (0, gain_pad))).reshape(
        owners, GAIN_ROWS, down_cols
    )
    s_bundle = Scatter(jnp.concatenate([grad_down, gain_grads], axis=1), 2)
    order.mark(s_bundle.blocks)
    s_bundle.start_x(order)
    s_bundle.start_x(order)
    s_out.forward(order)
    s_pack.forward(order)
    s_up.forward(order)
    grad_slots = tensor_gather(order(grad_share))
    s_bundle.forward(order)
    s_out.forward(order)
    s_pack.forward(order)
    s_bundle.forward(order)
    s_pack.forward(order)
    while s_bundle.step < nz:
        s_bundle.forward(order)
    bundle_share = s_bundle.total.astype(bf16)
    order.mark(bundle_share)
    bundle_list = from_slots(tensor_gather(bundle_share))
    grad_tokens = jnp.concatenate(from_slots(order(tuple(grad_slots))), axis=0).astype(f32)
    out_down = jnp.concatenate([b[:part_rows] for b in bundle_list], axis=0).astype(f32)
    gain_sum = sum(b[part_rows:].astype(f32) for b in bundle_list).reshape(-1)
    out_gains, start = [], 0
    for size in gain_sizes:
        out_gains.append(gain_sum[start : start + size])
        start += size
    out_query_up = s_pack.total[:query_rows].reshape(query_up.shape)
    out_latent_up = s_pack.total[query_rows:].reshape(latent_up.shape)

    return (
        mixed.reshape(tokens.shape),
        grad_tokens.reshape(tokens.shape),
        out_gains[0],
        out_down[:, :rank],
        out_gains[1],
        out_query_up,
        out_down[:, rank:],
        out_gains[2],
        out_latent_up,
        s_out.total,
        out_gains[3],
        s_gate.total,
        s_up.total,
        s_down.result(),
    )


def solution(mesh):
    return jax.shard_map(
        on_device,
        mesh=mesh,
        in_specs=(
            P(None, "fsdp", "ctx", None),
            P(None, "fsdp", None),
            P(("fsdp", "ctx")),
            P(("fsdp", "ctx"), None),
            P(("fsdp", "ctx")),
            P(("fsdp", "ctx"), "tensor"),
            P(("fsdp", "ctx"), None),
            P(("fsdp", "ctx")),
            P(("fsdp", "ctx"), "tensor"),
            P(("fsdp", "ctx"), "tensor"),
            P(("fsdp", "ctx")),
            P(("fsdp", "ctx"), "tensor"),
            P(("fsdp", "ctx"), "tensor"),
            P(("fsdp", "ctx"), "tensor"),
            P(None, "fsdp", "ctx", None),
        ),
        out_specs=(
            P(None, "fsdp", "ctx", None),
            P(None, "fsdp", "ctx", None),
            P(("fsdp", "ctx")),
            P(("fsdp", "ctx"), None),
            P(("fsdp", "ctx")),
            P(("fsdp", "ctx"), "tensor"),
            P(("fsdp", "ctx"), None),
            P(("fsdp", "ctx")),
            P(("fsdp", "ctx"), "tensor"),
            P(("fsdp", "ctx"), "tensor"),
            P(("fsdp", "ctx")),
            P(("fsdp", "ctx"), "tensor"),
            P(("fsdp", "ctx"), "tensor"),
            P(("fsdp", "ctx"), "tensor"),
        ),
        check_vma=False,
    )
```

```python
import functools
import math

import jax
import jax.numpy as jnp
from jax import lax
from jax.experimental import pallas as pl
from jax.experimental.pallas import tpu as pltpu
from jax.sharding import PartitionSpec as P

KVR = 256
ROPE = 32
HD = 64
VD = 64
LANES = 128
GAIN_ROWS = 16
TENSOR = 4

norm_eps = 1e-05
branch_scale = 1.4 / math.sqrt(62.0)
rope_base = 10000.0
masked_fill = -1e30
att_scale = (HD + ROPE) ** (-0.5)
att_scale_log2 = att_scale / math.log(2.0)

bf16 = jnp.bfloat16
f32 = jnp.float32


def product(left_side, right_side):
    return jnp.dot(left_side, right_side, preferred_element_type=f32)


def contract_rows(left_side, right_side):
    return lax.dot_general(
        left_side, right_side, (((0,), (0,)), ((), ())), preferred_element_type=f32
    )


def contract_cols(left_side, right_side):
    return lax.dot_general(
        left_side, right_side, (((1,), (1,)), ((), ())), preferred_element_type=f32
    )


def rms_scale(values, gain_vec):
    return (
        values * lax.rsqrt(jnp.mean(values * values, axis=-1, keepdims=True) + norm_eps) * gain_vec
    )


def norm_back(values, gain_vec, gradient):
    return jax.vjp(rms_scale, values, gain_vec)[1](gradient)


def add_low(left_side, right_side):
    return (left_side.astype(f32) + right_side.astype(f32)).astype(bf16)


def after(values, *others):
    return lax.optimization_barrier((values,) + others)[0]


def turn(values, axis):
    size = lax.axis_size(axis)
    return lax.ppermute(values, axis, [(i, (i + 1) % size) for i in range(size)])


class Order:
    def __init__(self):
        self.events = []

    def __call__(self, values):
        return after(values, *self.events[-10:]) if self.events else values

    def mark(self, event):
        self.events.append(event)


class Buffer:
    def __init__(self, shape, order):
        sizes = (lax.axis_size("fsdp"), lax.axis_size("ctx"))
        self.whole = jnp.broadcast_to(order(jnp.zeros((), bf16)), sizes + shape)

    def place(self, piece, x, z, row):
        self.whole = lax.dynamic_update_slice(self.whole, piece, (x, z, row, 0))

    def filled(self, order):
        order.mark(self.whole[0, 0, 0, :LANES])

    def result(self):
        return self.whole.reshape((-1,) + self.whole.shape[2:])


class Gather:
    def __init__(self, shard):
        self.nx, self.nz = lax.axis_size("fsdp"), lax.axis_size("ctx")
        self.x, self.z = lax.axis_index("fsdp"), lax.axis_index("ctx")
        self.piece = shard
        self.step = 0
        self.waiting = []

    def start_x(self, order):
        far = order(self.piece)
        self.waiting.append((far, 0, self.step))
        self.sent = True
        for e in range(1, self.nx):
            far = turn(far, "fsdp")
            self.waiting.append((far, e, self.step))

    def start_z(self, order):
        if self.step + 1 < self.nz:
            self.piece = turn(order(self.piece), "ctx")
            self.step += 1

    def pass_on(self, order):
        held, step = self.piece, self.step
        self.start_z(order)
        piece, self.piece, self.step = self.piece, held, step
        self.start_x(order)
        if step + 1 < self.nz:
            self.piece, self.step = piece, step + 1

    def arrive(self, order):
        order.mark((self.piece, self.waiting[-1][0]) if self.waiting else self.piece)

    def place_old(self, buffer, order, row=0):
        last = self.waiting[-1][2]
        late = [w for w in self.waiting if w[2] == last]
        self.waiting = [w for w in self.waiting if w[2] != last]
        self.place(buffer, order, row)
        self.waiting = late

    def place(self, buffer, order, row=0):
        for far, e, step in self.waiting:
            buffer.place(
                order(far)[None, None], (self.x - e) % self.nx, (self.z - step) % self.nz, row
            )
        self.waiting = []


class PairGather:
    def __init__(self, far, order):
        self.nx, self.nz = lax.axis_size("fsdp"), lax.axis_size("ctx")
        self.x, self.z = lax.axis_index("fsdp"), lax.axis_index("ctx")
        self.far = far
        self.step = 0
        self.line(order)

    def line(self, order):
        piece = jnp.broadcast_to(order(jnp.zeros((), bf16)), (self.nx, 1) + self.far[0].shape)
        for e, far in enumerate(self.far):
            piece = lax.dynamic_update_slice(
                piece, order(far)[None, None], ((self.x - e) % self.nx, 0, 0, 0)
            )
        self.piece = piece

    def start_z(self, order):
        self.before = self.piece
        self.piece = turn(order(self.piece), "ctx")
        self.step += 1

    def arrive(self, order):
        order.mark(self.piece)

    def place_before(self, buffer, order, row):
        buffer.place(order(self.before), 0, (self.z - self.step + 1) % self.nz, row)

    def place(self, buffer, order, row):
        buffer.place(order(self.piece), 0, (self.z - self.step) % self.nz, row)


class Scatter:
    def __init__(self, blocks, groups):
        self.nx, self.nz = lax.axis_size("fsdp"), lax.axis_size("ctx")
        self.x, self.z = lax.axis_index("fsdp"), lax.axis_index("ctx")
        self.blocks = blocks
        self.size = self.nz // groups
        self.far = []
        self.total = None
        self.step = 0

    def own(self, e, d):
        owner = ((self.x - 1 - e) % self.nx) * self.nz + (self.z - 1 - d) % self.nz
        return lax.dynamic_index_in_dim(self.blocks, owner, 0, keepdims=False)

    def start_x(self, order):
        first = len(self.far) * self.size
        blocks, self.blocks = self.blocks, order(self.blocks)
        part = None
        for e in range(self.nx - 1):
            own = jnp.stack([self.own(e, first + k) for k in range(self.size)])
            part = own if part is None else add_low(part, own)
            order.mark(part)
            part = turn(part, "fsdp")
        self.blocks = blocks
        self.far.append(part)

    def arrive(self, order):
        order.mark(self.far[-1])

    def forward(self, order):
        d = self.step
        total = self.own(self.nx - 1, d).astype(f32)
        if self.nx > 1:
            total = total + order(self.far[d // self.size])[d % self.size].astype(f32)
        if d:
            total = total + order(self.total).astype(f32)
        self.step += 1
        if self.step == self.nz:
            self.total = total
        else:
            total = total.astype(bf16)
            order.mark(total)
            self.total = turn(total, "ctx")


class PairScatter:
    def __init__(self, blocks, order):
        self.nx, self.nz = lax.axis_size("fsdp"), lax.axis_size("ctx")
        self.x, self.z = lax.axis_index("fsdp"), lax.axis_index("ctx")
        self.blocks = order(blocks).reshape((self.nx, self.nz) + blocks.shape[1:])
        self.step = 0
        first = self.own(0)
        order.mark(first)
        self.total = turn(first, "ctx")

    def own(self, d):
        return lax.dynamic_index_in_dim(
            self.blocks, (self.z - 1 - d) % self.nz, 1, keepdims=False
        )

    def forward(self, order):
        self.step += 1
        total = add_low(order(self.total), self.own(self.step))
        order.mark(total)
        if self.step + 1 < self.nz:
            self.total = turn(total, "ctx")
            return
        part = None
        for e in range(self.nx):
            own = lax.dynamic_index_in_dim(total, (self.x - 1 - e) % self.nx, 0, keepdims=False)
            part = own if part is None else add_low(turn(part, "fsdp"), own)
        self.total = part

    def result(self):
        return self.total.astype(f32)


def shift(values, d):
    size = lax.axis_size("ctx")
    return lax.ppermute(values, "ctx", [(i, (i + d) % size) for i in range(size)])


def gather_ctx(values):
    return [values] + [shift(values, d) for d in range(1, lax.axis_size("ctx"))]


def by_ctx(pieces):
    nz, z = lax.axis_size("ctx"), lax.axis_index("ctx")
    values = pieces[0]
    whole = jnp.zeros((nz,) + values.shape, values.dtype)
    for d, piece in enumerate(pieces):
        whole = lax.dynamic_update_slice_in_dim(whole, piece[None], (z - d) % nz, 0)
    return whole


def scatter_parts(blocks):
    nz, z = lax.axis_size("ctx"), lax.axis_index("ctx")
    parts = [lax.dynamic_index_in_dim(blocks, (z + d) % nz, 0, keepdims=False) for d in range(nz)]
    return parts[:1] + [shift(parts[d], d) for d in range(1, nz)]


SLOTS = (0, 2, 1, 3)


def swap(values, bit):
    return lax.ppermute(values, "tensor", [(i, i ^ bit) for i in range(TENSOR)])


def tensor_gather(values):
    near = swap(values, 1)
    far = swap(values, 2)
    return [values, far, near, swap(far, 1)]


def tensor_gather_now(values, order):
    order.mark(values)
    slots = tensor_gather(values)
    order.mark(tuple(slots[1:]))
    return slots


def tensor_scatter(kept, sent):
    near = swap(sent, 1)
    far = swap(add_low(kept[1], near[1]), 2)
    return kept[0].astype(f32) + near[0].astype(f32) + far.astype(f32)


def to_slots(blocks, axis=0):
    t = lax.axis_index("tensor")
    return [lax.dynamic_index_in_dim(blocks, t ^ j, axis, keepdims=False) for j in SLOTS]


def from_slots(slots):
    t = lax.axis_index("tensor")
    low, high = (t & 1) == 1, (t & 2) == 2
    own, far, near, both = slots
    a = [
        jnp.where(low, near, own),
        jnp.where(low, own, near),
        jnp.where(low, both, far),
        jnp.where(low, far, both),
    ]
    return [
        jnp.where(high, a[2], a[0]),
        jnp.where(high, a[3], a[1]),
        jnp.where(high, a[0], a[2]),
        jnp.where(high, a[1], a[3]),
    ]


MESH = pl.DeviceIdType.MESH
FRONT = 5


def front_kernel(nx, nz, *refs):
    shards, outs = refs[:FRONT], refs[FRONT : 2 * FRONT]
    own_sem, z_send, z_recv, x_send, x_recv, t_send, t_recv = refs[2 * FRONT :]
    x, z, t = lax.axis_index("fsdp"), lax.axis_index("ctx"), lax.axis_index("tensor")
    right_x, left_x = lax.rem(x + 1, nx), lax.rem(x + nx - 1, nx)
    right_z, left_z = lax.rem(z + 1, nz), lax.rem(z + nz - 1, nz)
    near_t = t + 1 - 2 * lax.rem(t, 2)
    far_t = lax.rem(t + 2, TENSOR)

    barrier = pltpu.get_barrier_semaphore()
    partners = (
        {"fsdp": right_x},
        {"fsdp": left_x},
        {"ctx": right_z},
        {"ctx": left_z},
        {"tensor": near_t},
        {"tensor": far_t},
    )
    for partner in partners:
        pl.semaphore_signal(barrier, 1, device_id=partner, device_id_type=MESH)
    pl.semaphore_wait(barrier, len(partners))

    def block(a, xx, zz):
        return outs[a].at[xx, zz, t] if a == 0 else outs[a].at[xx, zz]

    def own(a):
        return pltpu.make_async_copy(shards[a], block(a, x, z), own_sem.at[a])

    def along_z(a, d):
        zz = lax.rem(z + nz - d, nz)
        return pltpu.make_async_remote_copy(
            src_ref=shards[a] if d == 0 else block(a, x, zz),
            dst_ref=block(a, x, zz),
            send_sem=z_send.at[a, d],
            recv_sem=z_recv.at[a, d],
            device_id={"ctx": right_z},
            device_id_type=MESH,
        )

    def along_x(a, d, e):
        xx, zz = lax.rem(x + nx - e, nx), lax.rem(z + nz - d, nz)
        return pltpu.make_async_remote_copy(
            src_ref=shards[a] if d + e == 0 else block(a, xx, zz),
            dst_ref=block(a, xx, zz),
            send_sem=x_send.at[a, d, e],
            recv_sem=x_recv.at[a, d, e],
            device_id={"fsdp": right_x},
            device_id_type=MESH,
        )

    def along_t(k, owner, partner):
        part = outs[0].at[:, :, owner]
        return pltpu.make_async_remote_copy(
            src_ref=part,
            dst_ref=part,
            send_sem=t_send.at[k],
            recv_sem=t_recv.at[k],
            device_id={"tensor": partner},
            device_id_type=MESH,
        )

    early, late = (0, 1), (2, 3, 4)
    for a in range(FRONT):
        own(a).start()
    for a in early:
        along_z(a, 0).start()
        along_x(a, 0, 0).start()
    for d in range(1, nz):
        for a in early:
            along_z(a, d - 1).wait_recv()
            if d + 1 < nz:
                along_z(a, d).start()
            along_x(a, d, 0).start()
    for a in late:
        along_z(a, 0).start()
        along_x(a, 0, 0).start()
    for d in range(nz):
        for e in range(1, nx):
            for a in early:
                along_x(a, d, e - 1).wait_recv()
                if e + 1 < nx:
                    along_x(a, d, e).start()
    own(0).wait()
    along_t(0, t, near_t).start()
    along_t(1, t, far_t).start()
    for d in range(1, nz):
        for a in late:
            along_z(a, d - 1).wait_recv()
            if d + 1 < nz:
                along_z(a, d).start()
            along_x(a, d, 0).start()
    along_t(1, t, far_t).wait_recv()
    along_t(2, far_t, near_t).start()
    for d in range(nz):
        for e in range(1, nx):
            for a in late:
                along_x(a, d, e - 1).wait_recv()
                if e + 1 < nx:
                    along_x(a, d, e).start()
    along_t(0, t, near_t).wait_recv()
    along_t(2, far_t, near_t).wait_recv()
    for a in range(1, FRONT):
        own(a).wait()
    for a in range(FRONT):
        for d in range(nz):
            if d + 1 < nz:
                along_z(a, d).wait_send()
            for e in range(nx - 1):
                along_x(a, d, e).wait_send()
    along_t(0, t, near_t).wait_send()
    along_t(1, t, far_t).wait_send()
    along_t(2, far_t, near_t).wait_send()


def front_gather(down, gains, query_up, latent_up, out_weight):
    nx, nz = lax.axis_size("fsdp"), lax.axis_size("ctx")
    shards = (down, gains, query_up, latent_up, out_weight)
    shapes = [
        jax.ShapeDtypeStruct((nx, nz) + ((TENSOR,) if a == 0 else ()) + v.shape, v.dtype)
        for a, v in enumerate(shards)
    ]
    return pl.pallas_call(
        functools.partial(front_kernel, nx, nz),
        in_specs=[pl.BlockSpec(memory_space=pl.ANY)] * FRONT,
        out_specs=[pl.BlockSpec(memory_space=pl.ANY)] * FRONT,
        out_shape=shapes,
        scratch_shapes=[
            pltpu.SemaphoreType.DMA((FRONT,)),
            pltpu.SemaphoreType.DMA((FRONT, nz)),
            pltpu.SemaphoreType.DMA((FRONT, nz)),
            pltpu.SemaphoreType.DMA((FRONT, nz, nx)),
            pltpu.SemaphoreType.DMA((FRONT, nz, nx)),
            pltpu.SemaphoreType.DMA((3,)),
            pltpu.SemaphoreType.DMA((3,)),
        ],
        compiler_params=pltpu.CompilerParams(collective_id=0, has_side_effects=True),
        cost_estimate=cost(88),
        name="front_gather",
    )(*shards)


def rotate_lanes(values, cosine, sine):
    lane = lax.broadcasted_iota(jnp.int32, values.shape, 1)
    half = ROPE // 2
    other = jnp.where(
        lane < half, pltpu.roll(values, LANES - half, 1), pltpu.roll(values, half, 1)
    )
    return values * cosine + other * sine


def head_inputs(normed_ref, wq, latent, rope, lup, cos_ref, sin_ref):
    raw = product(normed_ref[0], wq)
    rotated = rotate_lanes(raw[:, LANES:], cos_ref[0], sin_ref[0])
    query = jnp.concatenate([raw[:, :LANES], rotated], axis=1).astype(bf16)
    pair = product(latent, lup).astype(bf16)
    key = jnp.concatenate([pair, rope], axis=1)
    return query, pair, key


def latent_rows(latent_ref):
    nz, _, rows, lanes = latent_ref.shape
    held = latent_ref[...].reshape(nz * rows, lanes)
    return held[:, :KVR], held[:, KVR:]


def allowed_mask(span_ref, shape):
    key_index = lax.broadcasted_iota(jnp.int32, shape, 0)
    return (key_index >= span_ref[0, 0:1, :]) & (key_index <= span_ref[0, 1:2, :])


def attend_kernel(
    normed_ref, wq_ref, latent_ref, lup_ref, cos_ref, sin_ref, span_ref, out_ref, log_ref
):
    latent, rope = latent_rows(latent_ref)
    found = []
    for j in range(2):
        query, pair, key = head_inputs(
            normed_ref,
            wq_ref[:, 2 * LANES * j : 2 * LANES * (j + 1)],
            latent,
            rope,
            lup_ref[:, LANES * j : LANES * (j + 1)],
            cos_ref,
            sin_ref,
        )
        scores = contract_cols(key, query)
        scores = jnp.where(allowed_mask(span_ref, scores.shape), scores, masked_fill)
        highest = jnp.max(scores, axis=0, keepdims=True)
        exps = jnp.exp2((scores - highest) * att_scale_log2)
        total = jnp.sum(exps, axis=0, keepdims=True)
        probs = (exps * (1.0 / total)).astype(bf16)
        found.append(contract_rows(pair, probs)[HD:, :])
        log_ref[0, 0, j : j + 1, :] = highest * att_scale_log2 + jnp.log2(total)
    out_ref[0] = jnp.concatenate(found, axis=0).T.astype(bf16)


def attend_back_kernel(
    normed_ref,
    wq_ref,
    latent_ref,
    lup_ref,
    cos_ref,
    sin_ref,
    span_ref,
    grad_ref,
    log_ref,
    g_normed_ref,
    g_latent_ref,
    g_wq_ref,
    g_lup_ref,
    sum_normed,
    sum_latent,
    sum_wq,
    sum_lup,
):
    step, micro = pl.program_id(0), pl.program_id(1)

    @pl.when(step == 0)
    def _():
        sum_normed[micro] = jnp.zeros(sum_normed.shape[1:], f32)
        sum_latent[micro] = jnp.zeros(sum_latent.shape[1:], f32)

    @pl.when(micro == 0)
    def _():
        sum_wq[...] = jnp.zeros_like(sum_wq)
        sum_lup[...] = jnp.zeros_like(sum_lup)

    latent, rope = latent_rows(latent_ref)
    grad_pair = grad_ref[0].astype(f32)
    lane = lax.broadcasted_iota(jnp.int32, grad_pair.shape, 1)
    for j in range(2):
        wq = wq_ref[:, 2 * LANES * j : 2 * LANES * (j + 1)]
        lup = lup_ref[:, LANES * j : LANES * (j + 1)]
        query, pair, key = head_inputs(normed_ref, wq, latent, rope, lup, cos_ref, sin_ref)
        grad_head = pltpu.roll(grad_pair, HD, 1) if j == 0 else grad_pair
        grad_head = jnp.where(lane >= HD, grad_head, 0.0).astype(bf16)
        scores = contract_cols(key, query)
        probs = jnp.where(
            allowed_mask(span_ref, scores.shape),
            jnp.exp2(scores * att_scale_log2 - log_ref[0, 0, j : j + 1, :]),
            0.0,
        )
        grad_probs = contract_cols(pair, grad_head)
        delta = jnp.sum(probs * grad_probs, axis=0, keepdims=True)
        grad_scores = (probs * (grad_probs - delta) * att_scale).astype(bf16)
        grad_key = product(grad_scores, query)
        sum_latent[micro, :, KVR:] += grad_key[:, LANES:]
        grad_key_value = (grad_key[:, :LANES] + product(probs.astype(bf16), grad_head)).astype(bf16)
        grad_query = contract_rows(grad_scores, key)
        rotated = rotate_lanes(grad_query[:, LANES:], cos_ref[0], -sin_ref[0])
        plain = jnp.where(lane < HD, grad_query[:, :LANES], 0.0)
        grad_raw = jnp.concatenate([plain, rotated], axis=1).astype(bf16)
        sum_lup[:, LANES * j : LANES * (j + 1)] += contract_rows(latent, grad_key_value)
        sum_latent[micro, :, :KVR] += contract_cols(grad_key_value, lup)
        sum_wq[:, 2 * LANES * j : 2 * LANES * (j + 1)] += contract_rows(normed_ref[0], grad_raw)
        sum_normed[micro] += contract_cols(grad_raw, wq)

    @pl.when(micro == pl.num_programs(1) - 1)
    def _():
        g_wq_ref[...] = sum_wq[...].astype(bf16)
        g_lup_ref[...] = sum_lup[...].astype(bf16)

    @pl.when(step == pl.num_programs(0) - 1)
    def _():
        g_normed_ref[micro] = sum_normed[micro].astype(bf16)
        nz, _, rows, lanes = g_latent_ref.shape
        g_latent_ref[:, micro] = sum_latent[micro].astype(bf16).reshape(nz, rows, lanes)


def cost(microseconds):
    return pl.CostEstimate(
        flops=int(microseconds * 1.15e9), bytes_accessed=1, transcendentals=0
    )


VMEM_ATTEND = 56 * 1024 * 1024
VMEM_FFN = 40 * 1024 * 1024


def attend(query_normed, wq, latent_all, lup, cosine, sine, spans):
    micros, rows, rank = query_normed.shape
    nz, _, _, lanes = latent_all.shape
    seq, kvr = nz * rows, KVR
    pairs = lup.shape[1] // (2 * LANES)
    return pl.pallas_call(
        attend_kernel,
        grid=(micros, pairs),
        in_specs=[
            pl.BlockSpec((1, rows, rank), lambda m, h: (m, 0, 0)),
            pl.BlockSpec((rank, 4 * LANES), lambda m, h: (0, h)),
            pl.BlockSpec((nz, 1, rows, lanes), lambda m, h: (0, m, 0, 0)),
            pl.BlockSpec((kvr, 2 * LANES), lambda m, h: (0, h)),
            pl.BlockSpec((1, rows, LANES), lambda m, h: (m, 0, 0)),
            pl.BlockSpec((1, rows, LANES), lambda m, h: (m, 0, 0)),
            pl.BlockSpec((1, 8, rows), lambda m, h: (m, 0, 0)),
        ],
        out_specs=[
            pl.BlockSpec((1, rows, LANES), lambda m, h: (m, 0, h)),
            pl.BlockSpec((1, 1, 2, rows), lambda m, h: (m, h, 0, 0)),
        ],
        out_shape=[
            jax.ShapeDtypeStruct((micros, rows, pairs * LANES), bf16),
            jax.ShapeDtypeStruct((micros, pairs, 2, rows), f32),
        ],
        compiler_params=pltpu.CompilerParams(vmem_limit_bytes=VMEM_ATTEND),
        cost_estimate=cost(42),
        name="attend",
    )(query_normed, wq, latent_all, lup, cosine, sine, spans)


def attend_back(first, pairs, query_normed, wq, latent_all, lup, cosine, sine, spans, grads, logs):
    micros, rows, rank = query_normed.shape
    nz, _, _, lanes = latent_all.shape
    seq, kvr = nz * rows, KVR
    return pl.pallas_call(
        attend_back_kernel,
        grid=(pairs, micros),
        in_specs=[
            pl.BlockSpec((1, rows, rank), lambda h, m: (m, 0, 0)),
            pl.BlockSpec((rank, 4 * LANES), lambda h, m: (0, h + first)),
            pl.BlockSpec((nz, 1, rows, lanes), lambda h, m: (0, m, 0, 0)),
            pl.BlockSpec((kvr, 2 * LANES), lambda h, m: (0, h + first)),
            pl.BlockSpec((1, rows, LANES), lambda h, m: (m, 0, 0)),
            pl.BlockSpec((1, rows, LANES), lambda h, m: (m, 0, 0)),
            pl.BlockSpec((1, 8, rows), lambda h, m: (m, 0, 0)),
            pl.BlockSpec((1, rows, LANES), lambda h, m: (m, 0, h + first)),
            pl.BlockSpec((1, 1, 2, rows), lambda h, m: (m, h + first, 0, 0)),
        ],
        out_specs=[
            pl.BlockSpec((micros, rows, rank), lambda h, m: (0, 0, 0)),
            pl.BlockSpec((nz, micros, rows, lanes), lambda h, m: (0, 0, 0, 0)),
            pl.BlockSpec((rank, 4 * LANES), lambda h, m: (0, h)),
            pl.BlockSpec((kvr, 2 * LANES), lambda h, m: (0, h)),
        ],
        out_shape=[
            jax.ShapeDtypeStruct((micros, rows, rank), bf16),
            jax.ShapeDtypeStruct((nz, micros, rows, lanes), bf16),
            jax.ShapeDtypeStruct((rank, pairs * 4 * LANES), bf16),
            jax.ShapeDtypeStruct((kvr, pairs * 2 * LANES), bf16),
        ],
        scratch_shapes=[
            pltpu.VMEM((micros, rows, rank), f32),
            pltpu.VMEM((micros, seq, lanes), f32),
            pltpu.VMEM((rank, 4 * LANES), f32),
            pltpu.VMEM((kvr, 2 * LANES), f32),
        ],
        compiler_params=pltpu.CompilerParams(vmem_limit_bytes=VMEM_ATTEND),
        cost_estimate=cost(18 * pairs),
        name="attend_back",
    )(query_normed, wq, latent_all, lup, cosine, sine, spans, grads, logs)


COLS = 256
WIDE = 512
WIDE_OUT = 640


def rows_of(ref):
    return ref[...].reshape(-1, ref.shape[2])


def column_block(weights, own_rows, kind):
    return pl.BlockSpec((weights.shape[0], own_rows, COLS), lambda i: (0, kind, i))


def ffn_up_kernel(x_ref, gate_ref, up_ref, gate_out, up_out, hidden_out):
    gate = product(x_ref[...], rows_of(gate_ref))
    up = product(x_ref[...], rows_of(up_ref))
    gate_out[...] = gate.astype(bf16)
    up_out[...] = up.astype(bf16)
    hidden_out[...] = (gate * jax.nn.sigmoid(gate) * up).astype(bf16)


def ffn_up(x, weights, own_rows):
    rows, width = x.shape
    units = weights.shape[2]
    tile = pl.BlockSpec((rows, COLS), lambda i: (0, i))
    return pl.pallas_call(
        ffn_up_kernel,
        grid=(pl.cdiv(units, COLS),),
        in_specs=[
            pl.BlockSpec((rows, width), lambda i: (0, 0)),
            column_block(weights, own_rows, 0),
            column_block(weights, own_rows, 1),
        ],
        out_specs=[tile] * 3,
        out_shape=[jax.ShapeDtypeStruct((rows, units), bf16)] * 3,
        compiler_params=pltpu.CompilerParams(vmem_limit_bytes=VMEM_FFN),
        cost_estimate=cost(18),
        name="ffn_up",
    )(x, weights, weights)


def ffn_back_kernel(x_ref, down_ref, gate_ref, up_ref, g_gate_out, g_up_out):
    grad = product(x_ref[...], rows_of(down_ref))
    gate = gate_ref[...].astype(f32)
    sig = jax.nn.sigmoid(gate)
    g_gate_out[...] = (
        grad * up_ref[...].astype(f32) * sig * (1.0 + gate * (1.0 - sig))
    ).astype(bf16)
    g_up_out[...] = (grad * gate * sig).astype(bf16)


def ffn_back(x, weights, gate, up, own_rows):
    rows, width = x.shape
    units = weights.shape[2]
    tile = pl.BlockSpec((rows, COLS), lambda i: (0, i))
    return pl.pallas_call(
        ffn_back_kernel,
        grid=(pl.cdiv(units, COLS),),
        in_specs=[
            pl.BlockSpec((rows, width), lambda i: (0, 0)),
            column_block(weights, own_rows, 2),
            tile,
            tile,
        ],
        out_specs=[tile] * 2,
        out_shape=[jax.ShapeDtypeStruct((rows, units), bf16)] * 2,
        compiler_params=pltpu.CompilerParams(vmem_limit_bytes=VMEM_FFN),
        cost_estimate=cost(12),
        name="ffn_back",
    )(x, weights, gate, up)


def to_width_kernel(count, *refs):
    total = None
    for a_ref, w_ref in zip(refs[:count], refs[count : 2 * count]):
        term = contract_cols(a_ref[...], rows_of(w_ref))
        total = term if total is None else total + term
    refs[-1][...] = total.astype(bf16)


def to_width(half, values, weights, kinds, own_rows):
    count = len(values)
    rows, units = values[0].shape[0] // 2, values[0].shape[1]
    width = weights.shape[0] * own_rows
    per = WIDE_OUT // own_rows

    def owner_block(kind):
        return pl.BlockSpec((per, own_rows, units), lambda i: (i, kind, 0))

    return pl.pallas_call(
        functools.partial(to_width_kernel, count),
        grid=(width // WIDE_OUT,),
        in_specs=[pl.BlockSpec((rows, units), lambda i: (half, 0))] * count
        + [owner_block(kind) for kind in kinds],
        out_specs=pl.BlockSpec((rows, WIDE_OUT), lambda i: (0, i)),
        out_shape=jax.ShapeDtypeStruct((rows, width), bf16),
        compiler_params=pltpu.CompilerParams(vmem_limit_bytes=VMEM_FFN),
        cost_estimate=cost(6 * count),
        name="to_width",
    )(*values, *([weights] * count))


def weight_grad_kernel(a_ref, b_ref, out_ref):
    out_ref[...] = contract_rows(a_ref[...], b_ref[...]).astype(bf16)


def weight_grad(a, b):
    rows, width = a.shape
    units = b.shape[1]
    return pl.pallas_call(
        weight_grad_kernel,
        grid=(width // WIDE,),
        in_specs=[
            pl.BlockSpec((rows, WIDE), lambda i: (0, i)),
            pl.BlockSpec((rows, units), lambda i: (0, 0)),
        ],
        out_specs=pl.BlockSpec((WIDE, units), lambda i: (i, 0)),
        out_shape=jax.ShapeDtypeStruct((width, units), bf16),
        compiler_params=pltpu.CompilerParams(vmem_limit_bytes=VMEM_FFN),
        cost_estimate=cost(units * 0.006),
        name="weight_grad",
    )(a, b)


def on_device(
    tokens,
    segments,
    attn_gain,
    query_down,
    query_gain,
    query_up,
    latent_down,
    latent_gain,
    latent_up,
    out_weight,
    ffn_gain,
    gate_weight,
    up_weight,
    down_weight,
    cotangent,
):
    nx, nz = lax.axis_size("fsdp"), lax.axis_size("ctx")
    owners = nx * nz
    z, t = lax.axis_index("ctx"), lax.axis_index("tensor")
    micros, _, rows, width = tokens.shape
    seq = segments.shape[2]
    count = micros * rows
    share = count // TENSOR
    heads = query_up.shape[1] // (HD + ROPE)
    rank = query_down.shape[1]
    down_cols = rank + KVR + ROPE
    own_rows = query_down.shape[0]
    part_rows = own_rows // TENSOR
    half = ROPE // 2
    gain_sizes = [v.shape[0] for v in (attn_gain, query_gain, latent_gain, ffn_gain)]
    gain_total = sum(gain_sizes)
    gain_pad = GAIN_ROWS * down_cols - gain_total

    def share_of(values):
        return lax.dynamic_slice_in_dim(values, t * share, share, 0)

    down_own = lax.dynamic_slice_in_dim(
        jnp.concatenate([query_down, latent_down], axis=1), t * part_rows, part_rows, 0
    )
    gains = jnp.concatenate([attn_gain, query_gain, latent_gain, ffn_gain])
    gains = jnp.pad(gains, (0, gain_pad)).reshape(GAIN_ROWS, down_cols)
    order = Order()
    down_all, gain_all, up_query, up_latent, weight_out = front_gather(
        down_own, gains, query_up, latent_up, out_weight
    )
    down_whole = down_all.reshape(width, down_cols)
    up_query = up_query.reshape(rank, -1)
    up_latent = up_latent.reshape(KVR, -1)
    weight_out = weight_out.reshape(width, -1)
    order.mark(gain_all)

    cut = own_rows // 2
    pack_cols = out_weight.shape[1]
    query_rows = query_up.size // pack_cols
    own_query_up, own_latent_up = query_up, latent_up
    units = gate_weight.shape[1]
    f_rows = 2 * own_rows + cut
    f_all = [order(jnp.concatenate([gate_weight, up_weight, down_weight], axis=0))]
    for _ in range(1, nx):
        f_all.append(turn(f_all[-1], "fsdp"))
    f_gather = Gather(f_all[0][:f_rows])
    gain_blocks = gain_all.reshape(owners, -1).astype(f32)
    gain_list, start = [], 0
    for size in gain_sizes:
        gain_list.append(gain_blocks[:, start : start + size].reshape(-1))
        start += size
    gain_attn, gain_query, gain_latent, gain_ffn = gain_list

    seg = segments[:, 0]
    first_end = jnp.sum((seg < 1).astype(jnp.int32), axis=1, keepdims=True)
    second_end = jnp.sum((seg < 2).astype(jnp.int32), axis=1, keepdims=True)
    seg_own = lax.dynamic_slice_in_dim(seg, z * rows, rows, 1)
    own_starts = jnp.where(seg_own < 1, 0, jnp.where(seg_own < 2, first_end, second_end))
    own_index = jnp.broadcast_to(z * rows + jnp.arange(rows, dtype=jnp.int32), own_starts.shape)
    spans = jnp.pad(jnp.stack([own_starts, own_index], axis=1), ((0, 0), (0, 6), (0, 0)))
    lane = jnp.arange(LANES, dtype=jnp.int32)
    frequency = rope_base ** (-(lane % half).astype(f32) * (2.0 / ROPE))
    angles = (own_index - own_starts).astype(f32)[:, :, None] * frequency
    cos_own = jnp.where(lane < ROPE, jnp.cos(angles), 0.0)
    sin_own = jnp.where(lane < ROPE, jnp.sin(angles), 0.0) * jnp.where(lane < half, -1.0, 1.0)
    cos_share = share_of(cos_own.reshape(count, LANES))[:, :half]
    sin_share = share_of(sin_own.reshape(count, LANES))[:, half:ROPE]

    def rotated(values, cosine, sine):
        first, second = values[..., :half], values[..., half:]
        return jnp.concatenate(
            [first * cosine - second * sine, first * sine + second * cosine], axis=-1
        )

    inputs_low = tokens.reshape(count, width)
    tokens_share = share_of(inputs_low).astype(f32)
    normed_share = rms_scale(tokens_share, gain_attn).astype(bf16)
    raw = product(normed_share, down_whole)
    query_latent, latent_raw = raw[:, :rank], raw[:, rank:]
    query_normed = rms_scale(query_latent, gain_query).astype(bf16)
    latent = rms_scale(latent_raw[:, :KVR], gain_latent).astype(bf16)
    key_rope = rotated(latent_raw[:, KVR:], cos_share, sin_share).astype(bf16)
    latent = jnp.concatenate(
        [latent, jnp.pad(key_rope, ((0, 0), (0, LANES - ROPE)))], axis=1
    )
    order.mark(latent)
    lanes = KVR + LANES
    shared_pieces = gather_ctx(latent)

    column = jnp.arange(heads * (HD + ROPE), dtype=jnp.int32)
    feature = column % (HD + ROPE)
    target = (column // (HD + ROPE)) * (2 * LANES) + jnp.where(
        feature < HD, feature, feature - HD + LANES
    )
    spread = (target[:, None] == jnp.arange(heads * 2 * LANES)[None, :]).astype(bf16)
    wq = product(order(up_query), spread).astype(bf16)
    order.mark((wq, shared_pieces[1]))
    f_gather.start_z(order)
    shared = by_ctx(order(tuple(shared_pieces)))
    shared = jnp.concatenate([query_normed] + [shared[d] for d in range(nz)], axis=1)
    order.mark(shared)
    shared_slots = tensor_gather(shared)
    f_buffer = Buffer((3 * own_rows, units), order)
    order.mark((f_gather.piece, f_all[-1]))
    f_gather.pass_on(order)
    order.mark((cos_own, spans))
    shared = jnp.stack(from_slots(order(tuple(shared_slots))))
    query_normed = shared[..., :rank].reshape(micros, rows, rank)
    latent_all = jnp.stack(
        [shared[..., rank + d * lanes : rank + (d + 1) * lanes] for d in range(nz)]
    ).reshape(nz, micros, rows, lanes)
    order.mark((query_normed, latent_all))
    attended, logs = attend(
        order(query_normed), wq, latent_all, up_latent, cos_own, sin_own, spans
    )
    order.mark(attended)
    f_gather.arrive(order)
    f_gather.pass_on(order)
    attended = order(attended)

    def slot_halves(values):
        slots = to_slots(values.reshape((TENSOR, share) + values.shape[1:]))
        return jnp.concatenate(slots[:2], axis=0), jnp.concatenate(slots[2:], axis=0)

    def halves(values):
        return values.reshape(2, share, width)

    attended_kept, attended_sent = slot_halves(attended.reshape(count, -1))
    sent = contract_cols(attended_sent, weight_out).astype(bf16)
    kept = contract_cols(attended_kept, weight_out).astype(bf16)
    kept, sent = halves(kept), halves(sent)
    order.mark((kept, sent))
    near = swap(sent, 1)
    passed = add_low(kept[1], near[1])
    order.mark(passed)
    far_share = swap(passed, 2)
    x = lax.axis_index("fsdp")
    for e, far in enumerate(f_all):
        f_buffer.place(far[None, None], (x - e) % nx, z, 0)
    f_gather.place_old(f_buffer, order)
    f_buffer.filled(order)
    attn_share = kept[0].astype(f32) + near[0].astype(f32) + order(far_share).astype(f32)
    middle = tokens_share + branch_scale * attn_share
    ffn_share_in = rms_scale(middle, gain_ffn).astype(bf16)
    h_gather = PairGather([far[f_rows:] for far in f_all], order)
    order.mark((ffn_share_in, h_gather.piece))
    ffn_slots = tensor_gather(ffn_share_in)
    while f_gather.step + 1 < nz:
        f_gather.arrive(order)
        f_gather.pass_on(order)
    f_gather.arrive(order)
    f_gather.start_x(order)
    h_gather.start_z(order)
    f_gather.place_old(f_buffer, order)
    f_buffer.filled(order)
    upstream_slots = jnp.concatenate(slot_halves(order(cotangent).reshape(count, width)), axis=0)
    upstream_share = upstream_slots[:share].astype(f32)
    grad_ffn = (branch_scale * upstream_slots.astype(f32)).astype(bf16)
    ffn_in = jnp.concatenate(order(tuple(ffn_slots)), axis=0)
    order.mark((grad_ffn, ffn_in))
    while h_gather.step + 1 < nz:
        h_gather.arrive(order)
        h_gather.start_z(order)
        h_gather.place_before(f_buffer, order, f_rows)
    f_gather.arrive(order)
    f_gather.place(f_buffer, order)
    gate_val, up_val, hidden = ffn_up(ffn_in, f_buffer.result(), own_rows)
    order.mark(hidden)

    def blocks_of(gradient):
        return gradient.reshape((owners, -1) + gradient.shape[1:])

    s_down = PairScatter(blocks_of(weight_grad(grad_ffn, hidden)), order)
    h_gather.arrive(order)
    h_gather.place(f_buffer, order, f_rows)
    weights = f_buffer.result()
    grad_gate, grad_up = ffn_back(order(grad_ffn), weights, gate_val, up_val, own_rows)
    s_gate = Scatter(blocks_of(weight_grad(ffn_in, grad_gate)), 2)
    s_gate.start_x(order)
    grad_gate, grad_up = order((grad_gate, grad_up))
    sent = to_width(1, (grad_gate, grad_up), weights, (0, 1), own_rows)
    order.mark(sent)
    kept = to_width(0, order((grad_gate, grad_up)), weights, (0, 1), own_rows)
    order.mark(kept)
    grad_ffn_in = tensor_scatter(halves(kept), halves(sent))
    s_up = Scatter(blocks_of(weight_grad(ffn_in, order(grad_up))), 2)
    order.mark(s_up.blocks)
    s_gate.arrive(order)
    s_gate.start_x(order)
    s_down.forward(order)
    grad_middle, grad_gain_ffn = norm_back(middle, gain_ffn, order(grad_ffn_in))
    grad_middle = grad_middle + upstream_share
    grad_attn_share = (branch_scale * grad_middle).astype(bf16)
    order.mark(grad_attn_share)
    grad_attn_slots = tensor_gather(grad_attn_share)

    hidden = order(hidden)
    mixed_sent = to_width(1, (hidden,), weights, (2,), own_rows)
    mixed_kept = to_width(0, (hidden,), weights, (2,), own_rows)
    order.mark((mixed_kept, mixed_sent))
    s_gate.forward(order)
    grad_attn = jnp.concatenate(order(tuple(grad_attn_slots)), axis=0)
    order.mark(grad_attn)

    grad_attended = product(grad_attn, weight_out).astype(bf16)
    grad_attended = jnp.concatenate(from_slots(jnp.split(grad_attended, TENSOR)), axis=0)
    attended_slots = jnp.concatenate([attended_kept, attended_sent], axis=0)
    s_out = Scatter(blocks_of(weight_grad(order(grad_attn), attended_slots)), 1)
    order.mark((s_out.blocks, grad_attended))
    s_gate.arrive(order)
    s_up.start_x(order)
    s_up.start_x(order)
    s_out.start_x(order)
    s_down.forward(order)
    operands = (
        query_normed,
        wq,
        latent_all,
        up_latent,
        cos_own,
        sin_own,
        spans,
        order(grad_attended).reshape(micros, rows, -1),
        logs,
    )
    pairs = heads // 2
    early = (pairs + 1) // 2
    one = attend_back(0, early, *operands)
    order.mark(one[0])
    ffn_share = tensor_scatter(halves(order(mixed_kept)), halves(order(mixed_sent)))
    s_gate.forward(order)
    s_up.forward(order)
    s_down.forward(order)
    two = attend_back(early, pairs - early, order(operands[0]), *operands[1:])
    order.mark((two[0], ffn_share))
    mixed_share = (middle + branch_scale * order(ffn_share)).astype(bf16)

    def gradient_slots(results):
        query = to_slots(results[0].reshape(TENSOR, share, rank))
        latents = to_slots(results[1].reshape(nz, TENSOR, share, lanes), 1)
        return [
            jnp.concatenate([q] + [v[d] for d in range(nz)], axis=1)
            for q, v in zip(query, latents)
        ]

    sums = [add_low(a, b) for a, b in zip(gradient_slots(one), gradient_slots(two))]
    kept, sent = jnp.stack(sums[:2]), jnp.stack(sums[2:])
    order.mark((kept, sent))
    g_share = tensor_scatter(kept, sent)
    s_gate.forward(order)
    s_up.forward(order)
    s_out.arrive(order)
    s_out.forward(order)
    g_wq = order(jnp.concatenate([one[2], two[2]], axis=1))
    grad_query_up = contract_cols(g_wq, spread).astype(bf16)
    s_pack = Scatter(
        jnp.concatenate(
            [
                grad_query_up.reshape(owners, -1, pack_cols),
                jnp.concatenate([one[3], two[3]], axis=1).reshape(owners, -1, pack_cols),
            ],
            axis=1,
        ),
        1,
    )
    order.mark((s_pack.blocks, mixed_share))
    g_latent_blocks = jnp.stack(
        [g_share[:, rank + d * lanes : rank + (d + 1) * lanes] for d in range(nz)]
    ).astype(bf16)
    order.mark(g_latent_blocks)
    latent_parts = scatter_parts(g_latent_blocks)
    g_latent_share = sum(v.astype(f32) for v in order(tuple(latent_parts)))
    grad_query_latent, grad_gain_query = norm_back(query_latent, gain_query, g_share[:, :rank])
    grad_latent_first, grad_gain_latent = norm_back(
        latent_raw[:, :KVR], gain_latent, g_latent_share[:, :KVR]
    )
    grad_rope = rotated(g_latent_share[:, KVR : KVR + ROPE], cos_share, -sin_share)
    grad_raw = jnp.concatenate(
        [grad_query_latent, grad_latent_first, grad_rope], axis=1
    ).astype(bf16)
    order.mark(grad_raw)
    grad_raw_slots = tensor_gather(grad_raw)
    s_gate.forward(order)
    s_up.forward(order)
    s_out.forward(order)
    s_pack.start_x(order)
    grad_normed = contract_cols(order(grad_raw), down_whole)
    grad_inputs, grad_gain_attn = norm_back(tokens_share, gain_attn, grad_normed)
    grad_share = (grad_inputs + grad_middle).astype(bf16)
    normed = rms_scale(order(inputs_low).astype(f32), gain_attn).astype(bf16)
    order.mark((grad_share, normed))
    grad_raw_all = jnp.concatenate(from_slots(order(tuple(grad_raw_slots))), axis=0)
    grad_down = weight_grad(normed, grad_raw_all).reshape(owners, TENSOR, part_rows, down_cols)
    grad_down = lax.dynamic_index_in_dim(grad_down, t, 1, keepdims=False)
    gain_grads = jnp.concatenate(
        [
            g.reshape(owners, -1)
            for g in (grad_gain_attn, grad_gain_query, grad_gain_latent, grad_gain_ffn)
        ],
        axis=1,
    ).astype(bf16)
    gain_grads = jnp.pad(gain_grads, ((0, 0), (0, gain_pad))).reshape(
        owners, GAIN_ROWS, down_cols
    )
    s_bundle = Scatter(jnp.concatenate([grad_down, gain_grads], axis=1), 1)
    s_bundle.start_x(order)
    s_pack.arrive(order)
    s_up.forward(order)
    s_out.forward(order)
    s_pack.forward(order)
    last_share = jnp.concatenate([order(grad_share), mixed_share], axis=0)
    order.mark(last_share)
    last_slots = tensor_gather(last_share)
    s_bundle.arrive(order)
    s_bundle.forward(order)
    s_pack.forward(order)
    s_bundle.forward(order)
    s_pack.forward(order)
    while s_bundle.step < nz:
        s_bundle.forward(order)
    bundle_share = s_bundle.total.astype(bf16)
    order.mark(bundle_share)
    bundle_slots = tensor_gather(bundle_share)
    for scatter in (s_up, s_out, s_pack):
        while scatter.step < nz:
            scatter.forward(order)
    last_list = from_slots(order(tuple(last_slots)))
    grad_tokens = jnp.concatenate([v[:share] for v in last_list], axis=0).astype(f32)
    mixed = jnp.concatenate([v[share:] for v in last_list], axis=0)
    bundle_list = from_slots(order(tuple(bundle_slots)))
    out_down = jnp.concatenate([b[:part_rows] for b in bundle_list], axis=0).astype(f32)
    gain_sum = sum(b[part_rows:].astype(f32) for b in bundle_list).reshape(-1)
    out_gains, start = [], 0
    for size in gain_sizes:
        out_gains.append(gain_sum[start : start + size])
        start += size
    out_query_up = s_pack.total[:query_rows].reshape(query_up.shape)
    out_latent_up = s_pack.total[query_rows:].reshape(latent_up.shape)

    return (
        mixed.reshape(tokens.shape),
        grad_tokens.reshape(tokens.shape),
        out_gains[0],
        out_down[:, :rank],
        out_gains[1],
        out_query_up,
        out_down[:, rank:],
        out_gains[2],
        out_latent_up,
        s_out.total,
        out_gains[3],
        s_gate.total,
        s_up.total,
        s_down.result(),
    )


def solution(mesh):
    return jax.shard_map(
        on_device,
        mesh=mesh,
        in_specs=(
            P(None, "fsdp", "ctx", None),
            P(None, "fsdp", None),
            P(("fsdp", "ctx")),
            P(("fsdp", "ctx"), None),
            P(("fsdp", "ctx")),
            P(("fsdp", "ctx"), "tensor"),
            P(("fsdp", "ctx"), None),
            P(("fsdp", "ctx")),
            P(("fsdp", "ctx"), "tensor"),
            P(("fsdp", "ctx"), "tensor"),
            P(("fsdp", "ctx")),
            P(("fsdp", "ctx"), "tensor"),
            P(("fsdp", "ctx"), "tensor"),
            P(("fsdp", "ctx"), "tensor"),
            P(None, "fsdp", "ctx", None),
        ),
        out_specs=(
            P(None, "fsdp", "ctx", None),
            P(None, "fsdp", "ctx", None),
            P(("fsdp", "ctx")),
            P(("fsdp", "ctx"), None),
            P(("fsdp", "ctx")),
            P(("fsdp", "ctx"), "tensor"),
            P(("fsdp", "ctx"), None),
            P(("fsdp", "ctx")),
            P(("fsdp", "ctx"), "tensor"),
            P(("fsdp", "ctx"), "tensor"),
            P(("fsdp", "ctx")),
            P(("fsdp", "ctx"), "tensor"),
            P(("fsdp", "ctx"), "tensor"),
            P(("fsdp", "ctx"), "tensor"),
        ),
        check_vma=False,
    )
```

```python
import functools
import math

import jax
import jax.numpy as jnp
from jax import lax
from jax.experimental import pallas as pl
from jax.experimental.pallas import tpu as pltpu
from jax.sharding import PartitionSpec as P

KVR = 256
ROPE = 32
HD = 64
VD = 64
LANES = 128
GAIN_ROWS = 16
TENSOR = 4

norm_eps = 1e-05
branch_scale = 1.4 / math.sqrt(62.0)
rope_base = 10000.0
masked_fill = -1e30
att_scale = (HD + ROPE) ** (-0.5)
att_scale_log2 = att_scale / math.log(2.0)

bf16 = jnp.bfloat16
f32 = jnp.float32


def product(left_side, right_side):
    return jnp.dot(left_side, right_side, preferred_element_type=f32)


def contract_rows(left_side, right_side):
    return lax.dot_general(
        left_side, right_side, (((0,), (0,)), ((), ())), preferred_element_type=f32
    )


def contract_cols(left_side, right_side):
    return lax.dot_general(
        left_side, right_side, (((1,), (1,)), ((), ())), preferred_element_type=f32
    )


def rms_scale(values, gain_vec):
    return (
        values * lax.rsqrt(jnp.mean(values * values, axis=-1, keepdims=True) + norm_eps) * gain_vec
    )


def norm_back(values, gain_vec, gradient):
    return jax.vjp(rms_scale, values, gain_vec)[1](gradient)


def add_low(left_side, right_side):
    return (left_side.astype(f32) + right_side.astype(f32)).astype(bf16)


def after(values, *others):
    return lax.optimization_barrier((values,) + others)[0]


def turn(values, axis):
    size = lax.axis_size(axis)
    return lax.ppermute(values, axis, [(i, (i + 1) % size) for i in range(size)])


class Order:
    def __init__(self):
        self.events = []

    def __call__(self, values):
        return after(values, *self.events[-10:]) if self.events else values

    def mark(self, event):
        self.events.append(event)


class Buffer:
    def __init__(self, shape, order):
        sizes = (lax.axis_size("fsdp"), lax.axis_size("ctx"))
        self.whole = jnp.broadcast_to(order(jnp.zeros((), bf16)), sizes + shape)

    def place(self, piece, x, z, row):
        self.whole = lax.dynamic_update_slice(self.whole, piece, (x, z, row, 0))

    def filled(self, order):
        order.mark(self.whole[0, 0, 0, :LANES])

    def result(self):
        return self.whole.reshape((-1,) + self.whole.shape[2:])


class Gather:
    def __init__(self, shard):
        self.nx, self.nz = lax.axis_size("fsdp"), lax.axis_size("ctx")
        self.x, self.z = lax.axis_index("fsdp"), lax.axis_index("ctx")
        self.piece = shard
        self.step = 0
        self.waiting = []

    def start_x(self, order):
        far = order(self.piece)
        self.waiting.append((far, 0, self.step))
        self.sent = True
        for e in range(1, self.nx):
            far = turn(far, "fsdp")
            self.waiting.append((far, e, self.step))

    def start_z(self, order):
        if self.step + 1 < self.nz:
            self.piece = turn(order(self.piece), "ctx")
            self.step += 1

    def pass_on(self, order):
        held, step = self.piece, self.step
        self.start_z(order)
        piece, self.piece, self.step = self.piece, held, step
        self.start_x(order)
        if step + 1 < self.nz:
            self.piece, self.step = piece, step + 1

    def arrive(self, order):
        order.mark((self.piece, self.waiting[-1][0]) if self.waiting else self.piece)

    def place_old(self, buffer, order, row=0):
        last = self.waiting[-1][2]
        late = [w for w in self.waiting if w[2] == last]
        self.waiting = [w for w in self.waiting if w[2] != last]
        self.place(buffer, order, row)
        self.waiting = late

    def place(self, buffer, order, row=0):
        for far, e, step in self.waiting:
            buffer.place(
                order(far)[None, None], (self.x - e) % self.nx, (self.z - step) % self.nz, row
            )
        self.waiting = []


class PairGather:
    def __init__(self, far, order):
        self.nx, self.nz = lax.axis_size("fsdp"), lax.axis_size("ctx")
        self.x, self.z = lax.axis_index("fsdp"), lax.axis_index("ctx")
        self.far = far
        self.step = 0
        self.line(order)

    def line(self, order):
        piece = jnp.broadcast_to(order(jnp.zeros((), bf16)), (self.nx, 1) + self.far[0].shape)
        for e, far in enumerate(self.far):
            piece = lax.dynamic_update_slice(
                piece, order(far)[None, None], ((self.x - e) % self.nx, 0, 0, 0)
            )
        self.piece = piece

    def start_z(self, order):
        self.before = self.piece
        self.piece = turn(order(self.piece), "ctx")
        self.step += 1

    def arrive(self, order):
        order.mark(self.piece)

    def place_before(self, buffer, order, row):
        buffer.place(order(self.before), 0, (self.z - self.step + 1) % self.nz, row)

    def place(self, buffer, order, row):
        buffer.place(order(self.piece), 0, (self.z - self.step) % self.nz, row)


class Scatter:
    def __init__(self, blocks, groups):
        self.nx, self.nz = lax.axis_size("fsdp"), lax.axis_size("ctx")
        self.x, self.z = lax.axis_index("fsdp"), lax.axis_index("ctx")
        self.blocks = blocks
        self.size = self.nz // groups
        self.far = []
        self.total = None
        self.step = 0

    def own(self, e, d):
        owner = ((self.x - 1 - e) % self.nx) * self.nz + (self.z - 1 - d) % self.nz
        return lax.dynamic_index_in_dim(self.blocks, owner, 0, keepdims=False)

    def start_x(self, order):
        first = len(self.far) * self.size
        blocks, self.blocks = self.blocks, order(self.blocks)
        part = None
        for e in range(self.nx - 1):
            own = jnp.stack([self.own(e, first + k) for k in range(self.size)])
            part = own if part is None else add_low(part, own)
            order.mark(part)
            part = turn(part, "fsdp")
        self.blocks = blocks
        self.far.append(part)

    def arrive(self, order):
        order.mark(self.far[-1])

    def forward(self, order):
        d = self.step
        total = self.own(self.nx - 1, d).astype(f32)
        if self.nx > 1:
            total = total + order(self.far[d // self.size])[d % self.size].astype(f32)
        if d:
            total = total + order(self.total).astype(f32)
        self.step += 1
        if self.step == self.nz:
            self.total = total
        else:
            total = total.astype(bf16)
            order.mark(total)
            self.total = turn(total, "ctx")


class PairScatter:
    def __init__(self, blocks, order):
        self.nx, self.nz = lax.axis_size("fsdp"), lax.axis_size("ctx")
        self.x, self.z = lax.axis_index("fsdp"), lax.axis_index("ctx")
        self.blocks = order(blocks).reshape((self.nx, self.nz) + blocks.shape[1:])
        self.step = 0
        first = self.own(0)
        order.mark(first)
        self.total = turn(first, "ctx")

    def own(self, d):
        return lax.dynamic_index_in_dim(
            self.blocks, (self.z - 1 - d) % self.nz, 1, keepdims=False
        )

    def forward(self, order):
        self.step += 1
        total = add_low(order(self.total), self.own(self.step))
        order.mark(total)
        if self.step + 1 < self.nz:
            self.total = turn(total, "ctx")
            return
        part = None
        for e in range(self.nx):
            own = lax.dynamic_index_in_dim(total, (self.x - 1 - e) % self.nx, 0, keepdims=False)
            part = own if part is None else add_low(turn(part, "fsdp"), own)
        self.total = part

    def result(self):
        return self.total.astype(f32)


def shift(values, d):
    size = lax.axis_size("ctx")
    return lax.ppermute(values, "ctx", [(i, (i + d) % size) for i in range(size)])


def gather_ctx(values):
    return [values] + [shift(values, d) for d in range(1, lax.axis_size("ctx"))]


def by_ctx(pieces):
    nz, z = lax.axis_size("ctx"), lax.axis_index("ctx")
    values = pieces[0]
    whole = jnp.zeros((nz,) + values.shape, values.dtype)
    for d, piece in enumerate(pieces):
        whole = lax.dynamic_update_slice_in_dim(whole, piece[None], (z - d) % nz, 0)
    return whole


def scatter_parts(blocks):
    nz, z = lax.axis_size("ctx"), lax.axis_index("ctx")
    parts = [lax.dynamic_index_in_dim(blocks, (z + d) % nz, 0, keepdims=False) for d in range(nz)]
    return parts[:1] + [shift(parts[d], d) for d in range(1, nz)]


SLOTS = (0, 2, 1, 3)


def swap(values, bit):
    return lax.ppermute(values, "tensor", [(i, i ^ bit) for i in range(TENSOR)])


def tensor_gather(values):
    near = swap(values, 1)
    far = swap(values, 2)
    return [values, far, near, swap(far, 1)]


def tensor_gather_now(values, order):
    order.mark(values)
    slots = tensor_gather(values)
    order.mark(tuple(slots[1:]))
    return slots


def tensor_scatter(kept, sent):
    near = swap(sent, 1)
    far = swap(add_low(kept[1], near[1]), 2)
    return kept[0].astype(f32) + near[0].astype(f32) + far.astype(f32)


def to_slots(blocks, axis=0):
    t = lax.axis_index("tensor")
    return [lax.dynamic_index_in_dim(blocks, t ^ j, axis, keepdims=False) for j in SLOTS]


def from_slots(slots):
    t = lax.axis_index("tensor")
    low, high = (t & 1) == 1, (t & 2) == 2
    own, far, near, both = slots
    a = [
        jnp.where(low, near, own),
        jnp.where(low, own, near),
        jnp.where(low, both, far),
        jnp.where(low, far, both),
    ]
    return [
        jnp.where(high, a[2], a[0]),
        jnp.where(high, a[3], a[1]),
        jnp.where(high, a[0], a[2]),
        jnp.where(high, a[1], a[3]),
    ]


MESH = pl.DeviceIdType.MESH
FRONT = 5


def front_kernel(nx, nz, *refs):
    shards, outs = refs[:FRONT], refs[FRONT : 2 * FRONT]
    own_sem, z_send, z_recv, x_send, x_recv, t_send, t_recv = refs[2 * FRONT :]
    x, z, t = lax.axis_index("fsdp"), lax.axis_index("ctx"), lax.axis_index("tensor")
    right_x, left_x = lax.rem(x + 1, nx), lax.rem(x + nx - 1, nx)
    right_z, left_z = lax.rem(z + 1, nz), lax.rem(z + nz - 1, nz)
    near_t = t + 1 - 2 * lax.rem(t, 2)
    far_t = lax.rem(t + 2, TENSOR)

    barrier = pltpu.get_barrier_semaphore()
    partners = (
        {"fsdp": right_x},
        {"fsdp": left_x},
        {"ctx": right_z},
        {"ctx": left_z},
        {"tensor": near_t},
        {"tensor": far_t},
    )
    for partner in partners:
        pl.semaphore_signal(barrier, 1, device_id=partner, device_id_type=MESH)
    pl.semaphore_wait(barrier, len(partners))

    def block(a, xx, zz):
        return outs[a].at[xx, zz, t] if a == 0 else outs[a].at[xx, zz]

    def own(a):
        return pltpu.make_async_copy(shards[a], block(a, x, z), own_sem.at[a])

    def along_z(a, d):
        zz = lax.rem(z + nz - d, nz)
        return pltpu.make_async_remote_copy(
            src_ref=shards[a] if d == 0 else block(a, x, zz),
            dst_ref=block(a, x, zz),
            send_sem=z_send.at[a, d],
            recv_sem=z_recv.at[a, d],
            device_id={"ctx": right_z},
            device_id_type=MESH,
        )

    def along_x(a, d, e):
        xx, zz = lax.rem(x + nx - e, nx), lax.rem(z + nz - d, nz)
        return pltpu.make_async_remote_copy(
            src_ref=shards[a] if d + e == 0 else block(a, xx, zz),
            dst_ref=block(a, xx, zz),
            send_sem=x_send.at[a, d, e],
            recv_sem=x_recv.at[a, d, e],
            device_id={"fsdp": right_x},
            device_id_type=MESH,
        )

    def along_t(k, owner, partner):
        part = outs[0].at[:, :, owner]
        return pltpu.make_async_remote_copy(
            src_ref=part,
            dst_ref=part,
            send_sem=t_send.at[k],
            recv_sem=t_recv.at[k],
            device_id={"tensor": partner},
            device_id_type=MESH,
        )

    early, late = (0, 1), (2, 3, 4)
    for a in range(FRONT):
        own(a).start()
    for a in early:
        along_z(a, 0).start()
        along_x(a, 0, 0).start()
    for d in range(1, nz):
        for a in early:
            along_z(a, d - 1).wait_recv()
            if d + 1 < nz:
                along_z(a, d).start()
            along_x(a, d, 0).start()
    for a in late:
        along_z(a, 0).start()
        along_x(a, 0, 0).start()
    for d in range(nz):
        for e in range(1, nx):
            for a in early:
                along_x(a, d, e - 1).wait_recv()
                if e + 1 < nx:
                    along_x(a, d, e).start()
    own(0).wait()
    along_t(0, t, near_t).start()
    along_t(1, t, far_t).start()
    for d in range(1, nz):
        for a in late:
            along_z(a, d - 1).wait_recv()
            if d + 1 < nz:
                along_z(a, d).start()
            along_x(a, d, 0).start()
    along_t(1, t, far_t).wait_recv()
    along_t(2, far_t, near_t).start()
    for d in range(nz):
        for e in range(1, nx):
            for a in late:
                along_x(a, d, e - 1).wait_recv()
                if e + 1 < nx:
                    along_x(a, d, e).start()
    along_t(0, t, near_t).wait_recv()
    along_t(2, far_t, near_t).wait_recv()
    for a in range(1, FRONT):
        own(a).wait()
    for a in range(FRONT):
        for d in range(nz):
            if d + 1 < nz:
                along_z(a, d).wait_send()
            for e in range(nx - 1):
                along_x(a, d, e).wait_send()
    along_t(0, t, near_t).wait_send()
    along_t(1, t, far_t).wait_send()
    along_t(2, far_t, near_t).wait_send()


def front_gather(down, gains, query_up, latent_up, out_weight):
    nx, nz = lax.axis_size("fsdp"), lax.axis_size("ctx")
    shards = (down, gains, query_up, latent_up, out_weight)
    shapes = [
        jax.ShapeDtypeStruct((nx, nz) + ((TENSOR,) if a == 0 else ()) + v.shape, v.dtype)
        for a, v in enumerate(shards)
    ]
    return pl.pallas_call(
        functools.partial(front_kernel, nx, nz),
        in_specs=[pl.BlockSpec(memory_space=pl.ANY)] * FRONT,
        out_specs=[pl.BlockSpec(memory_space=pl.ANY)] * FRONT,
        out_shape=shapes,
        scratch_shapes=[
            pltpu.SemaphoreType.DMA((FRONT,)),
            pltpu.SemaphoreType.DMA((FRONT, nz)),
            pltpu.SemaphoreType.DMA((FRONT, nz)),
            pltpu.SemaphoreType.DMA((FRONT, nz, nx)),
            pltpu.SemaphoreType.DMA((FRONT, nz, nx)),
            pltpu.SemaphoreType.DMA((3,)),
            pltpu.SemaphoreType.DMA((3,)),
        ],
        compiler_params=pltpu.CompilerParams(collective_id=0, has_side_effects=True),
        cost_estimate=cost(88),
        name="front_gather",
    )(*shards)


def rotate_lanes(values, cosine, sine):
    lane = lax.broadcasted_iota(jnp.int32, values.shape, 1)
    half = ROPE // 2
    other = jnp.where(
        lane < half, pltpu.roll(values, LANES - half, 1), pltpu.roll(values, half, 1)
    )
    return values * cosine + other * sine


def head_inputs(normed_ref, wq, latent, rope, lup, cos_ref, sin_ref):
    raw = product(normed_ref[0], wq)
    rotated = rotate_lanes(raw[:, LANES:], cos_ref[0], sin_ref[0])
    query = jnp.concatenate([raw[:, :LANES], rotated], axis=1).astype(bf16)
    pair = product(latent, lup).astype(bf16)
    key = jnp.concatenate([pair, rope], axis=1)
    return query, pair, key


def latent_rows(latent_ref):
    nz, _, rows, lanes = latent_ref.shape
    held = latent_ref[...].reshape(nz * rows, lanes)
    return held[:, :KVR], held[:, KVR:]


def allowed_mask(span_ref, shape):
    key_index = lax.broadcasted_iota(jnp.int32, shape, 0)
    return (key_index >= span_ref[0, 0:1, :]) & (key_index <= span_ref[0, 1:2, :])


def attend_kernel(
    normed_ref,
    wq_ref,
    latent_ref,
    lup_ref,
    cos_ref,
    sin_ref,
    span_ref,
    out_ref,
    log_ref,
    normed_t_ref,
    latent_t_ref,
):
    latent, rope = latent_rows(latent_ref)

    @pl.when(pl.program_id(1) == 0)
    def _():
        normed_t_ref[0] = normed_ref[0].T
        latent_t_ref[0] = latent.T

    found = []
    for j in range(2):
        query, pair, key = head_inputs(
            normed_ref,
            wq_ref[:, 2 * LANES * j : 2 * LANES * (j + 1)],
            latent,
            rope,
            lup_ref[:, LANES * j : LANES * (j + 1)],
            cos_ref,
            sin_ref,
        )
        scores = contract_cols(key, query)
        scores = jnp.where(allowed_mask(span_ref, scores.shape), scores, masked_fill)
        highest = jnp.max(scores, axis=0, keepdims=True)
        exps = jnp.exp2((scores - highest) * att_scale_log2)
        total = jnp.sum(exps, axis=0, keepdims=True)
        probs = (exps * (1.0 / total)).astype(bf16)
        found.append(contract_rows(pair, probs)[HD:, :])
        log_ref[0, 0, j : j + 1, :] = highest * att_scale_log2 + jnp.log2(total)
    out_ref[0] = jnp.concatenate(found, axis=0).T.astype(bf16)


def attend_back_kernel(
    normed_ref,
    wq_ref,
    latent_ref,
    lup_ref,
    cos_ref,
    sin_ref,
    span_ref,
    grad_ref,
    log_ref,
    normed_t_ref,
    latent_t_ref,
    g_normed_ref,
    g_latent_ref,
    g_wq_ref,
    g_lup_ref,
    sum_normed,
    sum_latent,
    sum_wq,
    sum_lup,
):
    step, micro = pl.program_id(0), pl.program_id(1)

    @pl.when(step == 0)
    def _():
        sum_normed[micro] = jnp.zeros(sum_normed.shape[1:], f32)
        sum_latent[micro] = jnp.zeros(sum_latent.shape[1:], f32)

    @pl.when(micro == 0)
    def _():
        sum_wq[...] = jnp.zeros_like(sum_wq)
        sum_lup[...] = jnp.zeros_like(sum_lup)

    latent, rope = latent_rows(latent_ref)
    grad_pair = grad_ref[0].astype(f32)
    lane = lax.broadcasted_iota(jnp.int32, grad_pair.shape, 1)
    raw = product(normed_ref[0], wq_ref[...])
    pairs = product(latent, lup_ref[...]).astype(bf16)
    grad_pairs, grad_raws = [], []
    for j in range(2):
        raw_head = raw[:, 2 * LANES * j : 2 * LANES * (j + 1)]
        rotated = rotate_lanes(raw_head[:, LANES:], cos_ref[0], sin_ref[0])
        query = jnp.concatenate([raw_head[:, :LANES], rotated], axis=1).astype(bf16)
        pair = pairs[:, LANES * j : LANES * (j + 1)]
        key = jnp.concatenate([pair, rope], axis=1)
        grad_head = pltpu.roll(grad_pair, HD, 1) if j == 0 else grad_pair
        grad_head = jnp.where(lane >= HD, grad_head, 0.0).astype(bf16)
        scores = contract_cols(key, query)
        probs = jnp.where(
            allowed_mask(span_ref, scores.shape),
            jnp.exp2(scores * att_scale_log2 - log_ref[0, 0, j : j + 1, :]),
            0.0,
        )
        grad_probs = contract_cols(pair, grad_head)
        delta = jnp.sum(probs * grad_probs, axis=0, keepdims=True)
        grad_scores = (probs * (grad_probs - delta) * att_scale).astype(bf16)
        grad_key = product(grad_scores, query)
        sum_latent[micro, :, KVR:] += grad_key[:, LANES:]
        grad_pairs.append(
            (grad_key[:, :LANES] + product(probs.astype(bf16), grad_head)).astype(bf16)
        )
        grad_query = contract_rows(grad_scores, key)
        rotated = rotate_lanes(grad_query[:, LANES:], cos_ref[0], -sin_ref[0])
        plain = jnp.where(lane < HD, grad_query[:, :LANES], 0.0)
        grad_raws += [plain, rotated]
    grad_pairs = jnp.concatenate(grad_pairs, axis=1)
    grad_raws = jnp.concatenate(grad_raws, axis=1).astype(bf16)
    sum_lup[...] += product(latent_t_ref[0], grad_pairs)
    sum_latent[micro, :, :KVR] += contract_cols(grad_pairs, lup_ref[...])
    sum_wq[...] += product(normed_t_ref[0], grad_raws)
    sum_normed[micro] += contract_cols(grad_raws, wq_ref[...])

    @pl.when(micro == pl.num_programs(1) - 1)
    def _():
        g_wq_ref[...] = sum_wq[...].astype(bf16)
        g_lup_ref[...] = sum_lup[...].astype(bf16)

    @pl.when(step == pl.num_programs(0) - 1)
    def _():
        g_normed_ref[micro] = sum_normed[micro].astype(bf16)
        nz, _, rows, lanes = g_latent_ref.shape
        g_latent_ref[:, micro] = sum_latent[micro].astype(bf16).reshape(nz, rows, lanes)


def cost(microseconds):
    return pl.CostEstimate(
        flops=int(microseconds * 1.15e9), bytes_accessed=1, transcendentals=0
    )


VMEM_ATTEND = 56 * 1024 * 1024
VMEM_FFN = 40 * 1024 * 1024


def attend(query_normed, wq, latent_all, lup, cosine, sine, spans):
    micros, rows, rank = query_normed.shape
    nz, _, _, lanes = latent_all.shape
    seq, kvr = nz * rows, KVR
    pairs = lup.shape[1] // (2 * LANES)
    return pl.pallas_call(
        attend_kernel,
        grid=(micros, pairs),
        in_specs=[
            pl.BlockSpec((1, rows, rank), lambda m, h: (m, 0, 0)),
            pl.BlockSpec((rank, 4 * LANES), lambda m, h: (0, h)),
            pl.BlockSpec((nz, 1, rows, lanes), lambda m, h: (0, m, 0, 0)),
            pl.BlockSpec((kvr, 2 * LANES), lambda m, h: (0, h)),
            pl.BlockSpec((1, rows, LANES), lambda m, h: (m, 0, 0)),
            pl.BlockSpec((1, rows, LANES), lambda m, h: (m, 0, 0)),
            pl.BlockSpec((1, 8, rows), lambda m, h: (m, 0, 0)),
        ],
        out_specs=[
            pl.BlockSpec((1, rows, LANES), lambda m, h: (m, 0, h)),
            pl.BlockSpec((1, 1, 2, rows), lambda m, h: (m, h, 0, 0)),
            pl.BlockSpec((1, rank, rows), lambda m, h: (m, 0, 0)),
            pl.BlockSpec((1, kvr, seq), lambda m, h: (m, 0, 0)),
        ],
        out_shape=[
            jax.ShapeDtypeStruct((micros, rows, pairs * LANES), bf16),
            jax.ShapeDtypeStruct((micros, pairs, 2, rows), f32),
            jax.ShapeDtypeStruct((micros, rank, rows), bf16),
            jax.ShapeDtypeStruct((micros, kvr, seq), bf16),
        ],
        compiler_params=pltpu.CompilerParams(vmem_limit_bytes=VMEM_ATTEND),
        cost_estimate=cost(42),
        name="attend",
    )(query_normed, wq, latent_all, lup, cosine, sine, spans)


def attend_back(first, pairs, *operands):
    query_normed, _, latent_all = operands[:3]
    micros, rows, rank = query_normed.shape
    nz, _, _, lanes = latent_all.shape
    seq, kvr = nz * rows, KVR
    return pl.pallas_call(
        attend_back_kernel,
        grid=(pairs, micros),
        in_specs=[
            pl.BlockSpec((1, rows, rank), lambda h, m: (m, 0, 0)),
            pl.BlockSpec((rank, 4 * LANES), lambda h, m: (0, h + first)),
            pl.BlockSpec((nz, 1, rows, lanes), lambda h, m: (0, m, 0, 0)),
            pl.BlockSpec((kvr, 2 * LANES), lambda h, m: (0, h + first)),
            pl.BlockSpec((1, rows, LANES), lambda h, m: (m, 0, 0)),
            pl.BlockSpec((1, rows, LANES), lambda h, m: (m, 0, 0)),
            pl.BlockSpec((1, 8, rows), lambda h, m: (m, 0, 0)),
            pl.BlockSpec((1, rows, LANES), lambda h, m: (m, 0, h + first)),
            pl.BlockSpec((1, 1, 2, rows), lambda h, m: (m, h + first, 0, 0)),
            pl.BlockSpec((1, rank, rows), lambda h, m: (m, 0, 0)),
            pl.BlockSpec((1, kvr, seq), lambda h, m: (m, 0, 0)),
        ],
        out_specs=[
            pl.BlockSpec((micros, rows, rank), lambda h, m: (0, 0, 0)),
            pl.BlockSpec((nz, micros, rows, lanes), lambda h, m: (0, 0, 0, 0)),
            pl.BlockSpec((rank, 4 * LANES), lambda h, m: (0, h)),
            pl.BlockSpec((kvr, 2 * LANES), lambda h, m: (0, h)),
        ],
        out_shape=[
            jax.ShapeDtypeStruct((micros, rows, rank), bf16),
            jax.ShapeDtypeStruct((nz, micros, rows, lanes), bf16),
            jax.ShapeDtypeStruct((rank, pairs * 4 * LANES), bf16),
            jax.ShapeDtypeStruct((kvr, pairs * 2 * LANES), bf16),
        ],
        scratch_shapes=[
            pltpu.VMEM((micros, rows, rank), f32),
            pltpu.VMEM((micros, seq, lanes), f32),
            pltpu.VMEM((rank, 4 * LANES), f32),
            pltpu.VMEM((kvr, 2 * LANES), f32),
        ],
        compiler_params=pltpu.CompilerParams(vmem_limit_bytes=VMEM_ATTEND),
        cost_estimate=cost(18 * pairs),
        name="attend_back",
    )(*operands)


COLS = 256
WIDE = 512
WIDE_OUT = 640


def rows_of(ref):
    return ref[...].reshape(-1, ref.shape[2])


def column_block(weights, own_rows, kind):
    return pl.BlockSpec((weights.shape[0], own_rows, COLS), lambda i: (0, kind, i))


def ffn_up_kernel(x_ref, gate_ref, up_ref, gate_out, up_out, hidden_out):
    gate = product(x_ref[...], rows_of(gate_ref))
    up = product(x_ref[...], rows_of(up_ref))
    gate_out[...] = gate.astype(bf16)
    up_out[...] = up.astype(bf16)
    hidden_out[...] = (gate * jax.nn.sigmoid(gate) * up).astype(bf16)


def ffn_up(x, weights, own_rows):
    rows, width = x.shape
    units = weights.shape[2]
    tile = pl.BlockSpec((rows, COLS), lambda i: (0, i))
    return pl.pallas_call(
        ffn_up_kernel,
        grid=(pl.cdiv(units, COLS),),
        in_specs=[
            pl.BlockSpec((rows, width), lambda i: (0, 0)),
            column_block(weights, own_rows, 0),
            column_block(weights, own_rows, 1),
        ],
        out_specs=[tile] * 3,
        out_shape=[jax.ShapeDtypeStruct((rows, units), bf16)] * 3,
        compiler_params=pltpu.CompilerParams(vmem_limit_bytes=VMEM_FFN),
        cost_estimate=cost(18),
        name="ffn_up",
    )(x, weights, weights)


def ffn_back_kernel(x_ref, down_ref, gate_ref, up_ref, g_gate_out, g_up_out):
    grad = product(x_ref[...], rows_of(down_ref))
    gate = gate_ref[...].astype(f32)
    sig = jax.nn.sigmoid(gate)
    g_gate_out[...] = (
        grad * up_ref[...].astype(f32) * sig * (1.0 + gate * (1.0 - sig))
    ).astype(bf16)
    g_up_out[...] = (grad * gate * sig).astype(bf16)


def ffn_back(x, weights, gate, up, own_rows):
    rows, width = x.shape
    units = weights.shape[2]
    tile = pl.BlockSpec((rows, COLS), lambda i: (0, i))
    return pl.pallas_call(
        ffn_back_kernel,
        grid=(pl.cdiv(units, COLS),),
        in_specs=[
            pl.BlockSpec((rows, width), lambda i: (0, 0)),
            column_block(weights, own_rows, 2),
            tile,
            tile,
        ],
        out_specs=[tile] * 2,
        out_shape=[jax.ShapeDtypeStruct((rows, units), bf16)] * 2,
        compiler_params=pltpu.CompilerParams(vmem_limit_bytes=VMEM_FFN),
        cost_estimate=cost(12),
        name="ffn_back",
    )(x, weights, gate, up)


def to_width_kernel(count, *refs):
    total = None
    for a_ref, w_ref in zip(refs[:count], refs[count : 2 * count]):
        term = contract_cols(a_ref[...], rows_of(w_ref))
        total = term if total is None else total + term
    refs[-1][...] = total.astype(bf16)


def to_width(half, values, weights, kinds, own_rows):
    count = len(values)
    rows, units = values[0].shape[0] // 2, values[0].shape[1]
    width = weights.shape[0] * own_rows
    per = WIDE_OUT // own_rows

    def owner_block(kind):
        return pl.BlockSpec((per, own_rows, units), lambda i: (i, kind, 0))

    return pl.pallas_call(
        functools.partial(to_width_kernel, count),
        grid=(width // WIDE_OUT,),
        in_specs=[pl.BlockSpec((rows, units), lambda i: (half, 0))] * count
        + [owner_block(kind) for kind in kinds],
        out_specs=pl.BlockSpec((rows, WIDE_OUT), lambda i: (0, i)),
        out_shape=jax.ShapeDtypeStruct((rows, width), bf16),
        compiler_params=pltpu.CompilerParams(vmem_limit_bytes=VMEM_FFN),
        cost_estimate=cost(6 * count),
        name="to_width",
    )(*values, *([weights] * count))


def weight_grad_kernel(a_ref, b_ref, out_ref):
    out_ref[...] = contract_rows(a_ref[...], b_ref[...]).astype(bf16)


def weight_grad(a, b):
    rows, width = a.shape
    units = b.shape[1]
    return pl.pallas_call(
        weight_grad_kernel,
        grid=(width // WIDE,),
        in_specs=[
            pl.BlockSpec((rows, WIDE), lambda i: (0, i)),
            pl.BlockSpec((rows, units), lambda i: (0, 0)),
        ],
        out_specs=pl.BlockSpec((WIDE, units), lambda i: (i, 0)),
        out_shape=jax.ShapeDtypeStruct((width, units), bf16),
        compiler_params=pltpu.CompilerParams(vmem_limit_bytes=VMEM_FFN),
        cost_estimate=cost(units * 0.006),
        name="weight_grad",
    )(a, b)


def on_device(
    tokens,
    segments,
    attn_gain,
    query_down,
    query_gain,
    query_up,
    latent_down,
    latent_gain,
    latent_up,
    out_weight,
    ffn_gain,
    gate_weight,
    up_weight,
    down_weight,
    cotangent,
):
    nx, nz = lax.axis_size("fsdp"), lax.axis_size("ctx")
    owners = nx * nz
    z, t = lax.axis_index("ctx"), lax.axis_index("tensor")
    micros, _, rows, width = tokens.shape
    seq = segments.shape[2]
    count = micros * rows
    share = count // TENSOR
    heads = query_up.shape[1] // (HD + ROPE)
    rank = query_down.shape[1]
    down_cols = rank + KVR + ROPE
    own_rows = query_down.shape[0]
    part_rows = own_rows // TENSOR
    half = ROPE // 2
    gain_sizes = [v.shape[0] for v in (attn_gain, query_gain, latent_gain, ffn_gain)]
    gain_total = sum(gain_sizes)
    gain_pad = GAIN_ROWS * down_cols - gain_total

    def share_of(values):
        return lax.dynamic_slice_in_dim(values, t * share, share, 0)

    down_own = lax.dynamic_slice_in_dim(
        jnp.concatenate([query_down, latent_down], axis=1), t * part_rows, part_rows, 0
    )
    gains = jnp.concatenate([attn_gain, query_gain, latent_gain, ffn_gain])
    gains = jnp.pad(gains, (0, gain_pad)).reshape(GAIN_ROWS, down_cols)
    order = Order()
    down_all, gain_all, up_query, up_latent, weight_out = front_gather(
        down_own, gains, query_up, latent_up, out_weight
    )
    down_whole = down_all.reshape(width, down_cols)
    up_query = up_query.reshape(rank, -1)
    up_latent = up_latent.reshape(KVR, -1)
    weight_out = weight_out.reshape(width, -1)
    order.mark(gain_all)

    cut = own_rows // 2
    pack_cols = out_weight.shape[1]
    query_rows = query_up.size // pack_cols
    own_query_up, own_latent_up = query_up, latent_up
    units = gate_weight.shape[1]
    f_rows = 2 * own_rows + cut
    f_all = [order(jnp.concatenate([gate_weight, up_weight, down_weight], axis=0))]
    for _ in range(1, nx):
        f_all.append(turn(f_all[-1], "fsdp"))
    f_gather = Gather(f_all[0][:f_rows])
    gain_blocks = gain_all.reshape(owners, -1).astype(f32)
    gain_list, start = [], 0
    for size in gain_sizes:
        gain_list.append(gain_blocks[:, start : start + size].reshape(-1))
        start += size
    gain_attn, gain_query, gain_latent, gain_ffn = gain_list

    seg = segments[:, 0]
    first_end = jnp.sum((seg < 1).astype(jnp.int32), axis=1, keepdims=True)
    second_end = jnp.sum((seg < 2).astype(jnp.int32), axis=1, keepdims=True)
    seg_own = lax.dynamic_slice_in_dim(seg, z * rows, rows, 1)
    own_starts = jnp.where(seg_own < 1, 0, jnp.where(seg_own < 2, first_end, second_end))
    own_index = jnp.broadcast_to(z * rows + jnp.arange(rows, dtype=jnp.int32), own_starts.shape)
    spans = jnp.pad(jnp.stack([own_starts, own_index], axis=1), ((0, 0), (0, 6), (0, 0)))
    lane = jnp.arange(LANES, dtype=jnp.int32)
    frequency = rope_base ** (-(lane % half).astype(f32) * (2.0 / ROPE))
    angles = (own_index - own_starts).astype(f32)[:, :, None] * frequency
    cos_own = jnp.where(lane < ROPE, jnp.cos(angles), 0.0)
    sin_own = jnp.where(lane < ROPE, jnp.sin(angles), 0.0) * jnp.where(lane < half, -1.0, 1.0)
    cos_share = share_of(cos_own.reshape(count, LANES))[:, :half]
    sin_share = share_of(sin_own.reshape(count, LANES))[:, half:ROPE]

    def rotated(values, cosine, sine):
        first, second = values[..., :half], values[..., half:]
        return jnp.concatenate(
            [first * cosine - second * sine, first * sine + second * cosine], axis=-1
        )

    inputs_low = tokens.reshape(count, width)
    tokens_share = share_of(inputs_low).astype(f32)
    normed_share = rms_scale(tokens_share, gain_attn).astype(bf16)
    raw = product(normed_share, down_whole)
    query_latent, latent_raw = raw[:, :rank], raw[:, rank:]
    query_normed = rms_scale(query_latent, gain_query).astype(bf16)
    latent = rms_scale(latent_raw[:, :KVR], gain_latent).astype(bf16)
    key_rope = rotated(latent_raw[:, KVR:], cos_share, sin_share).astype(bf16)
    latent = jnp.concatenate(
        [latent, jnp.pad(key_rope, ((0, 0), (0, LANES - ROPE)))], axis=1
    )
    order.mark(latent)
    lanes = KVR + LANES
    shared_pieces = gather_ctx(latent)

    column = jnp.arange(heads * (HD + ROPE), dtype=jnp.int32)
    feature = column % (HD + ROPE)
    target = (column // (HD + ROPE)) * (2 * LANES) + jnp.where(
        feature < HD, feature, feature - HD + LANES
    )
    spread = (target[:, None] == jnp.arange(heads * 2 * LANES)[None, :]).astype(bf16)
    wq = product(order(up_query), spread).astype(bf16)
    order.mark((wq, shared_pieces[1]))
    f_gather.start_z(order)
    shared = by_ctx(order(tuple(shared_pieces)))
    shared = jnp.concatenate([query_normed] + [shared[d] for d in range(nz)], axis=1)
    order.mark(shared)
    shared_slots = tensor_gather(shared)
    f_buffer = Buffer((3 * own_rows, units), order)
    order.mark((f_gather.piece, f_all[-1]))
    f_gather.pass_on(order)
    order.mark((cos_own, spans))
    shared = jnp.stack(from_slots(order(tuple(shared_slots))))
    query_normed = shared[..., :rank].reshape(micros, rows, rank)
    latent_all = jnp.stack(
        [shared[..., rank + d * lanes : rank + (d + 1) * lanes] for d in range(nz)]
    ).reshape(nz, micros, rows, lanes)
    order.mark((query_normed, latent_all))
    attended, logs, query_normed_t, latent_t = attend(
        order(query_normed), wq, latent_all, up_latent, cos_own, sin_own, spans
    )
    order.mark(attended)
    f_gather.arrive(order)
    f_gather.pass_on(order)
    attended = order(attended)

    def slot_halves(values):
        slots = to_slots(values.reshape((TENSOR, share) + values.shape[1:]))
        return jnp.concatenate(slots[:2], axis=0), jnp.concatenate(slots[2:], axis=0)

    def halves(values):
        return values.reshape(2, share, width)

    attended_kept, attended_sent = slot_halves(attended.reshape(count, -1))
    sent = contract_cols(attended_sent, weight_out).astype(bf16)
    kept = contract_cols(attended_kept, weight_out).astype(bf16)
    kept, sent = halves(kept), halves(sent)
    order.mark((kept, sent))
    near = swap(sent, 1)
    passed = add_low(kept[1], near[1])
    order.mark(passed)
    far_share = swap(passed, 2)
    x = lax.axis_index("fsdp")
    for e, far in enumerate(f_all):
        f_buffer.place(far[None, None], (x - e) % nx, z, 0)
    f_gather.place_old(f_buffer, order)
    f_buffer.filled(order)
    attn_share = kept[0].astype(f32) + near[0].astype(f32) + order(far_share).astype(f32)
    middle = tokens_share + branch_scale * attn_share
    ffn_share_in = rms_scale(middle, gain_ffn).astype(bf16)
    h_gather = PairGather([far[f_rows:] for far in f_all], order)
    order.mark((ffn_share_in, h_gather.piece))
    ffn_slots = tensor_gather(ffn_share_in)
    while f_gather.step + 1 < nz:
        f_gather.arrive(order)
        f_gather.pass_on(order)
    f_gather.arrive(order)
    f_gather.start_x(order)
    h_gather.start_z(order)
    f_gather.place_old(f_buffer, order)
    f_buffer.filled(order)
    upstream_slots = jnp.concatenate(slot_halves(order(cotangent).reshape(count, width)), axis=0)
    upstream_share = upstream_slots[:share].astype(f32)
    grad_ffn = (branch_scale * upstream_slots.astype(f32)).astype(bf16)
    ffn_in = jnp.concatenate(order(tuple(ffn_slots)), axis=0)
    order.mark((grad_ffn, ffn_in))
    while h_gather.step + 1 < nz:
        h_gather.arrive(order)
        h_gather.start_z(order)
        h_gather.place_before(f_buffer, order, f_rows)
    f_gather.arrive(order)
    f_gather.place(f_buffer, order)
    gate_val, up_val, hidden = ffn_up(ffn_in, f_buffer.result(), own_rows)
    order.mark(hidden)

    def blocks_of(gradient):
        return gradient.reshape((owners, -1) + gradient.shape[1:])

    s_down = PairScatter(blocks_of(weight_grad(grad_ffn, hidden)), order)
    h_gather.arrive(order)
    h_gather.place(f_buffer, order, f_rows)
    weights = f_buffer.result()
    grad_gate, grad_up = ffn_back(order(grad_ffn), weights, gate_val, up_val, own_rows)
    s_gate = Scatter(blocks_of(weight_grad(ffn_in, grad_gate)), 2)
    s_gate.start_x(order)
    grad_gate, grad_up = order((grad_gate, grad_up))
    sent = to_width(1, (grad_gate, grad_up), weights, (0, 1), own_rows)
    order.mark(sent)
    kept = to_width(0, order((grad_gate, grad_up)), weights, (0, 1), own_rows)
    order.mark(kept)
    grad_ffn_in = tensor_scatter(halves(kept), halves(sent))
    s_up = Scatter(blocks_of(weight_grad(ffn_in, order(grad_up))), 2)
    order.mark(s_up.blocks)
    s_gate.arrive(order)
    s_gate.start_x(order)
    s_down.forward(order)
    grad_middle, grad_gain_ffn = norm_back(middle, gain_ffn, order(grad_ffn_in))
    grad_middle = grad_middle + upstream_share
    grad_attn_share = (branch_scale * grad_middle).astype(bf16)
    order.mark(grad_attn_share)
    grad_attn_slots = tensor_gather(grad_attn_share)

    hidden = order(hidden)
    mixed_sent = to_width(1, (hidden,), weights, (2,), own_rows)
    mixed_kept = to_width(0, (hidden,), weights, (2,), own_rows)
    order.mark((mixed_kept, mixed_sent))
    s_gate.forward(order)
    grad_attn = jnp.concatenate(order(tuple(grad_attn_slots)), axis=0)
    order.mark(grad_attn)

    grad_attended = product(grad_attn, weight_out).astype(bf16)
    grad_attended = jnp.concatenate(from_slots(jnp.split(grad_attended, TENSOR)), axis=0)
    attended_slots = jnp.concatenate([attended_kept, attended_sent], axis=0)
    s_out = Scatter(blocks_of(weight_grad(order(grad_attn), attended_slots)), 1)
    order.mark((s_out.blocks, grad_attended))
    s_gate.arrive(order)
    s_up.start_x(order)
    s_up.start_x(order)
    s_out.start_x(order)
    s_down.forward(order)
    operands = (
        query_normed,
        wq,
        latent_all,
        up_latent,
        cos_own,
        sin_own,
        spans,
        order(grad_attended).reshape(micros, rows, -1),
        logs,
        query_normed_t,
        latent_t,
    )
    pairs = heads // 2
    early = (pairs + 1) // 2
    one = attend_back(0, early, *operands)
    order.mark(one[0])
    ffn_share = tensor_scatter(halves(order(mixed_kept)), halves(order(mixed_sent)))
    s_gate.forward(order)
    s_up.forward(order)
    s_down.forward(order)
    two = attend_back(early, pairs - early, order(operands[0]), *operands[1:])
    order.mark((two[0], ffn_share))
    mixed_share = (middle + branch_scale * order(ffn_share)).astype(bf16)

    def gradient_slots(results):
        query = to_slots(results[0].reshape(TENSOR, share, rank))
        latents = to_slots(results[1].reshape(nz, TENSOR, share, lanes), 1)
        return [
            jnp.concatenate([q] + [v[d] for d in range(nz)], axis=1)
            for q, v in zip(query, latents)
        ]

    sums = [add_low(a, b) for a, b in zip(gradient_slots(one), gradient_slots(two))]
    kept, sent = jnp.stack(sums[:2]), jnp.stack(sums[2:])
    order.mark((kept, sent))
    g_share = tensor_scatter(kept, sent)
    s_gate.forward(order)
    s_up.forward(order)
    s_out.arrive(order)
    s_out.forward(order)
    g_wq = order(jnp.concatenate([one[2], two[2]], axis=1))
    grad_query_up = contract_cols(g_wq, spread).astype(bf16)
    s_pack = Scatter(
        jnp.concatenate(
            [
                grad_query_up.reshape(owners, -1, pack_cols),
                jnp.concatenate([one[3], two[3]], axis=1).reshape(owners, -1, pack_cols),
            ],
            axis=1,
        ),
        1,
    )
    order.mark((s_pack.blocks, mixed_share))
    g_latent_blocks = jnp.stack(
        [g_share[:, rank + d * lanes : rank + (d + 1) * lanes] for d in range(nz)]
    ).astype(bf16)
    order.mark(g_latent_blocks)
    latent_parts = scatter_parts(g_latent_blocks)
    g_latent_share = sum(v.astype(f32) for v in order(tuple(latent_parts)))
    grad_query_latent, grad_gain_query = norm_back(query_latent, gain_query, g_share[:, :rank])
    grad_latent_first, grad_gain_latent = norm_back(
        latent_raw[:, :KVR], gain_latent, g_latent_share[:, :KVR]
    )
    grad_rope = rotated(g_latent_share[:, KVR : KVR + ROPE], cos_share, -sin_share)
    grad_raw = jnp.concatenate(
        [grad_query_latent, grad_latent_first, grad_rope], axis=1
    ).astype(bf16)
    order.mark(grad_raw)
    grad_raw_slots = tensor_gather(grad_raw)
    s_gate.forward(order)
    s_up.forward(order)
    s_out.forward(order)
    s_pack.start_x(order)
    grad_normed = contract_cols(order(grad_raw), down_whole)
    grad_inputs, grad_gain_attn = norm_back(tokens_share, gain_attn, grad_normed)
    grad_share = (grad_inputs + grad_middle).astype(bf16)
    normed = rms_scale(order(inputs_low).astype(f32), gain_attn).astype(bf16)
    order.mark((grad_share, normed))
    grad_raw_all = jnp.concatenate(from_slots(order(tuple(grad_raw_slots))), axis=0)
    grad_down = weight_grad(normed, grad_raw_all).reshape(owners, TENSOR, part_rows, down_cols)
    grad_down = lax.dynamic_index_in_dim(grad_down, t, 1, keepdims=False)
    gain_grads = jnp.concatenate(
        [
            g.reshape(owners, -1)
            for g in (grad_gain_attn, grad_gain_query, grad_gain_latent, grad_gain_ffn)
        ],
        axis=1,
    ).astype(bf16)
    gain_grads = jnp.pad(gain_grads, ((0, 0), (0, gain_pad))).reshape(
        owners, GAIN_ROWS, down_cols
    )
    s_bundle = Scatter(jnp.concatenate([grad_down, gain_grads], axis=1), 1)
    s_bundle.start_x(order)
    s_pack.arrive(order)
    s_up.forward(order)
    s_out.forward(order)
    s_pack.forward(order)
    last_share = jnp.concatenate([order(grad_share), mixed_share], axis=0)
    order.mark(last_share)
    last_slots = tensor_gather(last_share)
    s_bundle.arrive(order)
    s_bundle.forward(order)
    s_pack.forward(order)
    s_bundle.forward(order)
    s_pack.forward(order)
    while s_bundle.step < nz:
        s_bundle.forward(order)
    bundle_share = s_bundle.total.astype(bf16)
    order.mark(bundle_share)
    bundle_slots = tensor_gather(bundle_share)
    for scatter in (s_up, s_out, s_pack):
        while scatter.step < nz:
            scatter.forward(order)
    last_list = from_slots(order(tuple(last_slots)))
    grad_tokens = jnp.concatenate([v[:share] for v in last_list], axis=0).astype(f32)
    mixed = jnp.concatenate([v[share:] for v in last_list], axis=0)
    bundle_list = from_slots(order(tuple(bundle_slots)))
    out_down = jnp.concatenate([b[:part_rows] for b in bundle_list], axis=0).astype(f32)
    gain_sum = sum(b[part_rows:].astype(f32) for b in bundle_list).reshape(-1)
    out_gains, start = [], 0
    for size in gain_sizes:
        out_gains.append(gain_sum[start : start + size])
        start += size
    out_query_up = s_pack.total[:query_rows].reshape(query_up.shape)
    out_latent_up = s_pack.total[query_rows:].reshape(latent_up.shape)

    return (
        mixed.reshape(tokens.shape),
        grad_tokens.reshape(tokens.shape),
        out_gains[0],
        out_down[:, :rank],
        out_gains[1],
        out_query_up,
        out_down[:, rank:],
        out_gains[2],
        out_latent_up,
        s_out.total,
        out_gains[3],
        s_gate.total,
        s_up.total,
        s_down.result(),
    )


def solution(mesh):
    return jax.shard_map(
        on_device,
        mesh=mesh,
        in_specs=(
            P(None, "fsdp", "ctx", None),
            P(None, "fsdp", None),
            P(("fsdp", "ctx")),
            P(("fsdp", "ctx"), None),
            P(("fsdp", "ctx")),
            P(("fsdp", "ctx"), "tensor"),
            P(("fsdp", "ctx"), None),
            P(("fsdp", "ctx")),
            P(("fsdp", "ctx"), "tensor"),
            P(("fsdp", "ctx"), "tensor"),
            P(("fsdp", "ctx")),
            P(("fsdp", "ctx"), "tensor"),
            P(("fsdp", "ctx"), "tensor"),
            P(("fsdp", "ctx"), "tensor"),
            P(None, "fsdp", "ctx", None),
        ),
        out_specs=(
            P(None, "fsdp", "ctx", None),
            P(None, "fsdp", "ctx", None),
            P(("fsdp", "ctx")),
            P(("fsdp", "ctx"), None),
            P(("fsdp", "ctx")),
            P(("fsdp", "ctx"), "tensor"),
            P(("fsdp", "ctx"), None),
            P(("fsdp", "ctx")),
            P(("fsdp", "ctx"), "tensor"),
            P(("fsdp", "ctx"), "tensor"),
            P(("fsdp", "ctx")),
            P(("fsdp", "ctx"), "tensor"),
            P(("fsdp", "ctx"), "tensor"),
            P(("fsdp", "ctx"), "tensor"),
        ),
        check_vma=False,
    )
```

```python
import functools
import math

import jax
import jax.numpy as jnp
from jax import lax
from jax.experimental import pallas as pl
from jax.experimental.pallas import tpu as pltpu
from jax.sharding import PartitionSpec as P

KVR = 256
ROPE = 32
HD = 64
VD = 64
LANES = 128
GAIN_ROWS = 16
TENSOR = 4

norm_eps = 1e-05
branch_scale = 1.4 / math.sqrt(62.0)
rope_base = 10000.0
masked_fill = -1e30
att_scale = (HD + ROPE) ** (-0.5)
att_scale_log2 = att_scale / math.log(2.0)

bf16 = jnp.bfloat16
f32 = jnp.float32


def product(left_side, right_side):
    return jnp.dot(left_side, right_side, preferred_element_type=f32)


def contract_rows(left_side, right_side):
    return lax.dot_general(
        left_side, right_side, (((0,), (0,)), ((), ())), preferred_element_type=f32
    )


def contract_cols(left_side, right_side):
    return lax.dot_general(
        left_side, right_side, (((1,), (1,)), ((), ())), preferred_element_type=f32
    )


def rms_scale(values, gain_vec):
    return (
        values * lax.rsqrt(jnp.mean(values * values, axis=-1, keepdims=True) + norm_eps) * gain_vec
    )


def norm_back(values, gain_vec, gradient):
    return jax.vjp(rms_scale, values, gain_vec)[1](gradient)


def add_low(left_side, right_side):
    return (left_side.astype(f32) + right_side.astype(f32)).astype(bf16)


def after(values, *others):
    return lax.optimization_barrier((values,) + others)[0]


def turn(values, axis):
    size = lax.axis_size(axis)
    return lax.ppermute(values, axis, [(i, (i + 1) % size) for i in range(size)])


class Order:
    def __init__(self):
        self.events = []

    def __call__(self, values):
        return after(values, *self.events[-10:]) if self.events else values

    def mark(self, event):
        self.events.append(event)


class Buffer:
    def __init__(self, shape, order):
        sizes = (lax.axis_size("fsdp"), lax.axis_size("ctx"))
        self.whole = jnp.broadcast_to(order(jnp.zeros((), bf16)), sizes + shape)

    def place(self, piece, x, z, row):
        self.whole = lax.dynamic_update_slice(self.whole, piece, (x, z, row, 0))

    def filled(self, order):
        order.mark(self.whole[0, 0, 0, :LANES])

    def result(self):
        return self.whole.reshape((-1,) + self.whole.shape[2:])


class Gather:
    def __init__(self, shard):
        self.nx, self.nz = lax.axis_size("fsdp"), lax.axis_size("ctx")
        self.x, self.z = lax.axis_index("fsdp"), lax.axis_index("ctx")
        self.piece = shard
        self.step = 0
        self.waiting = []

    def start_x(self, order):
        far = order(self.piece)
        self.waiting.append((far, 0, self.step))
        self.sent = True
        for e in range(1, self.nx):
            far = turn(far, "fsdp")
            self.waiting.append((far, e, self.step))

    def start_z(self, order):
        if self.step + 1 < self.nz:
            self.piece = turn(order(self.piece), "ctx")
            self.step += 1

    def pass_on(self, order):
        held, step = self.piece, self.step
        self.start_z(order)
        piece, self.piece, self.step = self.piece, held, step
        self.start_x(order)
        if step + 1 < self.nz:
            self.piece, self.step = piece, step + 1

    def arrive(self, order):
        order.mark((self.piece, self.waiting[-1][0]) if self.waiting else self.piece)

    def place_old(self, buffer, order, row=0):
        last = self.waiting[-1][2]
        late = [w for w in self.waiting if w[2] == last]
        self.waiting = [w for w in self.waiting if w[2] != last]
        self.place(buffer, order, row)
        self.waiting = late

    def place(self, buffer, order, row=0):
        for far, e, step in self.waiting:
            buffer.place(
                order(far)[None, None], (self.x - e) % self.nx, (self.z - step) % self.nz, row
            )
        self.waiting = []


class PairGather:
    def __init__(self, far, order):
        self.nx, self.nz = lax.axis_size("fsdp"), lax.axis_size("ctx")
        self.x, self.z = lax.axis_index("fsdp"), lax.axis_index("ctx")
        self.far = far
        self.step = 0
        self.line(order)

    def line(self, order):
        piece = jnp.broadcast_to(order(jnp.zeros((), bf16)), (self.nx, 1) + self.far[0].shape)
        for e, far in enumerate(self.far):
            piece = lax.dynamic_update_slice(
                piece, order(far)[None, None], ((self.x - e) % self.nx, 0, 0, 0)
            )
        self.piece = piece

    def start_z(self, order):
        self.before = self.piece
        self.piece = turn(order(self.piece), "ctx")
        self.step += 1

    def arrive(self, order):
        order.mark(self.piece)

    def place_before(self, buffer, order, row):
        buffer.place(order(self.before), 0, (self.z - self.step + 1) % self.nz, row)

    def place(self, buffer, order, row):
        buffer.place(order(self.piece), 0, (self.z - self.step) % self.nz, row)


class Scatter:
    def __init__(self, blocks, groups):
        self.nx, self.nz = lax.axis_size("fsdp"), lax.axis_size("ctx")
        self.x, self.z = lax.axis_index("fsdp"), lax.axis_index("ctx")
        self.blocks = blocks
        self.size = self.nz // groups
        self.far = []
        self.total = None
        self.step = 0

    def own(self, e, d):
        owner = ((self.x - 1 - e) % self.nx) * self.nz + (self.z - 1 - d) % self.nz
        return lax.dynamic_index_in_dim(self.blocks, owner, 0, keepdims=False)

    def start_x(self, order):
        first = len(self.far) * self.size
        blocks, self.blocks = self.blocks, order(self.blocks)
        part = None
        for e in range(self.nx - 1):
            own = jnp.stack([self.own(e, first + k) for k in range(self.size)])
            part = own if part is None else add_low(part, own)
            order.mark(part)
            part = turn(part, "fsdp")
        self.blocks = blocks
        self.far.append(part)

    def arrive(self, order):
        order.mark(self.far[-1])

    def forward(self, order):
        d = self.step
        total = self.own(self.nx - 1, d).astype(f32)
        if self.nx > 1:
            total = total + order(self.far[d // self.size])[d % self.size].astype(f32)
        if d:
            total = total + order(self.total).astype(f32)
        self.step += 1
        if self.step == self.nz:
            self.total = total
        else:
            total = total.astype(bf16)
            order.mark(total)
            self.total = turn(total, "ctx")


class PairScatter:
    def __init__(self, blocks, order):
        self.nx, self.nz = lax.axis_size("fsdp"), lax.axis_size("ctx")
        self.x, self.z = lax.axis_index("fsdp"), lax.axis_index("ctx")
        self.blocks = order(blocks).reshape((self.nx, self.nz) + blocks.shape[1:])
        self.step = 0
        first = self.own(0)
        order.mark(first)
        self.total = turn(first, "ctx")

    def own(self, d):
        return lax.dynamic_index_in_dim(
            self.blocks, (self.z - 1 - d) % self.nz, 1, keepdims=False
        )

    def forward(self, order):
        self.step += 1
        total = add_low(order(self.total), self.own(self.step))
        order.mark(total)
        if self.step + 1 < self.nz:
            self.total = turn(total, "ctx")
            return
        part = None
        for e in range(self.nx):
            own = lax.dynamic_index_in_dim(total, (self.x - 1 - e) % self.nx, 0, keepdims=False)
            part = own if part is None else add_low(turn(part, "fsdp"), own)
        self.total = part

    def result(self):
        return self.total.astype(f32)


def shift(values, d):
    size = lax.axis_size("ctx")
    return lax.ppermute(values, "ctx", [(i, (i + d) % size) for i in range(size)])


def gather_ctx(values):
    return [values] + [shift(values, d) for d in range(1, lax.axis_size("ctx"))]


def by_ctx(pieces):
    nz, z = lax.axis_size("ctx"), lax.axis_index("ctx")
    values = pieces[0]
    whole = jnp.zeros((nz,) + values.shape, values.dtype)
    for d, piece in enumerate(pieces):
        whole = lax.dynamic_update_slice_in_dim(whole, piece[None], (z - d) % nz, 0)
    return whole


def scatter_parts(blocks):
    nz, z = lax.axis_size("ctx"), lax.axis_index("ctx")
    parts = [lax.dynamic_index_in_dim(blocks, (z + d) % nz, 0, keepdims=False) for d in range(nz)]
    return parts[:1] + [shift(parts[d], d) for d in range(1, nz)]


SLOTS = (0, 2, 1, 3)


def swap(values, bit):
    return lax.ppermute(values, "tensor", [(i, i ^ bit) for i in range(TENSOR)])


def tensor_gather(values):
    near = swap(values, 1)
    far = swap(values, 2)
    return [values, far, near, swap(far, 1)]


def tensor_gather_now(values, order):
    order.mark(values)
    slots = tensor_gather(values)
    order.mark(tuple(slots[1:]))
    return slots


def tensor_scatter(kept, sent):
    near = swap(sent, 1)
    far = swap(add_low(kept[1], near[1]), 2)
    return kept[0].astype(f32) + near[0].astype(f32) + far.astype(f32)


def to_slots(blocks, axis=0):
    t = lax.axis_index("tensor")
    return [lax.dynamic_index_in_dim(blocks, t ^ j, axis, keepdims=False) for j in SLOTS]


def from_slots(slots):
    t = lax.axis_index("tensor")
    low, high = (t & 1) == 1, (t & 2) == 2
    own, far, near, both = slots
    a = [
        jnp.where(low, near, own),
        jnp.where(low, own, near),
        jnp.where(low, both, far),
        jnp.where(low, far, both),
    ]
    return [
        jnp.where(high, a[2], a[0]),
        jnp.where(high, a[3], a[1]),
        jnp.where(high, a[0], a[2]),
        jnp.where(high, a[1], a[3]),
    ]


MESH = pl.DeviceIdType.MESH
FRONT = 5


def front_kernel(nx, nz, *refs):
    shards, outs = refs[:FRONT], refs[FRONT : 2 * FRONT]
    own_sem, z_send, z_recv, x_send, x_recv, t_send, t_recv = refs[2 * FRONT :]
    x, z, t = lax.axis_index("fsdp"), lax.axis_index("ctx"), lax.axis_index("tensor")
    right_x, left_x = lax.rem(x + 1, nx), lax.rem(x + nx - 1, nx)
    right_z, left_z = lax.rem(z + 1, nz), lax.rem(z + nz - 1, nz)
    near_t = t + 1 - 2 * lax.rem(t, 2)
    far_t = lax.rem(t + 2, TENSOR)

    barrier = pltpu.get_barrier_semaphore()
    partners = (
        {"fsdp": right_x},
        {"fsdp": left_x},
        {"ctx": right_z},
        {"ctx": left_z},
        {"tensor": near_t},
        {"tensor": far_t},
    )
    for partner in partners:
        pl.semaphore_signal(barrier, 1, device_id=partner, device_id_type=MESH)
    pl.semaphore_wait(barrier, len(partners))

    def block(a, xx, zz):
        return outs[a].at[xx, zz, t] if a == 0 else outs[a].at[xx, zz]

    def own(a):
        return pltpu.make_async_copy(shards[a], block(a, x, z), own_sem.at[a])

    def along_z(a, d):
        zz = lax.rem(z + nz - d, nz)
        return pltpu.make_async_remote_copy(
            src_ref=shards[a] if d == 0 else block(a, x, zz),
            dst_ref=block(a, x, zz),
            send_sem=z_send.at[a, d],
            recv_sem=z_recv.at[a, d],
            device_id={"ctx": right_z},
            device_id_type=MESH,
        )

    def along_x(a, d, e):
        xx, zz = lax.rem(x + nx - e, nx), lax.rem(z + nz - d, nz)
        return pltpu.make_async_remote_copy(
            src_ref=shards[a] if d + e == 0 else block(a, xx, zz),
            dst_ref=block(a, xx, zz),
            send_sem=x_send.at[a, d, e],
            recv_sem=x_recv.at[a, d, e],
            device_id={"fsdp": right_x},
            device_id_type=MESH,
        )

    def along_t(k, owner, partner):
        part = outs[0].at[:, :, owner]
        return pltpu.make_async_remote_copy(
            src_ref=part,
            dst_ref=part,
            send_sem=t_send.at[k],
            recv_sem=t_recv.at[k],
            device_id={"tensor": partner},
            device_id_type=MESH,
        )

    early, late = (0, 1), (2, 3, 4)
    for a in range(FRONT):
        own(a).start()
    for a in early:
        along_z(a, 0).start()
        along_x(a, 0, 0).start()
    for d in range(1, nz):
        for a in early:
            along_z(a, d - 1).wait_recv()
            if d + 1 < nz:
                along_z(a, d).start()
            along_x(a, d, 0).start()
    for a in late:
        along_z(a, 0).start()
        along_x(a, 0, 0).start()
    for d in range(nz):
        for e in range(1, nx):
            for a in early:
                along_x(a, d, e - 1).wait_recv()
                if e + 1 < nx:
                    along_x(a, d, e).start()
    own(0).wait()
    along_t(0, t, near_t).start()
    along_t(1, t, far_t).start()
    for d in range(1, nz):
        for a in late:
            along_z(a, d - 1).wait_recv()
            if d + 1 < nz:
                along_z(a, d).start()
            along_x(a, d, 0).start()
    along_t(1, t, far_t).wait_recv()
    along_t(2, far_t, near_t).start()
    for d in range(nz):
        for e in range(1, nx):
            for a in late:
                along_x(a, d, e - 1).wait_recv()
                if e + 1 < nx:
                    along_x(a, d, e).start()
    along_t(0, t, near_t).wait_recv()
    along_t(2, far_t, near_t).wait_recv()
    for a in range(1, FRONT):
        own(a).wait()
    for a in range(FRONT):
        for d in range(nz):
            if d + 1 < nz:
                along_z(a, d).wait_send()
            for e in range(nx - 1):
                along_x(a, d, e).wait_send()
    along_t(0, t, near_t).wait_send()
    along_t(1, t, far_t).wait_send()
    along_t(2, far_t, near_t).wait_send()


def front_gather(down, gains, query_up, latent_up, out_weight):
    nx, nz = lax.axis_size("fsdp"), lax.axis_size("ctx")
    shards = (down, gains, query_up, latent_up, out_weight)
    shapes = [
        jax.ShapeDtypeStruct((nx, nz) + ((TENSOR,) if a == 0 else ()) + v.shape, v.dtype)
        for a, v in enumerate(shards)
    ]
    return pl.pallas_call(
        functools.partial(front_kernel, nx, nz),
        in_specs=[pl.BlockSpec(memory_space=pl.ANY)] * FRONT,
        out_specs=[pl.BlockSpec(memory_space=pl.ANY)] * FRONT,
        out_shape=shapes,
        scratch_shapes=[
            pltpu.SemaphoreType.DMA((FRONT,)),
            pltpu.SemaphoreType.DMA((FRONT, nz)),
            pltpu.SemaphoreType.DMA((FRONT, nz)),
            pltpu.SemaphoreType.DMA((FRONT, nz, nx)),
            pltpu.SemaphoreType.DMA((FRONT, nz, nx)),
            pltpu.SemaphoreType.DMA((3,)),
            pltpu.SemaphoreType.DMA((3,)),
        ],
        compiler_params=pltpu.CompilerParams(collective_id=0, has_side_effects=True),
        cost_estimate=cost(88),
        name="front_gather",
    )(*shards)


def rotate_lanes(values, cosine, sine):
    lane = lax.broadcasted_iota(jnp.int32, values.shape, 1)
    half = ROPE // 2
    other = jnp.where(
        lane < half, pltpu.roll(values, LANES - half, 1), pltpu.roll(values, half, 1)
    )
    return values * cosine + other * sine


def head_inputs(normed_ref, wq, latent, rope, lup, cos_ref, sin_ref):
    raw = product(normed_ref[0], wq)
    rotated = rotate_lanes(raw[:, LANES:], cos_ref[0], sin_ref[0])
    query = jnp.concatenate([raw[:, :LANES], rotated], axis=1).astype(bf16)
    pair = product(latent, lup).astype(bf16)
    key = jnp.concatenate([pair, rope], axis=1)
    return query, pair, key


def latent_rows(latent_ref):
    nz, _, rows, lanes = latent_ref.shape
    held = latent_ref[...].reshape(nz * rows, lanes)
    return held[:, :KVR], held[:, KVR:]


def allowed_mask(span_ref, shape):
    key_index = lax.broadcasted_iota(jnp.int32, shape, 0)
    return (key_index >= span_ref[0, 0:1, :]) & (key_index <= span_ref[0, 1:2, :])


def attend_kernel(
    normed_ref,
    wq_ref,
    latent_ref,
    lup_ref,
    cos_ref,
    sin_ref,
    span_ref,
    out_ref,
    log_ref,
    normed_t_ref,
    latent_t_ref,
):
    latent, rope = latent_rows(latent_ref)

    @pl.when(pl.program_id(1) == 0)
    def _():
        normed_t_ref[0] = normed_ref[0].T
        latent_t_ref[0] = latent.T

    found = []
    for j in range(2):
        query, pair, key = head_inputs(
            normed_ref,
            wq_ref[:, 2 * LANES * j : 2 * LANES * (j + 1)],
            latent,
            rope,
            lup_ref[:, LANES * j : LANES * (j + 1)],
            cos_ref,
            sin_ref,
        )
        scores = contract_cols(key, query)
        scores = jnp.where(allowed_mask(span_ref, scores.shape), scores, masked_fill)
        highest = jnp.max(scores, axis=0, keepdims=True)
        exps = jnp.exp2((scores - highest) * att_scale_log2)
        total = jnp.sum(exps, axis=0, keepdims=True)
        probs = (exps * (1.0 / total)).astype(bf16)
        found.append(contract_rows(pair, probs)[HD:, :])
        log_ref[0, 0, j : j + 1, :] = highest * att_scale_log2 + jnp.log2(total)
    out_ref[0] = jnp.concatenate(found, axis=0).T.astype(bf16)


def attend_back_kernel(
    normed_ref,
    wq_ref,
    latent_ref,
    lup_ref,
    cos_ref,
    sin_ref,
    span_ref,
    grad_ref,
    log_ref,
    normed_t_ref,
    latent_t_ref,
    g_normed_ref,
    g_latent_ref,
    g_wq_ref,
    g_lup_ref,
    sum_normed,
    sum_latent,
    sum_wq,
    sum_lup,
):
    step, micro = pl.program_id(0), pl.program_id(1)

    @pl.when(step == 0)
    def _():
        sum_normed[micro] = jnp.zeros(sum_normed.shape[1:], f32)
        sum_latent[micro] = jnp.zeros(sum_latent.shape[1:], f32)

    @pl.when(micro == 0)
    def _():
        sum_wq[...] = jnp.zeros_like(sum_wq)
        sum_lup[...] = jnp.zeros_like(sum_lup)

    latent, rope = latent_rows(latent_ref)
    grad_pair = grad_ref[0].astype(f32)
    lane = lax.broadcasted_iota(jnp.int32, grad_pair.shape, 1)
    raw = product(normed_ref[0], wq_ref[...])
    pairs = product(latent, lup_ref[...]).astype(bf16)
    grad_pairs, grad_raws = [], []
    for j in range(2):
        raw_head = raw[:, 2 * LANES * j : 2 * LANES * (j + 1)]
        rotated = rotate_lanes(raw_head[:, LANES:], cos_ref[0], sin_ref[0])
        query = jnp.concatenate([raw_head[:, :LANES], rotated], axis=1).astype(bf16)
        pair = pairs[:, LANES * j : LANES * (j + 1)]
        key = jnp.concatenate([pair, rope], axis=1)
        grad_head = pltpu.roll(grad_pair, HD, 1) if j == 0 else grad_pair
        grad_head = jnp.where(lane >= HD, grad_head, 0.0).astype(bf16)
        scores = contract_cols(key, query)
        probs = jnp.where(
            allowed_mask(span_ref, scores.shape),
            jnp.exp2(scores * att_scale_log2 - log_ref[0, 0, j : j + 1, :]),
            0.0,
        )
        grad_probs = contract_cols(pair, grad_head)
        delta = jnp.sum(probs * grad_probs, axis=0, keepdims=True)
        grad_scores = (probs * (grad_probs - delta) * att_scale).astype(bf16)
        grad_key = product(grad_scores, query)
        sum_latent[micro, :, KVR:] += grad_key[:, LANES:]
        grad_pairs.append(
            (grad_key[:, :LANES] + product(probs.astype(bf16), grad_head)).astype(bf16)
        )
        grad_query = contract_rows(grad_scores, key)
        rotated = rotate_lanes(grad_query[:, LANES:], cos_ref[0], -sin_ref[0])
        plain = jnp.where(lane < HD, grad_query[:, :LANES], 0.0)
        grad_raws += [plain, rotated]
    grad_pairs = jnp.concatenate(grad_pairs, axis=1)
    grad_raws = jnp.concatenate(grad_raws, axis=1).astype(bf16)
    sum_lup[...] += product(latent_t_ref[0], grad_pairs)
    sum_latent[micro, :, :KVR] += contract_cols(grad_pairs, lup_ref[...])
    sum_wq[...] += product(normed_t_ref[0], grad_raws)
    sum_normed[micro] += contract_cols(grad_raws, wq_ref[...])

    @pl.when(micro == pl.num_programs(1) - 1)
    def _():
        g_wq_ref[...] = sum_wq[...].astype(bf16)
        g_lup_ref[...] = sum_lup[...].astype(bf16)

    @pl.when(step == pl.num_programs(0) - 1)
    def _():
        g_normed_ref[micro] = sum_normed[micro].astype(bf16)
        nz, _, rows, lanes = g_latent_ref.shape
        g_latent_ref[:, micro] = sum_latent[micro].astype(bf16).reshape(nz, rows, lanes)


def cost(microseconds):
    return pl.CostEstimate(
        flops=int(microseconds * 1.15e9), bytes_accessed=1, transcendentals=0
    )


VMEM_ATTEND = 56 * 1024 * 1024
VMEM_FFN = 40 * 1024 * 1024


def attend(query_normed, wq, latent_all, lup, cosine, sine, spans):
    micros, rows, rank = query_normed.shape
    nz, _, _, lanes = latent_all.shape
    seq, kvr = nz * rows, KVR
    pairs = lup.shape[1] // (2 * LANES)
    return pl.pallas_call(
        attend_kernel,
        grid=(micros, pairs),
        in_specs=[
            pl.BlockSpec((1, rows, rank), lambda m, h: (m, 0, 0)),
            pl.BlockSpec((rank, 4 * LANES), lambda m, h: (0, h)),
            pl.BlockSpec((nz, 1, rows, lanes), lambda m, h: (0, m, 0, 0)),
            pl.BlockSpec((kvr, 2 * LANES), lambda m, h: (0, h)),
            pl.BlockSpec((1, rows, LANES), lambda m, h: (m, 0, 0)),
            pl.BlockSpec((1, rows, LANES), lambda m, h: (m, 0, 0)),
            pl.BlockSpec((1, 8, rows), lambda m, h: (m, 0, 0)),
        ],
        out_specs=[
            pl.BlockSpec((1, rows, LANES), lambda m, h: (m, 0, h)),
            pl.BlockSpec((1, 1, 2, rows), lambda m, h: (m, h, 0, 0)),
            pl.BlockSpec((1, rank, rows), lambda m, h: (m, 0, 0)),
            pl.BlockSpec((1, kvr, seq), lambda m, h: (m, 0, 0)),
        ],
        out_shape=[
            jax.ShapeDtypeStruct((micros, rows, pairs * LANES), bf16),
            jax.ShapeDtypeStruct((micros, pairs, 2, rows), f32),
            jax.ShapeDtypeStruct((micros, rank, rows), bf16),
            jax.ShapeDtypeStruct((micros, kvr, seq), bf16),
        ],
        compiler_params=pltpu.CompilerParams(vmem_limit_bytes=VMEM_ATTEND),
        cost_estimate=cost(42),
        name="attend",
    )(query_normed, wq, latent_all, lup, cosine, sine, spans)


def attend_back(first, pairs, *operands):
    query_normed, _, latent_all = operands[:3]
    micros, rows, rank = query_normed.shape
    nz, _, _, lanes = latent_all.shape
    seq, kvr = nz * rows, KVR
    return pl.pallas_call(
        attend_back_kernel,
        grid=(pairs, micros),
        in_specs=[
            pl.BlockSpec((1, rows, rank), lambda h, m: (m, 0, 0)),
            pl.BlockSpec((rank, 4 * LANES), lambda h, m: (0, h + first)),
            pl.BlockSpec((nz, 1, rows, lanes), lambda h, m: (0, m, 0, 0)),
            pl.BlockSpec((kvr, 2 * LANES), lambda h, m: (0, h + first)),
            pl.BlockSpec((1, rows, LANES), lambda h, m: (m, 0, 0)),
            pl.BlockSpec((1, rows, LANES), lambda h, m: (m, 0, 0)),
            pl.BlockSpec((1, 8, rows), lambda h, m: (m, 0, 0)),
            pl.BlockSpec((1, rows, LANES), lambda h, m: (m, 0, h + first)),
            pl.BlockSpec((1, 1, 2, rows), lambda h, m: (m, h + first, 0, 0)),
            pl.BlockSpec((1, rank, rows), lambda h, m: (m, 0, 0)),
            pl.BlockSpec((1, kvr, seq), lambda h, m: (m, 0, 0)),
        ],
        out_specs=[
            pl.BlockSpec((micros, rows, rank), lambda h, m: (0, 0, 0)),
            pl.BlockSpec((nz, micros, rows, lanes), lambda h, m: (0, 0, 0, 0)),
            pl.BlockSpec((rank, 4 * LANES), lambda h, m: (0, h)),
            pl.BlockSpec((kvr, 2 * LANES), lambda h, m: (0, h)),
        ],
        out_shape=[
            jax.ShapeDtypeStruct((micros, rows, rank), bf16),
            jax.ShapeDtypeStruct((nz, micros, rows, lanes), bf16),
            jax.ShapeDtypeStruct((rank, pairs * 4 * LANES), bf16),
            jax.ShapeDtypeStruct((kvr, pairs * 2 * LANES), bf16),
        ],
        scratch_shapes=[
            pltpu.VMEM((micros, rows, rank), f32),
            pltpu.VMEM((micros, seq, lanes), f32),
            pltpu.VMEM((rank, 4 * LANES), f32),
            pltpu.VMEM((kvr, 2 * LANES), f32),
        ],
        compiler_params=pltpu.CompilerParams(vmem_limit_bytes=VMEM_ATTEND),
        cost_estimate=cost(18 * pairs),
        name="attend_back",
    )(*operands)


COLS = 256
WIDE = 512
WIDE_OUT = 640


def rows_of(ref):
    return ref[...].reshape(-1, ref.shape[2])


def column_block(weights, own_rows, kind):
    return pl.BlockSpec((weights.shape[0], own_rows, COLS), lambda i: (0, kind, i))


def ffn_up_kernel(x_ref, gate_ref, up_ref, gate_out, up_out, hidden_out):
    gate = product(x_ref[...], rows_of(gate_ref))
    up = product(x_ref[...], rows_of(up_ref))
    gate_out[...] = gate.astype(bf16)
    up_out[...] = up.astype(bf16)
    hidden_out[...] = (gate * jax.nn.sigmoid(gate) * up).astype(bf16)


def ffn_up(x, weights, own_rows):
    rows, width = x.shape
    units = weights.shape[2]
    tile = pl.BlockSpec((rows, COLS), lambda i: (0, i))
    return pl.pallas_call(
        ffn_up_kernel,
        grid=(pl.cdiv(units, COLS),),
        in_specs=[
            pl.BlockSpec((rows, width), lambda i: (0, 0)),
            column_block(weights, own_rows, 0),
            column_block(weights, own_rows, 1),
        ],
        out_specs=[tile] * 3,
        out_shape=[jax.ShapeDtypeStruct((rows, units), bf16)] * 3,
        compiler_params=pltpu.CompilerParams(vmem_limit_bytes=VMEM_FFN),
        cost_estimate=cost(18),
        name="ffn_up",
    )(x, weights, weights)


def ffn_back_kernel(x_ref, down_ref, gate_ref, up_ref, g_gate_out, g_up_out):
    grad = product(x_ref[...], rows_of(down_ref))
    gate = gate_ref[...].astype(f32)
    sig = jax.nn.sigmoid(gate)
    g_gate_out[...] = (
        grad * up_ref[...].astype(f32) * sig * (1.0 + gate * (1.0 - sig))
    ).astype(bf16)
    g_up_out[...] = (grad * gate * sig).astype(bf16)


def ffn_back(x, weights, gate, up, own_rows):
    rows, width = x.shape
    units = weights.shape[2]
    tile = pl.BlockSpec((rows, COLS), lambda i: (0, i))
    return pl.pallas_call(
        ffn_back_kernel,
        grid=(pl.cdiv(units, COLS),),
        in_specs=[
            pl.BlockSpec((rows, width), lambda i: (0, 0)),
            column_block(weights, own_rows, 2),
            tile,
            tile,
        ],
        out_specs=[tile] * 2,
        out_shape=[jax.ShapeDtypeStruct((rows, units), bf16)] * 2,
        compiler_params=pltpu.CompilerParams(vmem_limit_bytes=VMEM_FFN),
        cost_estimate=cost(12),
        name="ffn_back",
    )(x, weights, gate, up)


def to_width_kernel(count, *refs):
    total = None
    for a_ref, w_ref in zip(refs[:count], refs[count : 2 * count]):
        term = contract_cols(a_ref[...], rows_of(w_ref))
        total = term if total is None else total + term
    refs[-1][...] = total.astype(bf16)


def to_width(half, values, weights, kinds, own_rows):
    count = len(values)
    rows, units = values[0].shape[0] // 2, values[0].shape[1]
    width = weights.shape[0] * own_rows
    per = WIDE_OUT // own_rows

    def owner_block(kind):
        return pl.BlockSpec((per, own_rows, units), lambda i: (i, kind, 0))

    return pl.pallas_call(
        functools.partial(to_width_kernel, count),
        grid=(width // WIDE_OUT,),
        in_specs=[pl.BlockSpec((rows, units), lambda i: (half, 0))] * count
        + [owner_block(kind) for kind in kinds],
        out_specs=pl.BlockSpec((rows, WIDE_OUT), lambda i: (0, i)),
        out_shape=jax.ShapeDtypeStruct((rows, width), bf16),
        compiler_params=pltpu.CompilerParams(vmem_limit_bytes=VMEM_FFN),
        cost_estimate=cost(6 * count),
        name="to_width",
    )(*values, *([weights] * count))


def weight_grad_kernel(a_ref, b_ref, out_ref):
    out_ref[...] = contract_rows(a_ref[...], b_ref[...]).astype(bf16)


def weight_grad(a, b):
    rows, width = a.shape
    units = b.shape[1]
    return pl.pallas_call(
        weight_grad_kernel,
        grid=(width // WIDE,),
        in_specs=[
            pl.BlockSpec((rows, WIDE), lambda i: (0, i)),
            pl.BlockSpec((rows, units), lambda i: (0, 0)),
        ],
        out_specs=pl.BlockSpec((WIDE, units), lambda i: (i, 0)),
        out_shape=jax.ShapeDtypeStruct((width, units), bf16),
        compiler_params=pltpu.CompilerParams(vmem_limit_bytes=VMEM_FFN),
        cost_estimate=cost(units * 0.006),
        name="weight_grad",
    )(a, b)


def on_device(
    tokens,
    segments,
    attn_gain,
    query_down,
    query_gain,
    query_up,
    latent_down,
    latent_gain,
    latent_up,
    out_weight,
    ffn_gain,
    gate_weight,
    up_weight,
    down_weight,
    cotangent,
):
    nx, nz = lax.axis_size("fsdp"), lax.axis_size("ctx")
    owners = nx * nz
    z, t = lax.axis_index("ctx"), lax.axis_index("tensor")
    micros, _, rows, width = tokens.shape
    seq = segments.shape[2]
    count = micros * rows
    share = count // TENSOR
    heads = query_up.shape[1] // (HD + ROPE)
    rank = query_down.shape[1]
    down_cols = rank + KVR + ROPE
    own_rows = query_down.shape[0]
    part_rows = own_rows // TENSOR
    half = ROPE // 2
    gain_sizes = [v.shape[0] for v in (attn_gain, query_gain, latent_gain, ffn_gain)]
    gain_total = sum(gain_sizes)
    gain_pad = GAIN_ROWS * down_cols - gain_total

    def share_of(values):
        return lax.dynamic_slice_in_dim(values, t * share, share, 0)

    down_own = lax.dynamic_slice_in_dim(
        jnp.concatenate([query_down, latent_down], axis=1), t * part_rows, part_rows, 0
    )
    gains = jnp.concatenate([attn_gain, query_gain, latent_gain, ffn_gain])
    gains = jnp.pad(gains, (0, gain_pad)).reshape(GAIN_ROWS, down_cols)
    order = Order()
    down_all, gain_all, up_query, up_latent, weight_out = front_gather(
        down_own, gains, query_up, latent_up, out_weight
    )
    down_whole = down_all.reshape(width, down_cols)
    up_query = up_query.reshape(rank, -1)
    up_latent = up_latent.reshape(KVR, -1)
    weight_out = weight_out.reshape(width, -1)
    order.mark(gain_all)

    cut = own_rows // 2
    pack_cols = out_weight.shape[1]
    query_rows = query_up.size // pack_cols
    own_query_up, own_latent_up = query_up, latent_up
    units = gate_weight.shape[1]
    f_rows = 2 * own_rows + cut
    f_all = [order(jnp.concatenate([gate_weight, up_weight, down_weight], axis=0))]
    for _ in range(1, nx):
        f_all.append(turn(f_all[-1], "fsdp"))
    f_gather = Gather(f_all[0][:f_rows])
    gain_blocks = gain_all.reshape(owners, -1).astype(f32)
    gain_list, start = [], 0
    for size in gain_sizes:
        gain_list.append(gain_blocks[:, start : start + size].reshape(-1))
        start += size
    gain_attn, gain_query, gain_latent, gain_ffn = gain_list

    seg = segments[:, 0]
    first_end = jnp.sum((seg < 1).astype(jnp.int32), axis=1, keepdims=True)
    second_end = jnp.sum((seg < 2).astype(jnp.int32), axis=1, keepdims=True)
    seg_own = lax.dynamic_slice_in_dim(seg, z * rows, rows, 1)
    own_starts = jnp.where(seg_own < 1, 0, jnp.where(seg_own < 2, first_end, second_end))
    own_index = jnp.broadcast_to(z * rows + jnp.arange(rows, dtype=jnp.int32), own_starts.shape)
    spans = jnp.pad(jnp.stack([own_starts, own_index], axis=1), ((0, 0), (0, 6), (0, 0)))
    lane = jnp.arange(LANES, dtype=jnp.int32)
    frequency = rope_base ** (-(lane % half).astype(f32) * (2.0 / ROPE))
    angles = (own_index - own_starts).astype(f32)[:, :, None] * frequency
    cos_own = jnp.where(lane < ROPE, jnp.cos(angles), 0.0)
    sin_own = jnp.where(lane < ROPE, jnp.sin(angles), 0.0) * jnp.where(lane < half, -1.0, 1.0)
    cos_share = share_of(cos_own.reshape(count, LANES))[:, :half]
    sin_share = share_of(sin_own.reshape(count, LANES))[:, half:ROPE]

    def rotated(values, cosine, sine):
        first, second = values[..., :half], values[..., half:]
        return jnp.concatenate(
            [first * cosine - second * sine, first * sine + second * cosine], axis=-1
        )

    inputs_low = tokens.reshape(count, width)
    tokens_share = share_of(inputs_low).astype(f32)
    normed_share = rms_scale(tokens_share, gain_attn).astype(bf16)
    raw = product(normed_share, down_whole)
    query_latent, latent_raw = raw[:, :rank], raw[:, rank:]
    query_normed = rms_scale(query_latent, gain_query).astype(bf16)
    latent = rms_scale(latent_raw[:, :KVR], gain_latent).astype(bf16)
    key_rope = rotated(latent_raw[:, KVR:], cos_share, sin_share).astype(bf16)
    latent = jnp.concatenate(
        [latent, jnp.pad(key_rope, ((0, 0), (0, LANES - ROPE)))], axis=1
    )
    order.mark(latent)
    lanes = KVR + LANES
    shared_pieces = gather_ctx(latent)

    column = jnp.arange(heads * (HD + ROPE), dtype=jnp.int32)
    feature = column % (HD + ROPE)
    target = (column // (HD + ROPE)) * (2 * LANES) + jnp.where(
        feature < HD, feature, feature - HD + LANES
    )
    spread = (target[:, None] == jnp.arange(heads * 2 * LANES)[None, :]).astype(bf16)
    wq = product(order(up_query), spread).astype(bf16)
    order.mark((wq, shared_pieces[1]))
    f_gather.start_z(order)
    shared = by_ctx(order(tuple(shared_pieces)))
    shared = jnp.concatenate([query_normed] + [shared[d] for d in range(nz)], axis=1)
    order.mark(shared)
    shared_slots = tensor_gather(shared)
    f_buffer = Buffer((3 * own_rows, units), order)
    order.mark((f_gather.piece, f_all[-1]))
    f_gather.pass_on(order)
    order.mark((cos_own, spans))
    shared = jnp.stack(from_slots(order(tuple(shared_slots))))
    query_normed = shared[..., :rank].reshape(micros, rows, rank)
    latent_all = jnp.stack(
        [shared[..., rank + d * lanes : rank + (d + 1) * lanes] for d in range(nz)]
    ).reshape(nz, micros, rows, lanes)
    order.mark((query_normed, latent_all))
    attended, logs, query_normed_t, latent_t = attend(
        order(query_normed), wq, latent_all, up_latent, cos_own, sin_own, spans
    )
    order.mark(attended)
    f_gather.arrive(order)
    f_gather.pass_on(order)
    attended = order(attended)

    def slot_halves(values):
        slots = to_slots(values.reshape((TENSOR, share) + values.shape[1:]))
        return jnp.concatenate(slots[:2], axis=0), jnp.concatenate(slots[2:], axis=0)

    def halves(values):
        return values.reshape(2, share, width)

    attended_kept, attended_sent = slot_halves(attended.reshape(count, -1))
    sent = contract_cols(attended_sent, weight_out).astype(bf16)
    kept = contract_cols(attended_kept, weight_out).astype(bf16)
    kept, sent = halves(kept), halves(sent)
    order.mark((kept, sent))
    near = swap(sent, 1)
    passed = add_low(kept[1], near[1])
    order.mark(passed)
    far_share = swap(passed, 2)
    x = lax.axis_index("fsdp")
    for e, far in enumerate(f_all):
        f_buffer.place(far[None, None], (x - e) % nx, z, 0)
    f_gather.place_old(f_buffer, order)
    f_buffer.filled(order)
    attn_share = kept[0].astype(f32) + near[0].astype(f32) + order(far_share).astype(f32)
    middle = tokens_share + branch_scale * attn_share
    ffn_share_in = rms_scale(middle, gain_ffn).astype(bf16)
    h_gather = PairGather([far[f_rows:] for far in f_all], order)
    order.mark((ffn_share_in, h_gather.piece))
    ffn_slots = tensor_gather(ffn_share_in)
    while f_gather.step + 1 < nz:
        f_gather.arrive(order)
        f_gather.pass_on(order)
    f_gather.arrive(order)
    f_gather.start_x(order)
    h_gather.start_z(order)
    f_gather.place_old(f_buffer, order)
    f_buffer.filled(order)
    upstream_slots = jnp.concatenate(slot_halves(order(cotangent).reshape(count, width)), axis=0)
    upstream_share = upstream_slots[:share].astype(f32)
    grad_ffn = (branch_scale * upstream_slots.astype(f32)).astype(bf16)
    ffn_in = jnp.concatenate(order(tuple(ffn_slots)), axis=0)
    order.mark((grad_ffn, ffn_in))
    while h_gather.step + 1 < nz:
        h_gather.arrive(order)
        h_gather.start_z(order)
        h_gather.place_before(f_buffer, order, f_rows)
    f_gather.arrive(order)
    f_gather.place(f_buffer, order)
    gate_val, up_val, hidden = ffn_up(ffn_in, f_buffer.result(), own_rows)
    order.mark(hidden)

    def blocks_of(gradient):
        return gradient.reshape((owners, -1) + gradient.shape[1:])

    s_down = PairScatter(blocks_of(weight_grad(grad_ffn, hidden)), order)
    h_gather.arrive(order)
    h_gather.place(f_buffer, order, f_rows)
    weights = f_buffer.result()
    grad_gate, grad_up = ffn_back(order(grad_ffn), weights, gate_val, up_val, own_rows)
    s_gate = Scatter(blocks_of(weight_grad(ffn_in, grad_gate)), 2)
    s_gate.start_x(order)
    grad_gate, grad_up = order((grad_gate, grad_up))
    sent = to_width(1, (grad_gate, grad_up), weights, (0, 1), own_rows)
    order.mark(sent)
    kept = to_width(0, order((grad_gate, grad_up)), weights, (0, 1), own_rows)
    order.mark(kept)
    grad_ffn_in = tensor_scatter(halves(kept), halves(sent))
    s_up = Scatter(blocks_of(weight_grad(ffn_in, order(grad_up))), 2)
    order.mark(s_up.blocks)
    s_gate.arrive(order)
    s_gate.start_x(order)
    s_down.forward(order)
    grad_middle, grad_gain_ffn = norm_back(middle, gain_ffn, order(grad_ffn_in))
    grad_middle = grad_middle + upstream_share
    grad_attn_share = (branch_scale * grad_middle).astype(bf16)
    order.mark(grad_attn_share)
    grad_attn_slots = tensor_gather(grad_attn_share)

    hidden = order(hidden)
    mixed_sent = to_width(1, (hidden,), weights, (2,), own_rows)
    mixed_kept = to_width(0, (hidden,), weights, (2,), own_rows)
    order.mark((mixed_kept, mixed_sent))
    s_gate.forward(order)
    grad_attn = jnp.concatenate(order(tuple(grad_attn_slots)), axis=0)
    order.mark(grad_attn)

    grad_attended = product(grad_attn, weight_out).astype(bf16)
    grad_attended = jnp.concatenate(from_slots(jnp.split(grad_attended, TENSOR)), axis=0)
    attended_slots = jnp.concatenate([attended_kept, attended_sent], axis=0)
    s_out = Scatter(blocks_of(weight_grad(order(grad_attn), attended_slots)), 1)
    order.mark((s_out.blocks, grad_attended))
    s_gate.arrive(order)
    s_up.start_x(order)
    s_up.start_x(order)
    s_out.start_x(order)
    s_down.forward(order)
    operands = (
        query_normed,
        wq,
        latent_all,
        up_latent,
        cos_own,
        sin_own,
        spans,
        order(grad_attended).reshape(micros, rows, -1),
        logs,
        query_normed_t,
        latent_t,
    )
    pairs = heads // 2
    early = (pairs + 1) // 2
    one = attend_back(0, early, *operands)
    order.mark(one[0])
    ffn_share = tensor_scatter(halves(order(mixed_kept)), halves(order(mixed_sent)))
    s_gate.forward(order)
    s_up.forward(order)
    s_down.forward(order)
    two = attend_back(early, pairs - early, order(operands[0]), *operands[1:])
    order.mark((two[0], ffn_share))
    mixed_share = (middle + branch_scale * order(ffn_share)).astype(bf16)

    def gradient_slots(results):
        query = to_slots(results[0].reshape(TENSOR, share, rank))
        latents = to_slots(results[1].reshape(nz, TENSOR, share, lanes), 1)
        return [
            jnp.concatenate([q] + [v[d] for d in range(nz)], axis=1)
            for q, v in zip(query, latents)
        ]

    sums = [add_low(a, b) for a, b in zip(gradient_slots(one), gradient_slots(two))]
    kept, sent = jnp.stack(sums[:2]), jnp.stack(sums[2:])
    order.mark((kept, sent))
    g_share = tensor_scatter(kept, sent)
    s_gate.forward(order)
    s_up.forward(order)
    s_out.arrive(order)
    s_out.forward(order)
    g_wq = order(jnp.concatenate([one[2], two[2]], axis=1))
    grad_query_up = contract_cols(g_wq, spread).astype(bf16)
    s_pack = Scatter(
        jnp.concatenate(
            [
                grad_query_up.reshape(owners, -1, pack_cols),
                jnp.concatenate([one[3], two[3]], axis=1).reshape(owners, -1, pack_cols),
            ],
            axis=1,
        ),
        1,
    )
    order.mark((s_pack.blocks, mixed_share))
    g_latent_blocks = jnp.stack(
        [g_share[:, rank + d * lanes : rank + (d + 1) * lanes] for d in range(nz)]
    ).astype(bf16)
    order.mark(g_latent_blocks)
    latent_parts = scatter_parts(g_latent_blocks)
    g_latent_share = sum(v.astype(f32) for v in order(tuple(latent_parts)))
    grad_query_latent, grad_gain_query = norm_back(query_latent, gain_query, g_share[:, :rank])
    grad_latent_first, grad_gain_latent = norm_back(
        latent_raw[:, :KVR], gain_latent, g_latent_share[:, :KVR]
    )
    grad_rope = rotated(g_latent_share[:, KVR : KVR + ROPE], cos_share, -sin_share)
    grad_raw = jnp.concatenate(
        [grad_query_latent, grad_latent_first, grad_rope], axis=1
    ).astype(bf16)
    order.mark(grad_raw)
    grad_raw_slots = tensor_gather(grad_raw)
    s_gate.forward(order)
    s_up.forward(order)
    s_out.forward(order)
    s_pack.start_x(order)
    grad_normed = contract_cols(order(grad_raw), down_whole)
    grad_inputs, grad_gain_attn = norm_back(tokens_share, gain_attn, grad_normed)
    grad_share = (grad_inputs + grad_middle).astype(bf16)
    normed = rms_scale(order(inputs_low).astype(f32), gain_attn).astype(bf16)
    order.mark((grad_share, normed))
    grad_raw_all = jnp.concatenate(from_slots(order(tuple(grad_raw_slots))), axis=0)
    s_pack.arrive(order)
    last_share = jnp.concatenate([order(grad_share), mixed_share], axis=0)
    order.mark(last_share)
    last_slots = tensor_gather(last_share)
    grad_down = weight_grad(normed, order(grad_raw_all))
    grad_down = grad_down.reshape(owners, TENSOR, part_rows, down_cols)
    grad_down = lax.dynamic_index_in_dim(grad_down, t, 1, keepdims=False)
    gain_grads = jnp.concatenate(
        [
            g.reshape(owners, -1)
            for g in (grad_gain_attn, grad_gain_query, grad_gain_latent, grad_gain_ffn)
        ],
        axis=1,
    ).astype(bf16)
    gain_grads = jnp.pad(gain_grads, ((0, 0), (0, gain_pad))).reshape(
        owners, GAIN_ROWS, down_cols
    )
    s_bundle = Scatter(jnp.concatenate([grad_down, gain_grads], axis=1), 1)
    s_bundle.start_x(order)
    s_up.forward(order)
    s_out.forward(order)
    s_pack.forward(order)
    s_bundle.arrive(order)
    s_bundle.forward(order)
    s_pack.forward(order)
    s_bundle.forward(order)
    s_pack.forward(order)
    while s_bundle.step < nz:
        s_bundle.forward(order)
    bundle_share = s_bundle.total.astype(bf16)
    order.mark(bundle_share)
    bundle_slots = tensor_gather(bundle_share)
    for scatter in (s_up, s_out, s_pack):
        while scatter.step < nz:
            scatter.forward(order)
    last_list = from_slots(order(tuple(last_slots)))
    grad_tokens = jnp.concatenate([v[:share] for v in last_list], axis=0).astype(f32)
    mixed = jnp.concatenate([v[share:] for v in last_list], axis=0)
    bundle_list = from_slots(order(tuple(bundle_slots)))
    out_down = jnp.concatenate([b[:part_rows] for b in bundle_list], axis=0).astype(f32)
    gain_sum = sum(b[part_rows:].astype(f32) for b in bundle_list).reshape(-1)
    out_gains, start = [], 0
    for size in gain_sizes:
        out_gains.append(gain_sum[start : start + size])
        start += size
    out_query_up = s_pack.total[:query_rows].reshape(query_up.shape)
    out_latent_up = s_pack.total[query_rows:].reshape(latent_up.shape)

    return (
        mixed.reshape(tokens.shape),
        grad_tokens.reshape(tokens.shape),
        out_gains[0],
        out_down[:, :rank],
        out_gains[1],
        out_query_up,
        out_down[:, rank:],
        out_gains[2],
        out_latent_up,
        s_out.total,
        out_gains[3],
        s_gate.total,
        s_up.total,
        s_down.result(),
    )


def solution(mesh):
    return jax.shard_map(
        on_device,
        mesh=mesh,
        in_specs=(
            P(None, "fsdp", "ctx", None),
            P(None, "fsdp", None),
            P(("fsdp", "ctx")),
            P(("fsdp", "ctx"), None),
            P(("fsdp", "ctx")),
            P(("fsdp", "ctx"), "tensor"),
            P(("fsdp", "ctx"), None),
            P(("fsdp", "ctx")),
            P(("fsdp", "ctx"), "tensor"),
            P(("fsdp", "ctx"), "tensor"),
            P(("fsdp", "ctx")),
            P(("fsdp", "ctx"), "tensor"),
            P(("fsdp", "ctx"), "tensor"),
            P(("fsdp", "ctx"), "tensor"),
            P(None, "fsdp", "ctx", None),
        ),
        out_specs=(
            P(None, "fsdp", "ctx", None),
            P(None, "fsdp", "ctx", None),
            P(("fsdp", "ctx")),
            P(("fsdp", "ctx"), None),
            P(("fsdp", "ctx")),
            P(("fsdp", "ctx"), "tensor"),
            P(("fsdp", "ctx"), None),
            P(("fsdp", "ctx")),
            P(("fsdp", "ctx"), "tensor"),
            P(("fsdp", "ctx"), "tensor"),
            P(("fsdp", "ctx")),
            P(("fsdp", "ctx"), "tensor"),
            P(("fsdp", "ctx"), "tensor"),
            P(("fsdp", "ctx"), "tensor"),
        ),
        check_vma=False,
    )
```
